32 devices in a mesh: section: 2 (over core), ctx: 4 (over z), tp: 4 (over y, x).
Axes of the slice: x: 2, y: 2, z: 4, core: 2. Of those that a mesh axis runs over, the one named last changes fastest.
Arguments:
- inputs: bfloat16 [2, 2048, 2048], P(None, 'ctx'), may hold values from -6 to 6
- cotangent: bfloat16 [2, 2048, 2048], P(None, 'ctx'), may hold values from -6 to 6
- lengths: int32 [2, 3], replicated, may hold values from 1 to 1792, 2048 in all within a row
- norm_gains: float32 [2, 2, 2048], P('section'), may hold values from 0.5 to 1.5
- norm_shifts: float32 [2, 2, 2048], P('section'), may hold values from -1.5 to 1.5
- qkv_weight: bfloat16 [2, 3, 2048, 2048], P('section', None, 'ctx', 'tp'), may hold values from -0.125 to 0.125
- qkv_bias: float32 [2, 3, 2048], P('section', None, 'tp'), may hold values from -1.5 to 1.5
- out_weight: bfloat16 [2, 2048, 2048], P('section', 'tp', 'ctx'), may hold values from -2 to 2
- gate_up_weight: bfloat16 [2, 2, 2048, 5632], P('section', None, 'ctx', 'tp'), may hold values from -0.125 to 0.125
- down_weight: bfloat16 [2, 5632, 2048], P('section', 'tp', 'ctx'), may hold values from -0.078125 to 0.078125
Outputs:
- layer_outputs: bfloat16 [2, 2, 2048, 2048], P('section', None, 'ctx')
- input_grads: float32 [2, 2, 2048, 2048], P('section', None, 'ctx')
- norm_gain_grads: float32 [2, 2, 2048], P('section')
- norm_shift_grads: float32 [2, 2, 2048], P('section')
- qkv_weight_grads: float32 [2, 3, 2048, 2048], P('section', None, 'ctx', 'tp')
- qkv_bias_grads: float32 [2, 3, 2048], P('section', None, 'tp')
- out_weight_grads: float32 [2, 2048, 2048], P('section', 'tp', 'ctx')
- gate_up_grads: float32 [2, 2, 2048, 5632], P('section', None, 'ctx', 'tp')
- down_grads: float32 [2, 5632, 2048], P('section', 'tp', 'ctx')
The draws below stay inside these ranges and needn't reach their ends.
Inputs may be any that keep to these rules, and one draw needn't show every extreme that they name: In each micro-batch the 3 lengths sum to 2048, and one of them, at a place drawn from the seed, is 1792.
All inputs are finite; a program needn't handle non-finite values.
Results may differ from the reference program's by a relative error of at most 0.025.
Values may be sent and summed in bfloat16 or wider, within the bound.
No kernel may reach another device: no remote copies, remote signals or barrier semaphores. Data moves between devices by JAX's collectives and lax.ppermute only.
A program may use at most 320 MiB of HBM per device.

```python
import math
import jax
import jax.numpy as jnp
import numpy as np
from jax import lax

D = 2048
HEADS = 32
HEAD_DIM = 64
FF = 5632
ROTATED_ENTRIES = 16
MB = 2
SEQS = 3
PACK = 2048
ROWS = 512
LAYERS = 2


def level_of(key, dims, pieces, smallest, high):
    gain, own = 1.0, jax.random.fold_in(key, 6)
    for axis_at, shards_of in pieces:
        draws = jnp.exp(jax.random.uniform(jax.random.fold_in(own, axis_at), (shards_of,), jnp.float32, smallest / len(pieces), high / len(pieces)))
        gain = gain * jnp.repeat(draws, dims[axis_at] // shards_of).reshape([-1 if axis == axis_at else 1 for axis in range(len(dims))])
    return gain


def profile(number_of, total, limit, slope):
    loads = [(1 << 20) // math.isqrt(grade ** slope) + 1 for grade in range(2, number_of + 1)]
    rest, given = total - limit - (number_of - 1), [1] * (number_of - 1)
    while rest > 0:
        free = [i for i in range(number_of - 1) if given[i] < limit]
        whole, remaining = sum([loads[i] for i in free]), rest
        for i in free:
            addition = min(limit - given[i], max(1, remaining * loads[i] // whole), rest)
            given[i] = given[i] + addition
            rest = rest - addition
    return np.array([limit] + given)


def uneven_parts(key, number_of, total, most, slope):
    if number_of == 2:
        one = jax.random.randint(key, (), max(1, total - most), min(most, total - 1) + 1)
        return jnp.stack([one, total - one])
    tallies = jnp.asarray(profile(number_of, total, most, slope), jnp.int32)
    pairs = (number_of - 1) // 2
    source_of, taker = tallies[1:1 + 2 * pairs:2], tallies[2:2 + 2 * pairs:2]
    room = jnp.minimum(source_of - 1, most - taker)
    moved = jax.random.randint(jax.random.fold_in(key, 1), (pairs,), 0, 1 << 20) % (room + 1)
    tallies = tallies.at[1:1 + 2 * pairs:2].set(source_of - moved).at[2:2 + 2 * pairs:2].set(taker + moved)
    return tallies[jax.random.permutation(jax.random.fold_in(key, 2), number_of)]


def centred(rng, shape, scale, bound, split=(), held_as=jnp.bfloat16):
    gain = level_of(rng, shape, split, -0.22, 0.18) if split else 1.0
    drawn = jax.random.normal(rng, shape, jnp.float32) * scale * gain
    return jnp.minimum(jnp.maximum(drawn, -bound), bound).astype(held_as)


def setup_inputs(seed: int = 0) -> dict:
    key_of = jax.random.split(jax.random.key(seed), 11)
    return {
        "inputs": centred(key_of[0], (MB, PACK, D), 1.0, 6.0, ((1, 4),)),
        "cotangent": centred(key_of[1], (MB, PACK, D), 1.0, 6.0, ((1, 4),)),
        "lengths": jax.vmap(lambda own: uneven_parts(own, SEQS, PACK, PACK - ROWS // 2, 2))(jax.random.split(key_of[2], MB)).reshape((MB, SEQS)).astype(jnp.int32),
        "norm_gains": jnp.clip(1.0 + 0.1 * jax.random.normal(key_of[3], (LAYERS, 2, D), jnp.float32), 0.5, 1.5),
        "norm_shifts": centred(key_of[4], (LAYERS, 2, D), 0.3, 1.5, ((0, 2),), jnp.float32),
        "qkv_weight": centred(key_of[5], (LAYERS, 3, D, D), D ** -0.5, 0.125, ((0, 2), (2, 4), (3, 4))),
        "qkv_bias": centred(key_of[6], (LAYERS, 3, D), 0.3, 1.5, ((0, 2), (2, 4)), jnp.float32),
        "out_weight": centred(key_of[7], (LAYERS, D, D), (max(D // 256, 1)) ** -0.5, 2.0, ((0, 2), (1, 4), (2, 4))),
        "gate_up_weight": centred(key_of[8], (LAYERS, 2, D, FF), D ** -0.5, 0.125, ((0, 2), (2, 4), (3, 4))),
        "down_weight": centred(key_of[9], (LAYERS, FF, D), FF ** -0.5, 0.078125, ((0, 2), (1, 4), (2, 4))),
    }


@jax.custom_vjp
def low(v):
    return lax.optimization_barrier(v.astype(jnp.bfloat16)).astype(jnp.float32)

@jax.custom_vjp
def low_back(v):
    return v

def low_keep(v):
    return (low(v), None)

def low_pass(retained_values, grad):
    return (grad,)

def back_keep(v):
    return (v, None)

def back_low(retained_values, grad):
    return (low(grad),)
low.defvjp(low_keep, low_pass)
low_back.defvjp(back_keep, back_low)
EPSILON = 1e-05
NEGATIVE = -1e+30
ROTARY_BASE = 10000.0
HIGHEST = lax.Precision.HIGHEST

def layer_norm(values, norm_gain, norm_shift):
    centre = values - lax.optimization_barrier(jnp.mean(values, axis=-1, keepdims=True))
    spread = lax.optimization_barrier(jnp.mean(centre * centre, axis=-1, keepdims=True))
    return centre * lax.rsqrt(spread + EPSILON) * norm_gain + norm_shift

def rotary_tables(local_place):
    half_width = ROTATED_ENTRIES // 2
    frequency = jnp.exp(-(jnp.arange(half_width, dtype=jnp.float32) * 2.0 / ROTATED_ENTRIES) * math.log(ROTARY_BASE))
    angle = local_place.astype(jnp.float32)[:, None] * frequency[None, :]
    angle = jnp.concatenate([angle, angle], axis=1)
    return (jnp.cos(angle), jnp.sin(angle))

def rotate(values, cosine, sine_table):
    half_width = ROTATED_ENTRIES // 2
    turned_part = values[..., :ROTATED_ENTRIES]
    swapped = jnp.concatenate([-turned_part[..., half_width:], turned_part[..., :half_width]], axis=-1)
    moved = turned_part * cosine[:, None, :] + swapped * sine_table[:, None, :]
    return jnp.concatenate([moved, values[..., ROTATED_ENTRIES:]], axis=-1)

def document_places(length_row, first_place, row_count):
    ends = jnp.cumsum(length_row).astype(jnp.int32)
    global_place = (first_place + jnp.arange(row_count, dtype=jnp.int32)).astype(jnp.int32)
    passed = ends[None, :] <= global_place[:, None]
    document = lax.optimization_barrier(jnp.sum(passed.astype(jnp.int32), axis=1)).astype(jnp.int32)
    begins = lax.optimization_barrier(jnp.sum(jnp.where(passed, length_row[None, :], 0), axis=1)).astype(jnp.int32)
    return (document, global_place, (global_place - begins).astype(jnp.int32))

def attention(queries, keys, values, document, global_place):
    block_rows = math.gcd(PACK, 512)
    block_count = PACK // block_rows
    score_scale = HEAD_DIM ** (-0.5)

    def one_block(items):
        block_queries, block_document, block_place = items
        scores = jnp.einsum('qhd,khd->hqk', block_queries, keys, precision=HIGHEST) * score_scale
        scores = low_back(scores)
        allowed = (document[None, :] == block_document[:, None]) & (global_place[None, :] <= block_place[:, None])
        scores = jnp.where(allowed[None], scores, NEGATIVE)
        row_high = lax.optimization_barrier(jnp.max(scores, axis=2, keepdims=True))
        weights = jnp.exp(scores - row_high)
        weights = low(weights / lax.optimization_barrier(jnp.sum(weights, axis=2, keepdims=True)))
        return jnp.einsum('hqk,khd->qhd', weights, values, precision=HIGHEST)
    blocks = lax.map(jax.checkpoint(one_block), (queries.reshape(block_count, block_rows, HEADS, HEAD_DIM), document.reshape(block_count, block_rows), global_place.reshape(block_count, block_rows)))
    return blocks.reshape(PACK, D)

def one_layer(layer_input, norm_gain, norm_shift, weight_qkv, bias_qkv, weight_out, weight_gate_up, weight_down, layout):
    document, global_place, cosine, sine_table = layout
    normed_first = low(layer_norm(layer_input, norm_gain[0], norm_shift[0]))
    projected = jnp.einsum('ld,cdh->clh', normed_first, weight_qkv, precision=HIGHEST) + bias_qkv[:, None, :]
    projected = low_back(projected)
    queries = low(rotate(projected[0].reshape(PACK, HEADS, HEAD_DIM), cosine, sine_table))
    keys = low(rotate(projected[1].reshape(PACK, HEADS, HEAD_DIM), cosine, sine_table))
    values = low(projected[2].reshape(PACK, HEADS, HEAD_DIM))
    attended = attention(queries, keys, values, document, global_place)
    attended = low(low_back(attended))
    branch = low_back(jnp.dot(attended, weight_out, precision=HIGHEST))
    hidden_state = layer_input + branch
    normed_second = low(layer_norm(hidden_state, norm_gain[1], norm_shift[1]))
    gate_up = low_back(jnp.einsum('ld,cdf->clf', normed_second, weight_gate_up, precision=HIGHEST))
    activated = low(jax.nn.silu(gate_up[0]) * gate_up[1])
    mixer = low_back(jnp.dot(activated, weight_down, precision=HIGHEST))
    return hidden_state + mixer

def reference(inputs, cotangent, lengths, norm_gains, norm_shifts, qkv_weight, qkv_bias, out_weight, gate_up_weight, down_weight):
    layouts = []
    for batch_index in range(MB):
        document, global_place, local_place = document_places(lengths[batch_index], 0, PACK)
        cosine, sine_table = rotary_tables(local_place)
        layouts.append((document, global_place, cosine, sine_table))
    start_values = inputs.astype(jnp.float32)
    params = (norm_gains.astype(jnp.float32), norm_shifts.astype(jnp.float32), qkv_weight.astype(jnp.float32), qkv_bias.astype(jnp.float32), out_weight.astype(jnp.float32), gate_up_weight.astype(jnp.float32), down_weight.astype(jnp.float32))

    def forward(perturb, gains, shifts, weight_qkv, bias_qkv, weight_out, weight_gate_up, weight_down):
        batches = []
        for batch_index in range(MB):
            current = start_values[batch_index]
            produced = []
            for layer_index in range(LAYERS):
                current = current + perturb[layer_index, batch_index]
                raw = one_layer(current, gains[layer_index], shifts[layer_index], weight_qkv[layer_index], bias_qkv[layer_index], weight_out[layer_index], weight_gate_up[layer_index], weight_down[layer_index], layouts[batch_index])
                if layer_index + 1 < LAYERS:
                    current = low_back(low(raw))
                else:
                    current = low(raw)
                produced.append(current)
            batches.append(jnp.stack(produced))
        return jnp.stack(batches, axis=1)
    perturb = jnp.zeros((LAYERS, MB, PACK, D), jnp.float32)
    outputs, pullback = jax.vjp(forward, perturb, *params)
    seed_grad = jnp.concatenate([jnp.zeros((LAYERS - 1, MB, PACK, D), jnp.float32), cotangent.astype(jnp.float32)[None]], axis=0)
    grads = pullback(seed_grad)
    return (outputs.astype(jnp.bfloat16), grads[0], grads[1], grads[2], grads[3], grads[4], grads[5], grads[6], grads[7])
```

```python
import math

import jax
import jax.numpy as jnp
from jax import lax
from jax.experimental import pallas as pl
from jax.experimental.pallas import tpu as pltpu
from jax.sharding import PartitionSpec as P

HEAD_DIM = 64
ROTATED_ENTRIES = 16
EPSILON = 1e-05
NEGATIVE = -1e30
ROTARY_BASE = 10000.0
LANES = 128
F32 = jnp.float32
BF16 = jnp.bfloat16
CONTRACT_LAST = (((1,), (1,)), ((), ()))
CONTRACT_FIRST = (((0,), (0,)), ((), ()))
VMEM_BYTES = 48 * 1024 * 1024


def head_rows(values, head):
    lane = lax.broadcasted_iota(jnp.int32, values.shape, 1)
    return jnp.where(lane // HEAD_DIM == head, values, 0.0).astype(BF16)


def attend_kernel(chunks, flags, query_ref, bias_ref, *refs):
    key_refs, value_refs = refs[:chunks], refs[chunks : 2 * chunks]
    full_ref, low_ref, log_ref, high, total, summed = refs[2 * chunks :]
    rows = query_ref.shape[0]
    heads = LANES // HEAD_DIM
    scaled = query_ref[...].astype(F32) * HEAD_DIM**-0.5
    queries = [head_rows(scaled, head) for head in range(heads)]
    high[...] = jnp.full(high.shape, NEGATIVE, F32)
    total[...] = jnp.zeros(total.shape, F32)
    summed[...] = jnp.zeros(summed.shape, F32)
    for chunk in range(chunks):

        @pl.when(flags[chunk] != 0)
        def _():
            keys = key_refs[chunk][...]
            values = value_refs[chunk][...]
            for head in range(heads):
                scores = lax.dot_general(
                    keys, queries[head], CONTRACT_LAST, preferred_element_type=F32
                )
                scores = scores + bias_ref[chunk * rows : (chunk + 1) * rows, :]
                old = high[head]
                new = jnp.maximum(old, jnp.max(scores, axis=0, keepdims=True))
                weights = jnp.exp(scores - new)
                decay = jnp.exp(old - new)
                total[head] = total[head] * decay + jnp.sum(weights, axis=0, keepdims=True)
                summed[head] = summed[head] * decay + lax.dot_general(
                    values, weights.astype(BF16), CONTRACT_FIRST, preferred_element_type=F32
                )
                high[head] = new

    row = lax.broadcasted_iota(jnp.int32, (LANES, rows), 0)
    merged = jnp.zeros((LANES, rows), F32)
    for head in range(heads):
        merged = jnp.where(row // HEAD_DIM == head, summed[head] / total[head], merged)
        log_ref[0, head : head + 1, :] = high[head] + jnp.log(total[head])
    merged = merged.T
    full_ref[...] = merged
    low_ref[...] = merged.astype(BF16)


def column_spec(rows, shift):
    return pl.BlockSpec((rows, LANES), lambda pair, flags: (0, pair + shift))


def attend(queries, key_values, bias, flags):
    rows, width = queries.shape
    chunks = len(key_values)
    pairs = width // LANES
    heads = LANES // HEAD_DIM
    own = column_spec(rows, 0)
    return pl.pallas_call(
        lambda *refs: attend_kernel(chunks, *refs),
        out_shape=(
            jax.ShapeDtypeStruct((rows, width), F32),
            jax.ShapeDtypeStruct((rows, width), BF16),
            jax.ShapeDtypeStruct((pairs, heads, rows), F32),
        ),
        grid_spec=pltpu.PrefetchScalarGridSpec(
            num_scalar_prefetch=1,
            grid=(pairs,),
            in_specs=[own, pl.BlockSpec(bias.shape, lambda pair, flags: (0, 0))]
            + [column_spec(rows, 0)] * chunks
            + [column_spec(rows, pairs)] * chunks,
            out_specs=(
                own,
                own,
                pl.BlockSpec((1, heads, rows), lambda pair, flags: (pair, 0, 0)),
            ),
            scratch_shapes=[
                pltpu.VMEM((heads, 1, rows), F32),
                pltpu.VMEM((heads, 1, rows), F32),
                pltpu.VMEM((heads, LANES, rows), F32),
            ],
        ),
        compiler_params=pltpu.CompilerParams(vmem_limit_bytes=VMEM_BYTES),
        cost_estimate=pl.CostEstimate(
            flops=4 * chunks * rows * rows * width * 2,
            bytes_accessed=2 * chunks * rows * width * 2 + bias.size * 4,
            transcendentals=0,
        ),
        name="attend",
    )(flags, queries, bias, *key_values, *key_values)


def attend_back_kernel(chunks, flags, query_ref, bias_ref, grad_ref, full_ref, log_ref, *refs):
    key_refs, value_refs = refs[:chunks], refs[chunks : 2 * chunks]
    query_grad_ref = refs[2 * chunks]
    key_grad_refs = refs[2 * chunks + 1 : 3 * chunks + 1]
    value_grad_refs = refs[3 * chunks + 1 : 4 * chunks + 1]
    summed = refs[4 * chunks + 1]
    rows = query_ref.shape[0]
    heads = LANES // HEAD_DIM
    scale = HEAD_DIM**-0.5
    scaled = query_ref[...].astype(F32) * scale
    grad = grad_ref[...].astype(F32)
    product = (grad * full_ref[...]).T
    queries = [head_rows(scaled, head) for head in range(heads)]
    grads = [head_rows(grad, head) for head in range(heads)]
    deltas = [
        jnp.sum(product[head * HEAD_DIM : (head + 1) * HEAD_DIM, :], axis=0, keepdims=True)
        for head in range(heads)
    ]
    summed[...] = jnp.zeros(summed.shape, F32)
    for chunk in range(chunks):

        @pl.when(flags[chunk] != 0)
        def _():
            keys = key_refs[chunk][...]
            values = value_refs[chunk][...]
            key_float = keys.astype(F32)
            key_grad = jnp.zeros((rows, LANES), F32)
            value_grad = jnp.zeros((rows, LANES), F32)
            query_grad = summed[...]
            for head in range(heads):
                scores = lax.dot_general(
                    keys, queries[head], CONTRACT_LAST, preferred_element_type=F32
                )
                scores = scores + bias_ref[chunk * rows : (chunk + 1) * rows, :]
                weights = jnp.exp(scores - log_ref[0, head : head + 1, :])
                weight_grad = lax.dot_general(
                    values, grads[head], CONTRACT_LAST, preferred_element_type=F32
                )
                score_grad = (weights * (weight_grad - deltas[head])).astype(BF16)
                value_grad = value_grad + jnp.dot(
                    weights.astype(BF16), grads[head], preferred_element_type=F32
                )
                key_grad = key_grad + jnp.dot(
                    score_grad, queries[head], preferred_element_type=F32
                )
                query_grad = query_grad + lax.dot_general(
                    head_rows(key_float, head),
                    score_grad,
                    CONTRACT_FIRST,
                    preferred_element_type=F32,
                )
            summed[...] = query_grad
            key_grad_refs[chunk][...] = key_grad.astype(BF16)
            value_grad_refs[chunk][...] = value_grad.astype(BF16)

        @pl.when(flags[chunk] == 0)
        def _():
            key_grad_refs[chunk][...] = jnp.zeros((rows, LANES), BF16)
            value_grad_refs[chunk][...] = jnp.zeros((rows, LANES), BF16)

    query_grad_ref[...] = summed[...].T * scale


def attend_back(queries, key_values, bias, flags, grad, full, log_total):
    rows, width = queries.shape
    chunks = len(key_values)
    pairs = width // LANES
    heads = LANES // HEAD_DIM
    own = column_spec(rows, 0)
    results = pl.pallas_call(
        lambda *refs: attend_back_kernel(chunks, *refs),
        out_shape=[jax.ShapeDtypeStruct((rows, width), F32)]
        + [jax.ShapeDtypeStruct((rows, width), BF16)] * (2 * chunks),
        grid_spec=pltpu.PrefetchScalarGridSpec(
            num_scalar_prefetch=1,
            grid=(pairs,),
            in_specs=[
                own,
                pl.BlockSpec(bias.shape, lambda pair, flags: (0, 0)),
                own,
                own,
                pl.BlockSpec((1, heads, rows), lambda pair, flags: (pair, 0, 0)),
            ]
            + [column_spec(rows, 0)] * chunks
            + [column_spec(rows, pairs)] * chunks,
            out_specs=[own] * (2 * chunks + 1),
            scratch_shapes=[pltpu.VMEM((LANES, rows), F32)],
        ),
        compiler_params=pltpu.CompilerParams(vmem_limit_bytes=VMEM_BYTES),
        cost_estimate=pl.CostEstimate(
            flops=10 * chunks * rows * rows * width * 2,
            bytes_accessed=4 * chunks * rows * width * 2 + bias.size * 4,
            transcendentals=0,
        ),
        name="attend_back",
    )(flags, queries, bias, grad, full, log_total, *key_values, *key_values)
    return results[0], results[1 : chunks + 1], results[chunks + 1 :]


def swap_cores(block):
    return lax.ppermute(block, "section", [(0, 1), (1, 0)])


def exchange(block, axis, bit):
    return lax.ppermute(block, axis, [(i, i ^ bit) for i in range(lax.axis_size(axis))])


def tp_sum(partial):
    ranks = lax.axis_size("tp")
    rows, width = partial.shape
    pieces = partial.astype(BF16).reshape(ranks, rows // ranks, width)
    total = pieces[0].astype(F32)
    for k in range(1, ranks):
        total = total + exchange(pieces[k], "tp", k).astype(F32)
    total = total.astype(BF16)
    return jnp.concatenate([total] + [exchange(total, "tp", k) for k in range(1, ranks)], axis=0)


def gather_chunks(own):
    count = lax.axis_size("ctx")
    blocks = [own]
    bit = 1
    while bit < count:
        if bit < count // 2:
            blocks = blocks + [exchange(block, "ctx", bit) for block in blocks]
        else:
            blocks = blocks + [swap_cores(block) for block in blocks]
        bit *= 2
    return blocks


def scatter_chunks(blocks):
    count = lax.axis_size("ctx")
    bit = count // 2
    while bit >= 1:
        if bit == count // 2:
            arrived = [swap_cores(block) for block in blocks[bit:]]
        else:
            arrived = [exchange(block, "ctx", bit) for block in blocks[bit:]]
        blocks = [
            (mine.astype(F32) + other.astype(F32)).astype(BF16 if bit > 1 else F32)
            for mine, other in zip(blocks[:bit], arrived)
        ]
        bit //= 2
    return blocks[0]


def norm_forward(parts, gain, shift):
    width = 2 * parts[0].shape[1]
    mean = sum(jnp.sum(part, axis=1, keepdims=True) for part in parts) / width
    centred = [part - mean for part in parts]
    spread = sum(jnp.sum(part * part, axis=1, keepdims=True) for part in centred) / width
    inverse = lax.rsqrt(spread + EPSILON)
    normed = [(c * inverse * g + s).astype(BF16) for c, g, s in zip(centred, gain, shift)]
    return normed, (mean, inverse)


def norm_backward(parts, statistics, gain, grads):
    mean, inverse = statistics
    width = 2 * parts[0].shape[1]
    hats = [(part - mean) * inverse for part in parts]
    scaled = [g * d for g, d in zip(gain, grads)]
    first = sum(jnp.sum(e, axis=1, keepdims=True) for e in scaled) / width
    second = sum(jnp.sum(e * x, axis=1, keepdims=True) for e, x in zip(scaled, hats)) / width
    moved = [inverse * (e - first - x * second) for e, x in zip(scaled, hats)]
    gain_grad = [jnp.sum(d * x, axis=0) for d, x in zip(grads, hats)]
    shift_grad = [jnp.sum(d, axis=0) for d in grads]
    return moved, gain_grad, shift_grad


def rotary_tables(local_place, width):
    half = ROTATED_ENTRIES // 2
    entry = jnp.arange(HEAD_DIM)
    frequency = jnp.exp(
        -((entry % half).astype(F32) * 2.0 / ROTATED_ENTRIES) * math.log(ROTARY_BASE)
    )
    frequency = jnp.where(entry < ROTATED_ENTRIES, frequency, 0.0)
    angle = local_place.astype(F32)[:, None] * frequency[None, :]
    sine = jnp.sin(angle)
    tables = (
        jnp.cos(angle),
        jnp.where(entry < half, -sine, 0.0),
        jnp.where(entry >= half, sine, 0.0),
    )
    return tuple(jnp.tile(table, (1, width // HEAD_DIM)) for table in tables)


def rotate(values, tables, sign):
    half = ROTATED_ENTRIES // 2
    cosine, low, high = tables
    return (
        values * cosine
        + jnp.roll(values, -half, axis=1) * (low * sign)
        + jnp.roll(values, half, axis=1) * (high * sign)
    )


def dot(left, right):
    return jnp.dot(left, right, preferred_element_type=F32)


def dot_back(left, right):
    return lax.dot_general(left, right, CONTRACT_LAST, preferred_element_type=F32)


def layer_forward(parts, weights, gain, shift, bias_row, layout):
    tables, mask, flags = layout
    (qkv_own, out_own, gate_up_own, down_own), (qkv_other, out_other, gate_up_other, down_other) = weights
    residual = [part.astype(F32) for part in parts]
    normed_first, statistics_first = norm_forward(residual, gain[0], shift[0])

    def project(c):
        return (
            dot(normed_first[0], qkv_own[c]) + dot(normed_first[1], qkv_other[c]) + bias_row[c][None]
        )

    key_value = jnp.concatenate(
        [rotate(project(1), tables, 1.0).astype(BF16), project(2).astype(BF16)], axis=1
    )
    key_values = gather_chunks(key_value)
    queries = rotate(project(0), tables, 1.0).astype(BF16)
    attended, attended_low, log_total = attend(queries, key_values, mask, flags)
    hidden = [
        part + tp_sum(dot(attended_low, weight)).astype(F32)
        for part, weight in zip(residual, (out_own, out_other))
    ]
    normed_second, statistics_second = norm_forward(hidden, gain[1], shift[1])
    gate, up = [
        dot(normed_second[0], gate_up_own[c]) + dot(normed_second[1], gate_up_other[c])
        for c in range(2)
    ]
    activated = (gate * jax.nn.sigmoid(gate) * up).astype(BF16)
    output = [
        (part + tp_sum(dot(activated, weight)).astype(F32)).astype(BF16)
        for part, weight in zip(hidden, (down_own, down_other))
    ]
    saved = (
        parts,
        statistics_first,
        normed_first,
        queries,
        key_values,
        attended,
        attended_low,
        log_total,
        hidden,
        statistics_second,
        normed_second,
        gate,
        up,
        activated,
    )
    return output, saved


def shared_weight_grad(own, other):
    arrived = swap_cores(other.astype(BF16))
    return (own + arrived.astype(F32)).astype(BF16)


def scatter_weight_grad(total, axis):
    return lax.psum_scatter(total, "ctx", scatter_dimension=axis, tiled=True)


def layer_backward(output_grad, saved, weights, gain, layout):
    tables, mask, flags = layout
    (qkv_own, out_own, gate_up_own, down_own), (qkv_other, out_other, gate_up_other, down_other) = weights
    (
        parts,
        statistics_first,
        normed_first,
        queries,
        key_values,
        attended,
        attended_low,
        log_total,
        hidden,
        statistics_second,
        normed_second,
        gate,
        up,
        activated,
    ) = saved

    def token_sum(left, right):
        return lax.dot_general(left, right, CONTRACT_FIRST, preferred_element_type=F32)

    activated_grad = dot_back(output_grad[0], down_own) + dot_back(output_grad[1], down_other)
    down_grad = scatter_weight_grad(
        shared_weight_grad(
            token_sum(activated, output_grad[0]), token_sum(activated, output_grad[1])
        ),
        1,
    )
    sigmoid = jax.nn.sigmoid(gate)
    swish = gate * sigmoid
    gate_grad = (activated_grad * up * (sigmoid * (1.0 + gate * (1.0 - sigmoid)))).astype(BF16)
    up_grad = (activated_grad * swish).astype(BF16)
    second_grad = [
        tp_sum(dot_back(gate_grad, weight[0]) + dot_back(up_grad, weight[1])).astype(F32)
        for weight in (gate_up_own, gate_up_other)
    ]
    gate_up_grad = scatter_weight_grad(
        shared_weight_grad(
            *[
                jnp.stack([token_sum(normed, gate_grad), token_sum(normed, up_grad)])
                for normed in normed_second
            ]
        ),
        1,
    )
    moved, gain_second, shift_second = norm_backward(hidden, statistics_second, gain[1], second_grad)
    hidden_grad = [g.astype(F32) + m for g, m in zip(output_grad, moved)]
    branch_grad = [part.astype(BF16) for part in hidden_grad]
    attended_grad = (
        dot_back(branch_grad[0], out_own) + dot_back(branch_grad[1], out_other)
    ).astype(BF16)
    out_grad = scatter_weight_grad(
        shared_weight_grad(*[token_sum(attended_low, part) for part in branch_grad]), 1
    )
    query_grad, key_grads, value_grads = attend_back(
        queries, key_values, mask, flags, attended_grad, attended, log_total
    )
    key_grad = rotate(scatter_chunks(key_grads), tables, -1.0).astype(BF16)
    value_grad = scatter_chunks(value_grads).astype(BF16)
    query_grad = rotate(query_grad, tables, -1.0).astype(BF16)
    projected = (query_grad, key_grad, value_grad)
    first_grad = [
        tp_sum(sum(dot_back(part, weight[c]) for c, part in enumerate(projected))).astype(F32)
        for weight in (qkv_own, qkv_other)
    ]
    qkv_grad = scatter_weight_grad(
        shared_weight_grad(
            *[
                jnp.stack([token_sum(normed, part) for part in projected])
                for normed in normed_first
            ]
        ),
        1,
    )
    bias_grad = jnp.stack([jnp.sum(part.astype(F32), axis=0) for part in projected])
    moved, gain_first, shift_first = norm_backward(
        [part.astype(F32) for part in parts], statistics_first, gain[0], first_grad
    )
    input_grad = [g + m for g, m in zip(hidden_grad, moved)]
    weight_grads = (qkv_grad, out_grad, gate_up_grad, down_grad)
    small_grads = (
        [jnp.stack(pair) for pair in zip(gain_first, gain_second)],
        [jnp.stack(pair) for pair in zip(shift_first, shift_second)],
        bias_grad,
    )
    return input_grad, weight_grads, small_grads


def body(
    inputs,
    cotangent,
    lengths,
    norm_gains,
    norm_shifts,
    qkv_weight,
    qkv_bias,
    out_weight,
    gate_up_weight,
    down_weight,
):
    core = lax.axis_index("section")
    place_index = lax.axis_index("ctx")
    rank = lax.axis_index("tp")
    ranks = lax.axis_size("tp")
    count = lax.axis_size("ctx")
    rows, features = inputs.shape[1:]
    width = qkv_weight.shape[3]
    far = count // 2
    batch = place_index // far
    position = jnp.bitwise_xor(place_index, core * far)
    first_core = core == 0
    both = ("section", "ctx")

    def by_core(zero, one):
        return jnp.where(first_core, zero, one)

    def pick(array, index, axis=0):
        return lax.dynamic_index_in_dim(array, index, axis, keepdims=False)

    def reorder(block):
        pieces = block.reshape(ranks, rows // ranks, -1)
        return jnp.concatenate(
            [pick(pieces, jnp.bitwise_xor(rank, k)) for k in range(ranks)], axis=0
        )

    def split(array):
        cut = array.reshape(array.shape[:-1] + (count, 2, features // (2 * count)))
        shape = array.shape[:-1] + (features // 2,)
        axis = cut.ndim - 2
        return [pick(cut, index, axis).reshape(shape) for index in (core, 1 - core)]

    def unsplit(parts):
        lead = parts[0].shape[:-1]
        cut = [part.reshape(lead + (count, features // (2 * count))) for part in parts]
        joined = jnp.stack([by_core(cut[0], cut[1]), by_core(cut[1], cut[0])], axis=len(lead) + 1)
        return joined.reshape(lead + (features,))

    def take_in(array):
        arrived = lax.ppermute(
            pick(array, 1 - batch), both, [(count + i, count + (i ^ far)) for i in range(count)]
        )
        return split(reorder(by_core(pick(array, batch), arrived)))

    length_row = pick(lengths, batch)
    ends = jnp.cumsum(length_row)
    piece_rows = rows // ranks
    inner = jnp.arange(rows, dtype=jnp.int32)
    inner = jnp.bitwise_xor(inner // piece_rows, rank) * piece_rows + inner % piece_rows

    def documents(place):
        passed = ends[None, :] <= place[:, None]
        document = jnp.sum(passed.astype(jnp.int32), axis=1)
        begins = jnp.sum(jnp.where(passed, length_row[None, :], 0), axis=1)
        return document, place - begins

    query_place = position * rows + inner
    query_document, local_place = documents(query_place)
    tables = rotary_tables(local_place, width)
    masks = []
    for index in range(count):
        key_place = jnp.bitwise_xor(position, index) * rows + inner
        key_document, ignored = documents(key_place)
        masks.append(
            (key_document[:, None] == query_document[None, :])
            & (key_place[:, None] <= query_place[None, :])
        )
    flags = jnp.stack([jnp.any(mask) for mask in masks]).astype(jnp.int32)
    mask = jnp.where(jnp.concatenate(masks, axis=0), 0.0, NEGATIVE).astype(F32)
    layout = (tables, mask, flags)

    def both_layers(array):
        arrived = swap_cores(array)
        return [by_core(array, arrived), by_core(arrived, array)]

    gains = [split(array) for array in both_layers(norm_gains[0])]
    shifts = [split(array) for array in both_layers(norm_shifts[0])]
    biases = both_layers(qkv_bias[0])

    def norm_rows(parts):
        return [[part[j][None] for part in parts] for j in range(2)]

    shards = ((qkv_weight[0], 1), (out_weight[0], 1), (gate_up_weight[0], 1), (down_weight[0], 1))
    layers = [[], []]
    for shard, axis in shards:
        half = shard.shape[axis] // 2
        kept = lax.dynamic_slice_in_dim(shard, core * half, half, axis)
        arrived = swap_cores(lax.dynamic_slice_in_dim(shard, (1 - core) * half, half, axis))
        layers[0].append((by_core(kept, arrived), axis))
        layers[1].append((by_core(arrived, kept), axis))
    weights = []
    previous = None
    for layer in layers:
        own, other = [], []
        for piece, axis in layer:
            if previous is not None:
                piece, previous = lax.optimization_barrier((piece, previous))
            previous = lax.all_gather(piece, "ctx", axis=axis, tiled=True)
            own.append(previous)
            other.append(swap_cores(previous))
        weights.append((own, other))

    block = take_in(inputs)
    saved = []
    outputs = []
    for layer in range(2):
        block, kept = layer_forward(
            block,
            weights[layer],
            norm_rows(gains[layer]),
            norm_rows(shifts[layer]),
            biases[layer],
            layout,
        )
        saved.append(kept)
        outputs.append(reorder(unsplit(block)))

    grad = take_in(cotangent)
    weight_grads = [None, None]
    small_grads = [None, None]
    input_grads = [None, None]
    for layer in (1, 0):
        grad_full, weight_grads[layer], small = layer_backward(
            grad, saved[layer], weights[layer], norm_rows(gains[layer]), layout
        )
        input_grads[layer] = reorder(unsplit(grad_full))
        grad = [part.astype(BF16) for part in grad_full]
        small_grads[layer] = lax.psum((unsplit(small[0]), unsplit(small[1]), small[2]), both)

    def place_out(first, second):
        zero_far = lax.ppermute(
            first.astype(BF16), both, [(count + (i ^ far), i) for i in range(count)]
        )
        one_near = lax.ppermute(second, both, [(i, count + i) for i in range(count)])
        one_far = lax.ppermute(
            second.astype(BF16), both, [(count + (i ^ far), count + i) for i in range(count)]
        )
        near = by_core(first, one_near)
        distant = by_core(zero_far, one_far).astype(first.dtype)
        return jnp.stack(
            [jnp.where(batch == 0, near, distant), jnp.where(batch == 0, distant, near)]
        )[None]

    def join_halves(zero, one, axis):
        to_zero = lax.ppermute(zero, "section", [(1, 0)])
        to_one = lax.ppermute(one, "section", [(0, 1)])
        low = by_core(zero, to_one)
        high = by_core(to_zero, one)
        return jnp.concatenate([low, high], axis=axis).astype(F32)[None]

    joined = [
        join_halves(zero, one, axis)
        for zero, one, (shard, axis) in zip(weight_grads[0], weight_grads[1], shards)
    ]
    small = [by_core(zero, one)[None] for zero, one in zip(small_grads[0], small_grads[1])]
    return (
        place_out(outputs[0], outputs[1]),
        place_out(input_grads[0], input_grads[1]),
        small[0],
        small[1],
        joined[0],
        small[2],
        joined[1],
        joined[2],
        joined[3],
    )


def solution(mesh):
    placed = (
        P(None, "ctx", None),
        P(None, "ctx", None),
        P(),
        P("section", None, None),
        P("section", None, None),
        P("section", None, "ctx", "tp"),
        P("section", None, "tp"),
        P("section", "tp", "ctx"),
        P("section", None, "ctx", "tp"),
        P("section", "tp", "ctx"),
    )
    return jax.shard_map(
        body,
        mesh=mesh,
        in_specs=placed,
        out_specs=(
            P("section", None, "ctx", None),
            P("section", None, "ctx", None),
            P("section", None, None),
            P("section", None, None),
            P("section", None, "ctx", "tp"),
            P("section", None, "tp"),
            P("section", "tp", "ctx"),
            P("section", None, "ctx", "tp"),
            P("section", "tp", "ctx"),
        ),
        check_vma=False,
    )
```

```python
import math

import jax
import jax.numpy as jnp
from jax import lax
from jax.experimental import pallas as pl
from jax.experimental.pallas import tpu as pltpu
from jax.sharding import PartitionSpec as P

HEAD_DIM = 64
ROTATED_ENTRIES = 16
EPSILON = 1e-05
NEGATIVE = -1e30
ROTARY_BASE = 10000.0
LANES = 128
F32 = jnp.float32
BF16 = jnp.bfloat16
CONTRACT_LAST = (((1,), (1,)), ((), ()))
CONTRACT_FIRST = (((0,), (0,)), ((), ()))
VMEM_BYTES = 48 * 1024 * 1024


def head_rows(values, head):
    lane = lax.broadcasted_iota(jnp.int32, values.shape, 1)
    return jnp.where(lane // HEAD_DIM == head, values, 0.0).astype(BF16)


def attend_kernel(chunks, flags, query_ref, bias_ref, *refs):
    full_ref, low_ref, log_ref, high, total, summed = refs[chunks:]
    rows = query_ref.shape[0]
    heads = LANES // HEAD_DIM
    scaled = query_ref[...].astype(F32) * HEAD_DIM**-0.5
    queries = [head_rows(scaled, head) for head in range(heads)]
    high[...] = jnp.full(high.shape, NEGATIVE, F32)
    total[...] = jnp.zeros(total.shape, F32)
    summed[...] = jnp.zeros(summed.shape, F32)
    for chunk in range(chunks):

        @pl.when(flags[chunk] != 0)
        def _():
            keys = refs[chunk][0]
            values = refs[chunk][1]
            for head in range(heads):
                scores = lax.dot_general(
                    keys, queries[head], CONTRACT_LAST, preferred_element_type=F32
                )
                scores = scores + bias_ref[chunk * rows : (chunk + 1) * rows, :]
                old = high[head]
                new = jnp.maximum(old, jnp.max(scores, axis=0, keepdims=True))
                weights = jnp.exp(scores - new)
                decay = jnp.exp(old - new)
                total[head] = total[head] * decay + jnp.sum(weights, axis=0, keepdims=True)
                summed[head] = summed[head] * decay + lax.dot_general(
                    values, weights.astype(BF16), CONTRACT_FIRST, preferred_element_type=F32
                )
                high[head] = new

    row = lax.broadcasted_iota(jnp.int32, (LANES, rows), 0)
    merged = jnp.zeros((LANES, rows), F32)
    for head in range(heads):
        merged = jnp.where(row // HEAD_DIM == head, summed[head] / total[head], merged)
        log_ref[0, head : head + 1, :] = high[head] + jnp.log(total[head])
    merged = merged.T
    full_ref[...] = merged
    low_ref[...] = merged.astype(BF16)


def column_spec(rows):
    return pl.BlockSpec((rows, LANES), lambda pair, flags: (0, pair))


def double_spec(rows):
    return pl.BlockSpec((2, rows, LANES), lambda pair, flags: (0, 0, pair))


def attend(queries, key_values, bias, flags):
    rows, width = queries.shape
    chunks = len(key_values)
    pairs = width // LANES
    heads = LANES // HEAD_DIM
    own = column_spec(rows)
    return pl.pallas_call(
        lambda *refs: attend_kernel(chunks, *refs),
        out_shape=(
            jax.ShapeDtypeStruct((rows, width), F32),
            jax.ShapeDtypeStruct((rows, width), BF16),
            jax.ShapeDtypeStruct((pairs, heads, rows), F32),
        ),
        grid_spec=pltpu.PrefetchScalarGridSpec(
            num_scalar_prefetch=1,
            grid=(pairs,),
            in_specs=[own, pl.BlockSpec(bias.shape, lambda pair, flags: (0, 0))]
            + [double_spec(rows)] * chunks,
            out_specs=(
                own,
                own,
                pl.BlockSpec((1, heads, rows), lambda pair, flags: (pair, 0, 0)),
            ),
            scratch_shapes=[
                pltpu.VMEM((heads, 1, rows), F32),
                pltpu.VMEM((heads, 1, rows), F32),
                pltpu.VMEM((heads, LANES, rows), F32),
            ],
        ),
        compiler_params=pltpu.CompilerParams(vmem_limit_bytes=VMEM_BYTES),
        cost_estimate=pl.CostEstimate(
            flops=4 * chunks * rows * rows * width * 2,
            bytes_accessed=2 * chunks * rows * width * 2 + bias.size * 4,
            transcendentals=0,
        ),
        name="attend",
    )(flags, queries, bias, *key_values)


def attend_back_kernel(chunks, flags, query_ref, bias_ref, grad_ref, full_ref, log_ref, *refs):
    query_grad_ref = refs[chunks]
    grad_refs = refs[chunks + 1 : 2 * chunks + 1]
    summed = refs[2 * chunks + 1]
    rows = query_ref.shape[0]
    heads = LANES // HEAD_DIM
    scale = HEAD_DIM**-0.5
    scaled = query_ref[...].astype(F32) * scale
    grad = grad_ref[...].astype(F32)
    product = (grad * full_ref[...]).T
    queries = [head_rows(scaled, head) for head in range(heads)]
    grads = [head_rows(grad, head) for head in range(heads)]
    deltas = [
        jnp.sum(product[head * HEAD_DIM : (head + 1) * HEAD_DIM, :], axis=0, keepdims=True)
        for head in range(heads)
    ]
    summed[...] = jnp.zeros(summed.shape, F32)
    for chunk in range(chunks):

        @pl.when(flags[chunk] != 0)
        def _():
            keys = refs[chunk][0]
            values = refs[chunk][1]
            key_float = keys.astype(F32)
            key_grad = jnp.zeros((rows, LANES), F32)
            value_grad = jnp.zeros((rows, LANES), F32)
            query_grad = summed[...]
            for head in range(heads):
                scores = lax.dot_general(
                    keys, queries[head], CONTRACT_LAST, preferred_element_type=F32
                )
                scores = scores + bias_ref[chunk * rows : (chunk + 1) * rows, :]
                weights = jnp.exp(scores - log_ref[0, head : head + 1, :])
                weight_grad = lax.dot_general(
                    values, grads[head], CONTRACT_LAST, preferred_element_type=F32
                )
                score_grad = (weights * (weight_grad - deltas[head])).astype(BF16)
                value_grad = value_grad + jnp.dot(
                    weights.astype(BF16), grads[head], preferred_element_type=F32
                )
                key_grad = key_grad + jnp.dot(
                    score_grad, queries[head], preferred_element_type=F32
                )
                query_grad = query_grad + lax.dot_general(
                    head_rows(key_float, head),
                    score_grad,
                    CONTRACT_FIRST,
                    preferred_element_type=F32,
                )
            summed[...] = query_grad
            grad_refs[chunk][0] = key_grad.astype(BF16)
            grad_refs[chunk][1] = value_grad.astype(BF16)

        @pl.when(flags[chunk] == 0)
        def _():
            grad_refs[chunk][...] = jnp.zeros((2, rows, LANES), BF16)

    query_grad_ref[...] = summed[...].T * scale


def attend_back(queries, key_values, bias, flags, grad, full, log_total):
    rows, width = queries.shape
    chunks = len(key_values)
    pairs = width // LANES
    heads = LANES // HEAD_DIM
    own = column_spec(rows)
    results = pl.pallas_call(
        lambda *refs: attend_back_kernel(chunks, *refs),
        out_shape=[jax.ShapeDtypeStruct((rows, width), F32)]
        + [jax.ShapeDtypeStruct((2, rows, width), BF16)] * chunks,
        grid_spec=pltpu.PrefetchScalarGridSpec(
            num_scalar_prefetch=1,
            grid=(pairs,),
            in_specs=[
                own,
                pl.BlockSpec(bias.shape, lambda pair, flags: (0, 0)),
                own,
                own,
                pl.BlockSpec((1, heads, rows), lambda pair, flags: (pair, 0, 0)),
            ]
            + [double_spec(rows)] * chunks,
            out_specs=[own] + [double_spec(rows)] * chunks,
            scratch_shapes=[pltpu.VMEM((LANES, rows), F32)],
        ),
        compiler_params=pltpu.CompilerParams(vmem_limit_bytes=VMEM_BYTES),
        cost_estimate=pl.CostEstimate(
            flops=10 * chunks * rows * rows * width * 2,
            bytes_accessed=4 * chunks * rows * width * 2 + bias.size * 4,
            transcendentals=0,
        ),
        name="attend_back",
    )(flags, queries, bias, grad, full, log_total, *key_values)
    return results[0], results[1:]


def swap_cores(block):
    return lax.ppermute(block, "section", [(0, 1), (1, 0)])


def exchange(block, axis, bit):
    return lax.ppermute(block, axis, [(i, i ^ bit) for i in range(lax.axis_size(axis))])


def after(value, *others):
    return lax.optimization_barrier((value, others))[0]


def tp_scatter(partial):
    ranks = lax.axis_size("tp")
    rows, width = partial.shape
    pieces = partial.reshape(ranks, rows // ranks, width)
    total = pieces[0].astype(F32)
    for k in range(1, ranks):
        total = total + exchange(pieces[k], "tp", k).astype(F32)
    return total


def tp_gather(piece):
    ranks = lax.axis_size("tp")
    return jnp.concatenate([piece] + [exchange(piece, "tp", k) for k in range(1, ranks)], axis=0)


def across(blocks, bit, upward):
    count = lax.axis_size("ctx")
    pairs = [(i, i ^ bit) for i in range(count)]
    if bit == count // 4:
        pairs = [(i, j) for i, j in pairs if (step_of(i, count) < step_of(j, count)) == upward]
    return [lax.ppermute(block, "ctx", pairs) for block in blocks]


def step_of(index, count):
    return index if index < count // 2 else count - 1 - index


def gather_chunks(own):
    count = lax.axis_size("ctx")
    blocks = [own]
    bit = 1
    while bit < count // 2:
        blocks = blocks + across(blocks, bit, True)
        bit *= 2
    arrived = [swap_cores(block) for block in blocks]
    return [block for pair in zip(blocks, arrived) for block in pair]


def scatter_chunks(blocks):
    count = lax.axis_size("ctx")
    arrived = [swap_cores(block) for block in blocks[1::2]]
    blocks = [
        mine.astype(F32) + other.astype(F32) for mine, other in zip(blocks[::2], arrived)
    ]
    bit = count // 4
    while bit >= 1:
        arrived = across([block.astype(BF16) for block in blocks[bit:]], bit, False)
        blocks = [mine + other.astype(F32) for mine, other in zip(blocks[:bit], arrived)]
        bit //= 2
    return blocks[0]


def norm_forward(values, gain, shift):
    mean = jnp.mean(values, axis=1, keepdims=True)
    centred = values - mean
    spread = jnp.mean(centred * centred, axis=1, keepdims=True)
    inverse = lax.rsqrt(spread + EPSILON)
    return (centred * inverse * gain + shift).astype(BF16), (mean, inverse)


def norm_backward(values, statistics, gain, grad):
    mean, inverse = statistics
    hat = (values - mean) * inverse
    scaled = gain * grad
    first = jnp.mean(scaled, axis=1, keepdims=True)
    second = jnp.mean(scaled * hat, axis=1, keepdims=True)
    moved = inverse * (scaled - first - hat * second)
    return moved, jnp.sum(grad * hat, axis=0), jnp.sum(grad, axis=0)


def rotary_tables(local_place, width):
    half = ROTATED_ENTRIES // 2
    entry = jnp.arange(HEAD_DIM)
    frequency = jnp.exp(
        -((entry % half).astype(F32) * 2.0 / ROTATED_ENTRIES) * math.log(ROTARY_BASE)
    )
    frequency = jnp.where(entry < ROTATED_ENTRIES, frequency, 0.0)
    angle = local_place.astype(F32)[:, None] * frequency[None, :]
    sine = jnp.sin(angle)
    tables = (
        jnp.cos(angle),
        jnp.where(entry < half, -sine, 0.0),
        jnp.where(entry >= half, sine, 0.0),
    )
    return tuple(jnp.tile(table, (1, width // HEAD_DIM)) for table in tables)


def rotate(values, tables, sign):
    half = ROTATED_ENTRIES // 2
    cosine, low, high = tables
    return (
        values * cosine
        + jnp.roll(values, -half, axis=1) * (low * sign)
        + jnp.roll(values, half, axis=1) * (high * sign)
    )


def dot(left, right):
    return jnp.dot(left, right, preferred_element_type=F32)


def dot_back(left, right):
    return lax.dot_general(left, right, CONTRACT_LAST, preferred_element_type=F32)


def token_sum(left, right):
    return lax.dot_general(left, right, CONTRACT_FIRST, preferred_element_type=F32)


def into(values, halves):
    middle = values.shape[1] // 2
    return dot(values[:, :middle], halves[0]) + dot(values[:, middle:], halves[1])


def out_of(values, halves):
    return jnp.concatenate([dot_back(values, half).astype(BF16) for half in halves], axis=1)


def all_sum(value, axes):
    for axis in axes:
        bit = 1
        while bit < lax.axis_size(axis):
            value = value + exchange(value, axis, bit)
            bit *= 2
    return value


def project_forward(normed, weights, bias_row, layout):
    tables, mask, flags = layout

    def project(c):
        return into(normed, [half[c] for half in weights]) + bias_row[c][None]

    key_value = jnp.stack([rotate(project(1), tables, 1.0).astype(BF16), project(2).astype(BF16)])
    key_values = gather_chunks(key_value)
    return rotate(project(0), tables, 1.0).astype(BF16), key_values


def attention_forward(piece, queries, key_values, out_weights, layout):
    tables, mask, flags = layout
    attended, attended_low, log_total = attend(queries, key_values, mask, flags)
    partial = out_of(attended_low, [half[0] for half in out_weights])
    hidden = piece.astype(F32) + tp_scatter(partial)
    return hidden, (queries, key_values, attended, attended_low, log_total)


def gate_forward(normed, weights):
    gate, up = [into(normed, [half[c] for half in weights]) for c in range(2)]
    activated = (gate * jax.nn.sigmoid(gate) * up).astype(BF16)
    return gate, up, activated


def down_forward(hidden, activated, weights):
    partial = out_of(activated, [half[0] for half in weights])
    return (hidden + tp_scatter(partial)).astype(BF16)


def shared_weight_grad(own, other):
    arrived = swap_cores(other.astype(BF16))
    return (own + arrived.astype(F32)).astype(BF16)


def weight_grad(values, grads):
    middle = values.shape[1] // 2
    own, other = [
        jnp.stack([token_sum(half, grad) for grad in grads])
        for half in (values[:, :middle], values[:, middle:])
    ]
    return shared_weight_grad(own, other)


def scatter_weight_grad(total):
    return lax.psum_scatter(total, "ctx", scatter_dimension=1, tiled=True)


def gate_backward(grad_full, kept, down):
    gate, up, activated = kept
    activated_grad = into(grad_full, [half[0] for half in down])
    sigmoid = jax.nn.sigmoid(gate)
    swish = gate * sigmoid
    gate_grad = (activated_grad * up * (sigmoid * (1.0 + gate * (1.0 - sigmoid)))).astype(BF16)
    up_grad = (activated_grad * swish).astype(BF16)
    return gate_grad, up_grad


def feed_partial(gate_grad, up_grad, weights):
    return jnp.concatenate(
        [
            (dot_back(gate_grad, half[0]) + dot_back(up_grad, half[1])).astype(BF16)
            for half in weights
        ],
        axis=1,
    )


def projected_partial(projected, weights):
    return jnp.concatenate(
        [
            sum(dot_back(part, half[c]) for c, part in enumerate(projected)).astype(BF16)
            for half in weights
        ],
        axis=1,
    )


def body(
    inputs,
    cotangent,
    lengths,
    norm_gains,
    norm_shifts,
    qkv_weight,
    qkv_bias,
    out_weight,
    gate_up_weight,
    down_weight,
):
    core = lax.axis_index("section")
    place_index = lax.axis_index("ctx")
    rank = lax.axis_index("tp")
    ranks = lax.axis_size("tp")
    count = lax.axis_size("ctx")
    rows, features = inputs.shape[1:]
    width = qkv_weight.shape[3]
    far = count // 2
    batch = place_index // far
    position = 2 * jnp.where(batch == 0, place_index, count - 1 - place_index) + core
    first_core = core == 0
    both = ("section", "ctx")
    piece_rows = rows // ranks

    def by_core(zero, one):
        return jnp.where(first_core, zero, one)

    def pick(array, index, axis=0):
        return lax.dynamic_index_in_dim(array, index, axis, keepdims=False)

    def reorder(block):
        pieces = block.reshape(ranks, piece_rows, -1)
        return jnp.concatenate(
            [pick(pieces, jnp.bitwise_xor(rank, k)) for k in range(ranks)], axis=0
        )

    def split(array):
        cut = array.reshape(array.shape[:-1] + (count, 2, features // (2 * count)))
        shape = array.shape[:-1] + (features // 2,)
        axis = cut.ndim - 2
        return jnp.concatenate(
            [pick(cut, index, axis).reshape(shape) for index in (core, 1 - core)], axis=-1
        )

    def unsplit(array):
        lead = array.shape[:-1]
        cut = array.reshape(lead + (2, count, features // (2 * count)))
        first, second = [lax.index_in_dim(cut, j, len(lead), keepdims=False) for j in range(2)]
        joined = jnp.stack([by_core(first, second), by_core(second, first)], axis=len(lead) + 1)
        return joined.reshape(lead + (features,))

    def seat(index, half):
        step = index // 2
        return (index % 2) * count + (step if half == 0 else count - 1 - step)

    def take_in(array):
        piece = pick(pick(array, core).reshape(ranks, piece_rows, features), rank)
        pairs = [(half * count + i, seat(i, half)) for half in range(2) for i in range(count)]
        return split(lax.ppermute(piece, both, pairs))

    def send_home(layer, piece):
        piece = unsplit(piece)
        return jnp.stack(
            [
                lax.ppermute(piece, both, [(seat(i, half), layer * count + i) for i in range(count)])
                for half in range(2)
            ]
        )

    def spread_home(layer, own):
        blocks = [own]
        for k in range(1, ranks):
            pairs = [(layer * ranks + i, layer * ranks + (i ^ k)) for i in range(ranks)]
            blocks.append(lax.ppermute(own, ("section", "tp"), pairs))
        return blocks

    def assemble(zero, one, dtype):
        whole = jnp.zeros((2, rows, features), dtype)
        for k, pair in enumerate(zip(zero, one)):
            start_row = jnp.bitwise_xor(rank, k) * piece_rows
            whole = lax.dynamic_update_slice_in_dim(
                whole, by_core(*pair).astype(dtype), start_row, axis=1
            )
        return whole[None]

    length_row = pick(lengths, batch)
    ends = jnp.cumsum(length_row)
    inner = jnp.arange(rows, dtype=jnp.int32)
    inner = jnp.bitwise_xor(inner // piece_rows, rank) * piece_rows + inner % piece_rows

    def documents(place):
        passed = ends[None, :] <= place[:, None]
        document = jnp.sum(passed.astype(jnp.int32), axis=1)
        begins = jnp.sum(jnp.where(passed, length_row[None, :], 0), axis=1)
        return document, place - begins

    query_place = position * rows + inner
    query_document, local_place = documents(query_place)
    tables = rotary_tables(local_place, width)
    masks = []
    for index in range(count):
        key_place = jnp.bitwise_xor(position, index) * rows + inner
        key_document, ignored = documents(key_place)
        masks.append(
            (key_document[:, None] == query_document[None, :])
            & (key_place[:, None] <= query_place[None, :])
        )
    flags = jnp.stack([jnp.any(mask) for mask in masks]).astype(jnp.int32)
    mask = jnp.where(jnp.concatenate(masks, axis=0), 0.0, NEGATIVE).astype(F32)
    layout = (tables, mask, flags)

    def both_layers(array):
        arrived = swap_cores(array)
        return [by_core(array, arrived), by_core(arrived, array)]

    gains = [split(array) for array in both_layers(norm_gains[0])]
    shifts = [split(array) for array in both_layers(norm_shifts[0])]
    biases = both_layers(qkv_bias[0])

    def shard_halves(shard):
        half = shard.shape[1] // 2
        kept = lax.dynamic_slice_in_dim(shard, core * half, half, 1)
        arrived = swap_cores(lax.dynamic_slice_in_dim(shard, (1 - core) * half, half, 1))
        return [by_core(kept, arrived), by_core(arrived, kept)]

    def gather(piece, *others):
        return lax.all_gather(after(piece, *others), "ctx", axis=1, tiled=True)

    def halves(own, *others):
        own = after(own, *others)
        return own, swap_cores(own)

    qkv_shards = shard_halves(qkv_weight[0])
    out_shards = shard_halves(out_weight[0].T[None])
    gate_up_shards = shard_halves(gate_up_weight[0])
    down_shards = shard_halves(down_weight[0].T[None])

    start = take_in(inputs)
    normed_zero, statistics_zero = norm_forward(start.astype(F32), gains[0][0], shifts[0][0])
    normed_zero = tp_gather(normed_zero)
    attention_zero = gather(jnp.concatenate([qkv_shards[0], out_shards[0]], axis=0))
    attention_zero, normed_zero, layout = lax.optimization_barrier(
        (attention_zero, normed_zero, layout)
    )
    feed_zero = gather(jnp.concatenate([gate_up_shards[0], down_shards[0]], axis=0))
    attention_one = gather(
        jnp.concatenate([qkv_shards[1], out_shards[1]], axis=0), attention_zero
    )
    attention_halves = halves(attention_zero)
    qkv_weights = [[half[:3] for half in attention_halves], None]
    out_weights = [[half[3:] for half in attention_halves], None]
    queries_zero, key_values_zero = project_forward(normed_zero, qkv_weights[0], biases[0], layout)
    hidden_zero, kept_attention_zero = attention_forward(
        start, queries_zero, key_values_zero, out_weights[0], layout
    )
    second_zero, second_statistics_zero = norm_forward(hidden_zero, gains[0][1], shifts[0][1])
    second_zero = tp_gather(second_zero)
    grad = take_in(after(cotangent, normed_zero))
    grad_full = tp_gather(after(grad, second_zero))
    feed_zero, second_zero, grad_full = lax.optimization_barrier((feed_zero, second_zero, grad_full))
    gate_up_one = gather(gate_up_shards[1], feed_zero)
    feed_halves = halves(feed_zero)
    gate_up_weights = [[half[:2] for half in feed_halves], None]
    down_weights = [[half[2:] for half in feed_halves], None]
    kept_feed_zero = gate_forward(second_zero, gate_up_weights[0])
    middle = down_forward(hidden_zero, kept_feed_zero[2], down_weights[0])
    normed_one, statistics_one = norm_forward(middle.astype(F32), gains[1][0], shifts[1][0])
    normed_one = tp_gather(normed_one)
    attention_one, normed_one = lax.optimization_barrier((attention_one, normed_one))
    down_one = gather(down_shards[1], attention_one)
    attention_halves = halves(attention_one)
    qkv_weights[1] = [half[:3] for half in attention_halves]
    out_weights[1] = [half[3:] for half in attention_halves]
    queries_one, key_values_one = project_forward(normed_one, qkv_weights[1], biases[1], layout)
    hidden_one, kept_attention_one = attention_forward(
        middle, queries_one, key_values_one, out_weights[1], layout
    )
    second_one, second_statistics_one = norm_forward(hidden_one, gains[1][1], shifts[1][1])
    second_one = tp_gather(second_one)
    gate_up_one, second_one = lax.optimization_barrier((gate_up_one, second_one))
    gate_up_weights[1] = halves(gate_up_one)
    kept_feed_one = gate_forward(second_one, gate_up_weights[1])
    home_zero = send_home(0, after(middle, second_one))

    kept_feed = (kept_feed_zero, kept_feed_one)
    kept_attention = (kept_attention_zero, kept_attention_one)
    second_norm = (
        (hidden_zero, second_statistics_zero, gains[0][1]),
        (hidden_one, second_statistics_one, gains[1][1]),
    )
    first_norm = (
        (start.astype(F32), statistics_zero, gains[0][0]),
        (middle.astype(F32), statistics_one, gains[1][0]),
    )
    first_normed = (normed_zero, normed_one)
    second_normed = (second_zero, second_one)
    input_grads = [None, None]
    small_grads = [None, None]
    scattered = [None, None]
    tables, mask, flags = layout
    for layer in (1, 0):
        down_total = weight_grad(grad_full, [kept_feed[layer][2]])
        if layer == 1:
            down_one, down_total, grad_full = lax.optimization_barrier(
                (down_one, down_total, grad_full)
            )
            down_weights[1] = halves(down_one)
        gate_grad, up_grad = gate_backward(grad_full, kept_feed[layer], down_weights[layer])
        partial = feed_partial(gate_grad, up_grad, gate_up_weights[layer])
        down_grad = scatter_weight_grad(down_total)
        second_grad = tp_scatter(partial)
        gate_total = weight_grad(second_normed[layer], [gate_grad])
        second_grad, gate_total = lax.optimization_barrier((second_grad, gate_total))
        moved, gain_second, shift_second = norm_backward(*second_norm[layer], second_grad)
        hidden_grad = grad.astype(F32) + moved
        branch_grad = tp_gather(hidden_grad.astype(BF16))
        up_total = weight_grad(second_normed[layer], [up_grad])
        branch_grad, up_total = lax.optimization_barrier((branch_grad, up_total))
        if layer == 1:
            branch_grad, home_zero = lax.optimization_barrier((branch_grad, home_zero))
            home_zero = spread_home(0, home_zero)
            last = down_forward(hidden_one, after(kept_feed_one[2], branch_grad), down_weights[1])
        if layer == 0:
            branch_grad = after(branch_grad, attention_grad)
        queries, key_values, attended, attended_low, log_total = kept_attention[layer]
        attended_grad = into(branch_grad, [half[0] for half in out_weights[layer]]).astype(BF16)
        if layer == 0:
            attended_grad, home_one, home_grad_one = lax.optimization_barrier(
                (attended_grad, home_one, home_grad_one)
            )
            home_one = spread_home(1, home_one)
            home_grad_one = spread_home(1, home_grad_one)
        query_grad, key_value_grads = attend_back(
            queries, key_values, mask, flags, attended_grad, attended, log_total
        )
        query_grad, key_value_grads = after((query_grad, key_value_grads), down_grad)
        gate_weight_grad = scatter_weight_grad(gate_total)
        key_value_grad = after(scatter_chunks(key_value_grads), gate_weight_grad)
        up_weight_grad = scatter_weight_grad(after(up_total, key_value_grad))
        out_total = weight_grad(branch_grad, [attended_low])
        query_grad = rotate(query_grad, tables, -1.0).astype(BF16)
        key_value_grad, out_total, query_grad = lax.optimization_barrier(
            (key_value_grad, out_total, query_grad)
        )
        if layer == 1:
            key_value_grad, home_zero, last = lax.optimization_barrier(
                (key_value_grad, home_zero, last)
            )
            home_one = send_home(1, last)
        else:
            key_value_grad, home_one, home_grad_one = lax.optimization_barrier(
                (key_value_grad, home_one, home_grad_one)
            )
        key_grad = rotate(key_value_grad[0], tables, -1.0).astype(BF16)
        projected = (query_grad, key_grad, key_value_grad[1].astype(BF16))
        partial = projected_partial(projected, qkv_weights[layer])
        first_grad = tp_scatter(partial)
        qkv_total = weight_grad(first_normed[layer], projected)
        first_grad, qkv_total = lax.optimization_barrier((first_grad, qkv_total))
        attention_total = jnp.concatenate([qkv_total, out_total])
        if layer == 0:
            attention_total = after(attention_total, up_weight_grad)
        attention_grad = scatter_weight_grad(attention_total)
        bias_grad = jnp.stack([jnp.sum(part.astype(F32), axis=0) for part in projected])
        moved, gain_first, shift_first = norm_backward(*first_norm[layer], first_grad)
        grad = (hidden_grad + moved).astype(BF16)
        input_grads[layer] = grad
        if layer == 1:
            grad_full = after(tp_gather(grad), up_weight_grad)
            home_grad_one = send_home(1, after(grad, grad_full))
        norm_grads = unsplit(jnp.stack([gain_first, gain_second, shift_first, shift_second]))
        small_grads[layer] = (norm_grads, bias_grad)
        gate_up_grad = jnp.concatenate([gate_weight_grad, up_weight_grad])
        scattered[layer] = (attention_grad, gate_up_grad, down_grad)

    norm_grads, bias_grads = [
        jnp.stack(parts) for parts in zip(*[after(small, attention_total) for small in small_grads])
    ]
    packed = jnp.concatenate([norm_grads.reshape(-1, LANES), bias_grads.reshape(-1, LANES)])
    packed = all_sum(packed, ("section", "ctx"))
    norm_rows = norm_grads.size // LANES
    norm_grads = all_sum(packed[:norm_rows], ("tp",)).reshape(norm_grads.shape)
    bias_grads = packed[norm_rows:].reshape(bias_grads.shape)
    norm_grads, bias_grads = by_core(norm_grads[0], norm_grads[1]), by_core(bias_grads[0], bias_grads[1])
    home_grad_zero = spread_home(0, send_home(0, after(input_grads[0], attention_total)))
    layer_outputs = assemble(home_zero, home_one, BF16)
    grad_outputs = assemble(home_grad_zero, home_grad_one, F32)

    def join_halves(zero, one):
        to_zero = lax.ppermute(zero, "section", [(1, 0)])
        to_one = lax.ppermute(one, "section", [(0, 1)])
        low = by_core(zero, to_one)
        high = by_core(to_zero, one)
        return jnp.concatenate([low, high], axis=1).astype(F32)

    joined = [join_halves(zero, one) for zero, one in zip(*scattered)]
    return (
        layer_outputs,
        grad_outputs,
        norm_grads[None, :2],
        norm_grads[None, 2:],
        joined[0][None, :3],
        bias_grads[None],
        joined[0][3].T[None],
        joined[1][None],
        joined[2][0].T[None],
    )


def solution(mesh):
    placed = (
        P(None, "ctx", None),
        P(None, "ctx", None),
        P(),
        P("section", None, None),
        P("section", None, None),
        P("section", None, "ctx", "tp"),
        P("section", None, "tp"),
        P("section", "tp", "ctx"),
        P("section", None, "ctx", "tp"),
        P("section", "tp", "ctx"),
    )
    return jax.shard_map(
        body,
        mesh=mesh,
        in_specs=placed,
        out_specs=(
            P("section", None, "ctx", None),
            P("section", None, "ctx", None),
            P("section", None, None),
            P("section", None, None),
            P("section", None, "ctx", "tp"),
            P("section", None, "tp"),
            P("section", "tp", "ctx"),
            P("section", None, "ctx", "tp"),
            P("section", "tp", "ctx"),
        ),
        check_vma=False,
    )
```

```python
import math

import jax
import jax.numpy as jnp
from jax import lax
from jax.experimental import pallas as pl
from jax.experimental.pallas import tpu as pltpu
from jax.sharding import PartitionSpec as P

HEAD_DIM = 64
ROTATED_ENTRIES = 16
EPSILON = 1e-05
NEGATIVE = -1e30
ROTARY_BASE = 10000.0
LANES = 128
F32 = jnp.float32
BF16 = jnp.bfloat16
CONTRACT_LAST = (((1,), (1,)), ((), ()))
CONTRACT_FIRST = (((0,), (0,)), ((), ()))
VMEM_BYTES = 48 * 1024 * 1024


def head_rows(values, head):
    lane = lax.broadcasted_iota(jnp.int32, values.shape, 1)
    return jnp.where(lane // HEAD_DIM == head, values, 0.0).astype(BF16)


def attend_kernel(chunks, flags, query_ref, bias_ref, *refs):
    full_ref, low_ref, log_ref, high, total, summed = refs[chunks:]
    rows = query_ref.shape[0]
    heads = LANES // HEAD_DIM
    scaled = query_ref[...].astype(F32) * HEAD_DIM**-0.5
    queries = [head_rows(scaled, head) for head in range(heads)]
    high[...] = jnp.full(high.shape, NEGATIVE, F32)
    total[...] = jnp.zeros(total.shape, F32)
    summed[...] = jnp.zeros(summed.shape, F32)
    for chunk in range(chunks):

        @pl.when(flags[chunk] != 0)
        def _():
            keys = refs[chunk][0]
            values = refs[chunk][1]
            for head in range(heads):
                scores = lax.dot_general(
                    keys, queries[head], CONTRACT_LAST, preferred_element_type=F32
                )
                scores = scores + bias_ref[chunk * rows : (chunk + 1) * rows, :]
                old = high[head]
                new = jnp.maximum(old, jnp.max(scores, axis=0, keepdims=True))
                weights = jnp.exp(scores - new)
                decay = jnp.exp(old - new)
                total[head] = total[head] * decay + jnp.sum(weights, axis=0, keepdims=True)
                summed[head] = summed[head] * decay + lax.dot_general(
                    values, weights.astype(BF16), CONTRACT_FIRST, preferred_element_type=F32
                )
                high[head] = new

    row = lax.broadcasted_iota(jnp.int32, (LANES, rows), 0)
    merged = jnp.zeros((LANES, rows), F32)
    for head in range(heads):
        merged = jnp.where(row // HEAD_DIM == head, summed[head] / total[head], merged)
        log_ref[0, head : head + 1, :] = high[head] + jnp.log(total[head])
    merged = merged.T
    full_ref[...] = merged
    low_ref[...] = merged.astype(BF16)


def column_spec(rows):
    return pl.BlockSpec((rows, LANES), lambda pair, flags: (0, pair))


def double_spec(rows):
    return pl.BlockSpec((2, rows, LANES), lambda pair, flags: (0, 0, pair))


def attend(queries, key_values, bias, flags):
    rows, width = queries.shape
    chunks = len(key_values)
    pairs = width // LANES
    heads = LANES // HEAD_DIM
    own = column_spec(rows)
    return pl.pallas_call(
        lambda *refs: attend_kernel(chunks, *refs),
        out_shape=(
            jax.ShapeDtypeStruct((rows, width), F32),
            jax.ShapeDtypeStruct((rows, width), BF16),
            jax.ShapeDtypeStruct((pairs, heads, rows), F32),
        ),
        grid_spec=pltpu.PrefetchScalarGridSpec(
            num_scalar_prefetch=1,
            grid=(pairs,),
            in_specs=[own, pl.BlockSpec(bias.shape, lambda pair, flags: (0, 0))]
            + [double_spec(rows)] * chunks,
            out_specs=(
                own,
                own,
                pl.BlockSpec((1, heads, rows), lambda pair, flags: (pair, 0, 0)),
            ),
            scratch_shapes=[
                pltpu.VMEM((heads, 1, rows), F32),
                pltpu.VMEM((heads, 1, rows), F32),
                pltpu.VMEM((heads, LANES, rows), F32),
            ],
        ),
        compiler_params=pltpu.CompilerParams(vmem_limit_bytes=VMEM_BYTES),
        cost_estimate=pl.CostEstimate(
            flops=4 * chunks * rows * rows * width * 2,
            bytes_accessed=2 * chunks * rows * width * 2 + bias.size * 4,
            transcendentals=0,
        ),
        name="attend",
    )(flags, queries, bias, *key_values)


def attend_back_kernel(chunks, flags, query_ref, bias_ref, grad_ref, full_ref, log_ref, *refs):
    query_grad_ref = refs[chunks]
    grad_refs = refs[chunks + 1 : 2 * chunks + 1]
    summed = refs[2 * chunks + 1]
    rows = query_ref.shape[0]
    heads = LANES // HEAD_DIM
    scale = HEAD_DIM**-0.5
    scaled = query_ref[...].astype(F32) * scale
    grad = grad_ref[...].astype(F32)
    product = (grad * full_ref[...]).T
    queries = [head_rows(scaled, head) for head in range(heads)]
    grads = [head_rows(grad, head) for head in range(heads)]
    deltas = [
        jnp.sum(product[head * HEAD_DIM : (head + 1) * HEAD_DIM, :], axis=0, keepdims=True)
        for head in range(heads)
    ]
    summed[...] = jnp.zeros(summed.shape, F32)
    for chunk in range(chunks):

        @pl.when(flags[chunk] != 0)
        def _():
            keys = refs[chunk][0]
            values = refs[chunk][1]
            key_float = keys.astype(F32)
            key_grad = jnp.zeros((rows, LANES), F32)
            value_grad = jnp.zeros((rows, LANES), F32)
            query_grad = summed[...]
            for head in range(heads):
                scores = lax.dot_general(
                    keys, queries[head], CONTRACT_LAST, preferred_element_type=F32
                )
                scores = scores + bias_ref[chunk * rows : (chunk + 1) * rows, :]
                weights = jnp.exp(scores - log_ref[0, head : head + 1, :])
                weight_grad = lax.dot_general(
                    values, grads[head], CONTRACT_LAST, preferred_element_type=F32
                )
                score_grad = (weights * (weight_grad - deltas[head])).astype(BF16)
                value_grad = value_grad + jnp.dot(
                    weights.astype(BF16), grads[head], preferred_element_type=F32
                )
                key_grad = key_grad + jnp.dot(
                    score_grad, queries[head], preferred_element_type=F32
                )
                query_grad = query_grad + lax.dot_general(
                    head_rows(key_float, head),
                    score_grad,
                    CONTRACT_FIRST,
                    preferred_element_type=F32,
                )
            summed[...] = query_grad
            grad_refs[chunk][0] = key_grad.astype(BF16)
            grad_refs[chunk][1] = value_grad.astype(BF16)

        @pl.when(flags[chunk] == 0)
        def _():
            grad_refs[chunk][...] = jnp.zeros((2, rows, LANES), BF16)

    query_grad_ref[...] = summed[...].T * scale


def attend_back(queries, key_values, bias, flags, grad, full, log_total):
    rows, width = queries.shape
    chunks = len(key_values)
    pairs = width // LANES
    heads = LANES // HEAD_DIM
    own = column_spec(rows)
    results = pl.pallas_call(
        lambda *refs: attend_back_kernel(chunks, *refs),
        out_shape=[jax.ShapeDtypeStruct((rows, width), F32)]
        + [jax.ShapeDtypeStruct((2, rows, width), BF16)] * chunks,
        grid_spec=pltpu.PrefetchScalarGridSpec(
            num_scalar_prefetch=1,
            grid=(pairs,),
            in_specs=[
                own,
                pl.BlockSpec(bias.shape, lambda pair, flags: (0, 0)),
                own,
                own,
                pl.BlockSpec((1, heads, rows), lambda pair, flags: (pair, 0, 0)),
            ]
            + [double_spec(rows)] * chunks,
            out_specs=[own] + [double_spec(rows)] * chunks,
            scratch_shapes=[pltpu.VMEM((LANES, rows), F32)],
        ),
        compiler_params=pltpu.CompilerParams(vmem_limit_bytes=VMEM_BYTES),
        cost_estimate=pl.CostEstimate(
            flops=10 * chunks * rows * rows * width * 2,
            bytes_accessed=4 * chunks * rows * width * 2 + bias.size * 4,
            transcendentals=0,
        ),
        name="attend_back",
    )(flags, queries, bias, grad, full, log_total, *key_values)
    return results[0], results[1:]


def swap_cores(block):
    return lax.ppermute(block, "section", [(0, 1), (1, 0)])


def exchange(block, axis, bit):
    return lax.ppermute(block, axis, [(i, i ^ bit) for i in range(lax.axis_size(axis))])


def after(value, *others):
    return lax.optimization_barrier((value, others))[0]


def tp_scatter(partial):
    ranks = lax.axis_size("tp")
    rows, width = partial.shape
    pieces = partial.reshape(ranks, rows // ranks, width)
    total = pieces[0].astype(F32)
    for k in range(1, ranks):
        total = total + exchange(pieces[k], "tp", k).astype(F32)
    return total


def tp_gather(piece):
    ranks = lax.axis_size("tp")
    return jnp.concatenate([piece] + [exchange(piece, "tp", k) for k in range(1, ranks)], axis=0)


def across(blocks, bit, upward):
    count = lax.axis_size("ctx")
    pairs = [(i, i ^ bit) for i in range(count)]
    if bit == count // 4:
        pairs = [(i, j) for i, j in pairs if (step_of(i, count) < step_of(j, count)) == upward]
    return [lax.ppermute(block, "ctx", pairs) for block in blocks]


def step_of(index, count):
    return index if index < count // 2 else count - 1 - index


def gather_chunks(own):
    count = lax.axis_size("ctx")
    blocks = [own]
    bit = 1
    while bit < count // 2:
        blocks = blocks + across(blocks, bit, True)
        bit *= 2
    arrived = [swap_cores(block) for block in blocks]
    return [block for pair in zip(blocks, arrived) for block in pair]


def scatter_chunks(blocks):
    count = lax.axis_size("ctx")
    arrived = [swap_cores(block) for block in blocks[1::2]]
    blocks = [
        mine.astype(F32) + other.astype(F32) for mine, other in zip(blocks[::2], arrived)
    ]
    bit = count // 4
    while bit >= 1:
        arrived = across([block.astype(BF16) for block in blocks[bit:]], bit, False)
        blocks = [mine + other.astype(F32) for mine, other in zip(blocks[:bit], arrived)]
        bit //= 2
    return blocks[0]


def norm_forward(values, gain, shift):
    mean = jnp.mean(values, axis=1, keepdims=True)
    centred = values - mean
    spread = jnp.mean(centred * centred, axis=1, keepdims=True)
    inverse = lax.rsqrt(spread + EPSILON)
    return (centred * inverse * gain + shift).astype(BF16), (mean, inverse)


def norm_backward(values, statistics, gain, grad):
    mean, inverse = statistics
    hat = (values - mean) * inverse
    scaled = gain * grad
    first = jnp.mean(scaled, axis=1, keepdims=True)
    second = jnp.mean(scaled * hat, axis=1, keepdims=True)
    moved = inverse * (scaled - first - hat * second)
    return moved, jnp.sum(grad * hat, axis=0), jnp.sum(grad, axis=0)


def rotary_tables(local_place, width):
    half = ROTATED_ENTRIES // 2
    entry = jnp.arange(HEAD_DIM)
    frequency = jnp.exp(
        -((entry % half).astype(F32) * 2.0 / ROTATED_ENTRIES) * math.log(ROTARY_BASE)
    )
    frequency = jnp.where(entry < ROTATED_ENTRIES, frequency, 0.0)
    angle = local_place.astype(F32)[:, None] * frequency[None, :]
    sine = jnp.sin(angle)
    tables = (
        jnp.cos(angle),
        jnp.where(entry < half, -sine, 0.0),
        jnp.where(entry >= half, sine, 0.0),
    )
    return tuple(jnp.tile(table, (1, width // HEAD_DIM)) for table in tables)


def rotate(values, tables, sign):
    half = ROTATED_ENTRIES // 2
    cosine, low, high = tables
    return (
        values * cosine
        + jnp.roll(values, -half, axis=1) * (low * sign)
        + jnp.roll(values, half, axis=1) * (high * sign)
    )


def dot(left, right):
    return jnp.dot(left, right, preferred_element_type=F32)


def dot_back(left, right):
    return lax.dot_general(left, right, CONTRACT_LAST, preferred_element_type=F32)


def token_sum(left, right):
    return lax.dot_general(left, right, CONTRACT_FIRST, preferred_element_type=F32)


def into(values, halves):
    middle = values.shape[1] // 2
    return dot(values[:, :middle], halves[0]) + dot(values[:, middle:], halves[1])


def out_of(values, halves):
    return jnp.concatenate([dot_back(values, half).astype(BF16) for half in halves], axis=1)


def all_sum(value, axes):
    for axis in axes:
        bit = 1
        while bit < lax.axis_size(axis):
            value = value + exchange(value, axis, bit)
            bit *= 2
    return value


def project_forward(normed, weights, bias_row, layout):
    tables, mask, flags = layout

    def project(c):
        return into(normed, [half[c] for half in weights]) + bias_row[c][None]

    key_value = jnp.stack([rotate(project(1), tables, 1.0).astype(BF16), project(2).astype(BF16)])
    key_values = gather_chunks(key_value)
    return rotate(project(0), tables, 1.0).astype(BF16), key_values


def attention_forward(piece, queries, key_values, out_weights, layout):
    tables, mask, flags = layout
    attended, attended_low, log_total = attend(queries, key_values, mask, flags)
    partial = out_of(attended_low, [half[0] for half in out_weights])
    hidden = piece.astype(F32) + tp_scatter(partial)
    return hidden, (queries, key_values, attended, attended_low, log_total)


def gate_forward(normed, weights):
    gate, up = [into(normed, [half[c] for half in weights]) for c in range(2)]
    activated = (gate * jax.nn.sigmoid(gate) * up).astype(BF16)
    return gate, up, activated


def down_forward(hidden, activated, weights):
    partial = out_of(activated, [half[0] for half in weights])
    return (hidden + tp_scatter(partial)).astype(BF16)


def shared_weight_grad(own, other):
    arrived = swap_cores(other.astype(BF16))
    return (own + arrived.astype(F32)).astype(BF16)


def weight_grad(values, grads):
    middle = values.shape[1] // 2
    own, other = [
        jnp.stack([token_sum(half, grad) for grad in grads])
        for half in (values[:, :middle], values[:, middle:])
    ]
    return shared_weight_grad(own, other)


def scatter_weight_grad(total):
    return lax.psum_scatter(total, "ctx", scatter_dimension=1, tiled=True)


def gate_backward(grad_full, kept, down):
    gate, up, activated = kept
    activated_grad = into(grad_full, [half[0] for half in down])
    sigmoid = jax.nn.sigmoid(gate)
    swish = gate * sigmoid
    gate_grad = (activated_grad * up * (sigmoid * (1.0 + gate * (1.0 - sigmoid)))).astype(BF16)
    up_grad = (activated_grad * swish).astype(BF16)
    return gate_grad, up_grad


def feed_partial(gate_grad, up_grad, weights):
    return jnp.concatenate(
        [
            (dot_back(gate_grad, half[0]) + dot_back(up_grad, half[1])).astype(BF16)
            for half in weights
        ],
        axis=1,
    )


def projected_partial(projected, weights):
    return jnp.concatenate(
        [
            sum(dot_back(part, half[c]) for c, part in enumerate(projected)).astype(BF16)
            for half in weights
        ],
        axis=1,
    )


def body(
    inputs,
    cotangent,
    lengths,
    norm_gains,
    norm_shifts,
    qkv_weight,
    qkv_bias,
    out_weight,
    gate_up_weight,
    down_weight,
):
    core = lax.axis_index("section")
    place_index = lax.axis_index("ctx")
    rank = lax.axis_index("tp")
    ranks = lax.axis_size("tp")
    count = lax.axis_size("ctx")
    rows, features = inputs.shape[1:]
    width = qkv_weight.shape[3]
    far = count // 2
    batch = place_index // far
    position = 2 * jnp.where(batch == 0, place_index, count - 1 - place_index) + core
    first_core = core == 0
    both = ("section", "ctx")
    piece_rows = rows // ranks

    def by_core(zero, one):
        return jnp.where(first_core, zero, one)

    def pick(array, index, axis=0):
        return lax.dynamic_index_in_dim(array, index, axis, keepdims=False)

    def reorder(block):
        pieces = block.reshape(ranks, piece_rows, -1)
        return jnp.concatenate(
            [pick(pieces, jnp.bitwise_xor(rank, k)) for k in range(ranks)], axis=0
        )

    def split(array):
        cut = array.reshape(array.shape[:-1] + (count, 2, features // (2 * count)))
        shape = array.shape[:-1] + (features // 2,)
        axis = cut.ndim - 2
        return jnp.concatenate(
            [pick(cut, index, axis).reshape(shape) for index in (core, 1 - core)], axis=-1
        )

    def unsplit(array):
        lead = array.shape[:-1]
        cut = array.reshape(lead + (2, count, features // (2 * count)))
        first, second = [lax.index_in_dim(cut, j, len(lead), keepdims=False) for j in range(2)]
        joined = jnp.stack([by_core(first, second), by_core(second, first)], axis=len(lead) + 1)
        return joined.reshape(lead + (features,))

    def seat(index, half):
        step = index // 2
        return (index % 2) * count + (step if half == 0 else count - 1 - step)

    def take_in(array):
        piece = pick(pick(array, core).reshape(ranks, piece_rows, features), rank)
        pairs = [(half * count + i, seat(i, half)) for half in range(2) for i in range(count)]
        return split(lax.ppermute(piece, both, pairs))

    def send_home(layer, piece):
        piece = unsplit(piece)
        return jnp.stack(
            [
                lax.ppermute(piece, both, [(seat(i, half), layer * count + i) for i in range(count)])
                for half in range(2)
            ]
        )

    def spread_home(layer, own):
        blocks = [own]
        for k in range(1, ranks):
            pairs = [(layer * ranks + i, layer * ranks + (i ^ k)) for i in range(ranks)]
            blocks.append(lax.ppermute(own, ("section", "tp"), pairs))
        return blocks

    def assemble(blocks, dtype):
        whole = jnp.zeros((2, rows, features), dtype)
        for k, block in enumerate(blocks):
            start_row = jnp.bitwise_xor(rank, k) * piece_rows
            whole = lax.dynamic_update_slice_in_dim(
                whole, block.astype(dtype), start_row, axis=1
            )
        return whole[None]

    length_row = pick(lengths, batch)
    ends = jnp.cumsum(length_row)
    inner = jnp.arange(rows, dtype=jnp.int32)
    inner = jnp.bitwise_xor(inner // piece_rows, rank) * piece_rows + inner % piece_rows

    def documents(place):
        passed = ends[None, :] <= place[:, None]
        document = jnp.sum(passed.astype(jnp.int32), axis=1)
        begins = jnp.sum(jnp.where(passed, length_row[None, :], 0), axis=1)
        return document, place - begins

    query_place = position * rows + inner
    query_document, local_place = documents(query_place)
    tables = rotary_tables(local_place, width)
    masks = []
    for index in range(count):
        key_place = jnp.bitwise_xor(position, index) * rows + inner
        key_document, ignored = documents(key_place)
        masks.append(
            (key_document[:, None] == query_document[None, :])
            & (key_place[:, None] <= query_place[None, :])
        )
    flags = jnp.stack([jnp.any(mask) for mask in masks]).astype(jnp.int32)
    mask = jnp.where(jnp.concatenate(masks, axis=0), 0.0, NEGATIVE).astype(F32)
    layout = (tables, mask, flags)

    def both_layers(array):
        arrived = swap_cores(array)
        return [by_core(array, arrived), by_core(arrived, array)]

    gains = [split(array) for array in both_layers(norm_gains[0])]
    shifts = [split(array) for array in both_layers(norm_shifts[0])]
    biases = both_layers(qkv_bias[0])

    def shard_halves(shard):
        half = shard.shape[1] // 2
        kept = lax.dynamic_slice_in_dim(shard, core * half, half, 1)
        arrived = swap_cores(lax.dynamic_slice_in_dim(shard, (1 - core) * half, half, 1))
        return [by_core(kept, arrived), by_core(arrived, kept)]

    def gather(piece, *others):
        return lax.all_gather(after(piece, *others), "ctx", axis=1, tiled=True)

    def halves(own, *others):
        own = after(own, *others)
        return own, swap_cores(own)

    qkv_shards = shard_halves(qkv_weight[0])
    out_shards = shard_halves(out_weight[0].T[None])
    gate_up_shards = shard_halves(gate_up_weight[0])
    down_shards = shard_halves(down_weight[0].T[None])

    start = take_in(inputs)
    normed_zero, statistics_zero = norm_forward(start.astype(F32), gains[0][0], shifts[0][0])
    normed_zero = tp_gather(normed_zero)
    attention_zero = gather(jnp.concatenate([qkv_shards[0], out_shards[0]], axis=0))
    attention_zero, normed_zero, layout = lax.optimization_barrier(
        (attention_zero, normed_zero, layout)
    )
    feed_zero = gather(jnp.concatenate([gate_up_shards[0], down_shards[0]], axis=0))
    attention_one = gather(
        jnp.concatenate([qkv_shards[1], out_shards[1]], axis=0), attention_zero
    )
    attention_halves = halves(attention_zero)
    qkv_weights = [[half[:3] for half in attention_halves], None]
    out_weights = [[half[3:] for half in attention_halves], None]
    queries_zero, key_values_zero = project_forward(normed_zero, qkv_weights[0], biases[0], layout)
    hidden_zero, kept_attention_zero = attention_forward(
        start, queries_zero, key_values_zero, out_weights[0], layout
    )
    second_zero, second_statistics_zero = norm_forward(hidden_zero, gains[0][1], shifts[0][1])
    second_zero = tp_gather(second_zero)
    grad = take_in(after(cotangent, normed_zero))
    grad_full = tp_gather(after(grad, second_zero))
    feed_zero, second_zero, grad_full = lax.optimization_barrier((feed_zero, second_zero, grad_full))
    gate_up_one = gather(gate_up_shards[1], feed_zero)
    feed_halves = halves(feed_zero)
    gate_up_weights = [[half[:2] for half in feed_halves], None]
    down_weights = [[half[2:] for half in feed_halves], None]
    kept_feed_zero = gate_forward(second_zero, gate_up_weights[0])
    middle = down_forward(hidden_zero, kept_feed_zero[2], down_weights[0])
    normed_one, statistics_one = norm_forward(middle.astype(F32), gains[1][0], shifts[1][0])
    normed_one = tp_gather(normed_one)
    attention_one, normed_one = lax.optimization_barrier((attention_one, normed_one))
    down_one = gather(down_shards[1], attention_one)
    attention_halves = halves(attention_one)
    qkv_weights[1] = [half[:3] for half in attention_halves]
    out_weights[1] = [half[3:] for half in attention_halves]
    queries_one, key_values_one = project_forward(normed_one, qkv_weights[1], biases[1], layout)
    hidden_one, kept_attention_one = attention_forward(
        middle, queries_one, key_values_one, out_weights[1], layout
    )
    second_one, second_statistics_one = norm_forward(hidden_one, gains[1][1], shifts[1][1])
    second_one = tp_gather(second_one)
    gate_up_one, second_one = lax.optimization_barrier((gate_up_one, second_one))
    gate_up_weights[1] = halves(gate_up_one)
    kept_feed_one = gate_forward(second_one, gate_up_weights[1])
    home_zero = send_home(0, after(middle, second_one))

    kept_feed = (kept_feed_zero, kept_feed_one)
    kept_attention = (kept_attention_zero, kept_attention_one)
    second_norm = (
        (hidden_zero, second_statistics_zero, gains[0][1]),
        (hidden_one, second_statistics_one, gains[1][1]),
    )
    first_norm = (
        (start.astype(F32), statistics_zero, gains[0][0]),
        (middle.astype(F32), statistics_one, gains[1][0]),
    )
    first_normed = (normed_zero, normed_one)
    second_normed = (second_zero, second_one)
    input_grads = [None, None]
    small_grads = [None, None]
    scattered = [None, None]
    tables, mask, flags = layout
    for layer in (1, 0):
        down_total = weight_grad(grad_full, [kept_feed[layer][2]])
        if layer == 1:
            down_one, down_total, grad_full = lax.optimization_barrier(
                (down_one, down_total, grad_full)
            )
            down_weights[1] = halves(down_one)
        gate_grad, up_grad = gate_backward(grad_full, kept_feed[layer], down_weights[layer])
        partial = feed_partial(gate_grad, up_grad, gate_up_weights[layer])
        down_grad = scatter_weight_grad(down_total)
        second_grad = tp_scatter(partial)
        gate_total = weight_grad(second_normed[layer], [gate_grad])
        second_grad, gate_total = lax.optimization_barrier((second_grad, gate_total))
        moved, gain_second, shift_second = norm_backward(*second_norm[layer], second_grad)
        hidden_grad = grad.astype(F32) + moved
        branch_grad = tp_gather(hidden_grad.astype(BF16))
        up_total = weight_grad(second_normed[layer], [up_grad])
        branch_grad, up_total = lax.optimization_barrier((branch_grad, up_total))
        if layer == 1:
            branch_grad, home_zero = lax.optimization_barrier((branch_grad, home_zero))
            home_zero = spread_home(0, home_zero)
        if layer == 0:
            branch_grad = after(branch_grad, attention_grad)
        queries, key_values, attended, attended_low, log_total = kept_attention[layer]
        attended_grad = into(branch_grad, [half[0] for half in out_weights[layer]]).astype(BF16)
        if layer == 0:
            last = down_forward(
                hidden_one, after(kept_feed_one[2], attended_grad), down_weights[1]
            )
        query_grad, key_value_grads = attend_back(
            queries, key_values, mask, flags, attended_grad, attended, log_total
        )
        query_grad, key_value_grads = after((query_grad, key_value_grads), down_grad)
        gate_weight_grad = scatter_weight_grad(gate_total)
        key_value_grad = after(scatter_chunks(key_value_grads), gate_weight_grad)
        up_weight_grad = scatter_weight_grad(after(up_total, key_value_grad))
        if layer == 0:
            home_one = send_home(1, after(jnp.concatenate([last, input_grads[1]]), query_grad))
            key_value_grad, home_one = lax.optimization_barrier((key_value_grad, home_one))
            home_one = spread_home(1, home_one)
        out_total = weight_grad(branch_grad, [attended_low])
        query_grad = rotate(query_grad, tables, -1.0).astype(BF16)
        key_value_grad, out_total, query_grad = lax.optimization_barrier(
            (key_value_grad, out_total, query_grad)
        )
        if layer == 1:
            key_value_grad, home_zero = lax.optimization_barrier((key_value_grad, home_zero))
        key_grad = rotate(key_value_grad[0], tables, -1.0).astype(BF16)
        projected = (query_grad, key_grad, key_value_grad[1].astype(BF16))
        partial = projected_partial(projected, qkv_weights[layer])
        first_grad = tp_scatter(partial)
        qkv_total = weight_grad(first_normed[layer], projected)
        first_grad, qkv_total = lax.optimization_barrier((first_grad, qkv_total))
        bias_grad = jnp.stack([jnp.sum(part.astype(F32), axis=0) for part in projected])
        moved, gain_first, shift_first = norm_backward(*first_norm[layer], first_grad)
        grad = (hidden_grad + moved).astype(BF16)
        input_grads[layer] = grad
        attention_total = jnp.concatenate([qkv_total, out_total])
        if layer == 0:
            home_grad, home_one, attention_total = lax.optimization_barrier(
                (send_home(0, grad), home_one, attention_total)
            )
        attention_grad = scatter_weight_grad(attention_total)
        if layer == 1:
            grad_full = after(tp_gather(grad), up_weight_grad)
        norm_grads = unsplit(jnp.stack([gain_first, gain_second, shift_first, shift_second]))
        small_grads[layer] = (norm_grads, bias_grad)
        gate_up_grad = jnp.concatenate([gate_weight_grad, up_weight_grad])
        scattered[layer] = (attention_grad, gate_up_grad, down_grad)

    norm_grads, bias_grads = [
        jnp.stack(parts) for parts in zip(*[after(small, attention_total) for small in small_grads])
    ]
    norm_rows = norm_grads.size // LANES
    packed = jnp.concatenate(
        [all_sum(norm_grads.reshape(-1, LANES), ("tp",)), bias_grads.reshape(-1, LANES)]
    )
    packed = all_sum(packed, ("section",))
    packed = packed + sum(exchange(packed, "ctx", k) for k in range(1, count))
    norm_grads = packed[:norm_rows].reshape(norm_grads.shape)
    bias_grads = packed[norm_rows:].reshape(bias_grads.shape)
    norm_grads, bias_grads = by_core(norm_grads[0], norm_grads[1]), by_core(bias_grads[0], bias_grads[1])
    home_grad = spread_home(0, home_grad)
    layer_outputs = assemble(
        [by_core(zero, one[:, :piece_rows]) for zero, one in zip(home_zero, home_one)], BF16
    )
    grad_outputs = assemble(
        [by_core(zero, one[:, piece_rows:]) for zero, one in zip(home_grad, home_one)], F32
    )

    def join_halves(zero, one):
        to_zero = lax.ppermute(zero, "section", [(1, 0)])
        to_one = lax.ppermute(one, "section", [(0, 1)])
        low = by_core(zero, to_one)
        high = by_core(to_zero, one)
        return jnp.concatenate([low, high], axis=1).astype(F32)

    joined = [join_halves(zero, one) for zero, one in zip(*scattered)]
    return (
        layer_outputs,
        grad_outputs,
        norm_grads[None, :2],
        norm_grads[None, 2:],
        joined[0][None, :3],
        bias_grads[None],
        joined[0][3].T[None],
        joined[1][None],
        joined[2][0].T[None],
    )


def solution(mesh):
    placed = (
        P(None, "ctx", None),
        P(None, "ctx", None),
        P(),
        P("section", None, None),
        P("section", None, None),
        P("section", None, "ctx", "tp"),
        P("section", None, "tp"),
        P("section", "tp", "ctx"),
        P("section", None, "ctx", "tp"),
        P("section", "tp", "ctx"),
    )
    return jax.shard_map(
        body,
        mesh=mesh,
        in_specs=placed,
        out_specs=(
            P("section", None, "ctx", None),
            P("section", None, "ctx", None),
            P("section", None, None),
            P("section", None, None),
            P("section", None, "ctx", "tp"),
            P("section", None, "tp"),
            P("section", "tp", "ctx"),
            P("section", None, "ctx", "tp"),
            P("section", "tp", "ctx"),
        ),
        check_vma=False,
    )
```

```python
import math

import jax
import jax.numpy as jnp
from jax import lax
from jax.experimental import pallas as pl
from jax.experimental.pallas import tpu as pltpu
from jax.sharding import PartitionSpec as P

HEAD_DIM = 64
ROTATED_ENTRIES = 16
EPSILON = 1e-05
NEGATIVE = -1e30
ROTARY_BASE = 10000.0
LANES = 128
F32 = jnp.float32
BF16 = jnp.bfloat16
CONTRACT_LAST = (((1,), (1,)), ((), ()))
CONTRACT_FIRST = (((0,), (0,)), ((), ()))
VMEM_BYTES = 48 * 1024 * 1024


def head_rows(values, head):
    lane = lax.broadcasted_iota(jnp.int32, values.shape, 1)
    return jnp.where(lane // HEAD_DIM == head, values, 0.0).astype(BF16)


def attend_kernel(chunks, flags, query_ref, bias_ref, *refs):
    full_ref, low_ref, log_ref, high, total, summed = refs[chunks:]
    rows = query_ref.shape[0]
    heads = LANES // HEAD_DIM
    scaled = query_ref[...].astype(F32) * HEAD_DIM**-0.5
    queries = [head_rows(scaled, head) for head in range(heads)]
    high[...] = jnp.full(high.shape, NEGATIVE, F32)
    total[...] = jnp.zeros(total.shape, F32)
    summed[...] = jnp.zeros(summed.shape, F32)
    for chunk in range(chunks):

        @pl.when(flags[chunk] != 0)
        def _():
            keys = refs[chunk][0]
            values = refs[chunk][1]
            for head in range(heads):
                scores = lax.dot_general(
                    keys, queries[head], CONTRACT_LAST, preferred_element_type=F32
                )
                scores = scores + bias_ref[chunk * rows : (chunk + 1) * rows, :]
                old = high[head]
                new = jnp.maximum(old, jnp.max(scores, axis=0, keepdims=True))
                weights = jnp.exp(scores - new)
                decay = jnp.exp(old - new)
                total[head] = total[head] * decay + jnp.sum(weights, axis=0, keepdims=True)
                summed[head] = summed[head] * decay + lax.dot_general(
                    values, weights.astype(BF16), CONTRACT_FIRST, preferred_element_type=F32
                )
                high[head] = new

    row = lax.broadcasted_iota(jnp.int32, (LANES, rows), 0)
    merged = jnp.zeros((LANES, rows), F32)
    for head in range(heads):
        merged = jnp.where(row // HEAD_DIM == head, summed[head] / total[head], merged)
        log_ref[0, head : head + 1, :] = high[head] + jnp.log(total[head])
    merged = merged.T
    full_ref[...] = merged
    low_ref[...] = merged.astype(BF16)


def column_spec(rows):
    return pl.BlockSpec((rows, LANES), lambda pair, flags: (0, pair))


def double_spec(rows):
    return pl.BlockSpec((2, rows, LANES), lambda pair, flags: (0, 0, pair))


def attend(queries, key_values, bias, flags):
    rows, width = queries.shape
    chunks = len(key_values)
    pairs = width // LANES
    heads = LANES // HEAD_DIM
    own = column_spec(rows)
    return pl.pallas_call(
        lambda *refs: attend_kernel(chunks, *refs),
        out_shape=(
            jax.ShapeDtypeStruct((rows, width), F32),
            jax.ShapeDtypeStruct((rows, width), BF16),
            jax.ShapeDtypeStruct((pairs, heads, rows), F32),
        ),
        grid_spec=pltpu.PrefetchScalarGridSpec(
            num_scalar_prefetch=1,
            grid=(pairs,),
            in_specs=[own, pl.BlockSpec(bias.shape, lambda pair, flags: (0, 0))]
            + [double_spec(rows)] * chunks,
            out_specs=(
                own,
                own,
                pl.BlockSpec((1, heads, rows), lambda pair, flags: (pair, 0, 0)),
            ),
            scratch_shapes=[
                pltpu.VMEM((heads, 1, rows), F32),
                pltpu.VMEM((heads, 1, rows), F32),
                pltpu.VMEM((heads, LANES, rows), F32),
            ],
        ),
        compiler_params=pltpu.CompilerParams(vmem_limit_bytes=VMEM_BYTES),
        cost_estimate=pl.CostEstimate(
            flops=4 * chunks * rows * rows * width * 2,
            bytes_accessed=2 * chunks * rows * width * 2 + bias.size * 4,
            transcendentals=0,
        ),
        name="attend",
    )(flags, queries, bias, *key_values)


def attend_back_kernel(chunks, flags, query_ref, bias_ref, grad_ref, full_ref, log_ref, *refs):
    query_grad_ref = refs[chunks]
    grad_refs = refs[chunks + 1 : 2 * chunks + 1]
    summed = refs[2 * chunks + 1]
    rows = query_ref.shape[0]
    heads = LANES // HEAD_DIM
    scale = HEAD_DIM**-0.5
    scaled = query_ref[...].astype(F32) * scale
    grad = grad_ref[...].astype(F32)
    product = (grad * full_ref[...]).T
    queries = [head_rows(scaled, head) for head in range(heads)]
    grads = [head_rows(grad, head) for head in range(heads)]
    deltas = [
        jnp.sum(product[head * HEAD_DIM : (head + 1) * HEAD_DIM, :], axis=0, keepdims=True)
        for head in range(heads)
    ]
    summed[...] = jnp.zeros(summed.shape, F32)
    for chunk in range(chunks):

        @pl.when(flags[chunk] != 0)
        def _():
            keys = refs[chunk][0]
            values = refs[chunk][1]
            key_float = keys.astype(F32)
            key_grad = jnp.zeros((rows, LANES), F32)
            value_grad = jnp.zeros((rows, LANES), F32)
            query_grad = summed[...]
            for head in range(heads):
                scores = lax.dot_general(
                    keys, queries[head], CONTRACT_LAST, preferred_element_type=F32
                )
                scores = scores + bias_ref[chunk * rows : (chunk + 1) * rows, :]
                weights = jnp.exp(scores - log_ref[0, head : head + 1, :])
                weight_grad = lax.dot_general(
                    values, grads[head], CONTRACT_LAST, preferred_element_type=F32
                )
                score_grad = (weights * (weight_grad - deltas[head])).astype(BF16)
                value_grad = value_grad + jnp.dot(
                    weights.astype(BF16), grads[head], preferred_element_type=F32
                )
                key_grad = key_grad + jnp.dot(
                    score_grad, queries[head], preferred_element_type=F32
                )
                query_grad = query_grad + lax.dot_general(
                    head_rows(key_float, head),
                    score_grad,
                    CONTRACT_FIRST,
                    preferred_element_type=F32,
                )
            summed[...] = query_grad
            grad_refs[chunk][0] = key_grad.astype(BF16)
            grad_refs[chunk][1] = value_grad.astype(BF16)

        @pl.when(flags[chunk] == 0)
        def _():
            grad_refs[chunk][...] = jnp.zeros((2, rows, LANES), BF16)

    query_grad_ref[...] = summed[...].T * scale


def attend_back(queries, key_values, bias, flags, grad, full, log_total):
    rows, width = queries.shape
    chunks = len(key_values)
    pairs = width // LANES
    heads = LANES // HEAD_DIM
    own = column_spec(rows)
    results = pl.pallas_call(
        lambda *refs: attend_back_kernel(chunks, *refs),
        out_shape=[jax.ShapeDtypeStruct((rows, width), F32)]
        + [jax.ShapeDtypeStruct((2, rows, width), BF16)] * chunks,
        grid_spec=pltpu.PrefetchScalarGridSpec(
            num_scalar_prefetch=1,
            grid=(pairs,),
            in_specs=[
                own,
                pl.BlockSpec(bias.shape, lambda pair, flags: (0, 0)),
                own,
                own,
                pl.BlockSpec((1, heads, rows), lambda pair, flags: (pair, 0, 0)),
            ]
            + [double_spec(rows)] * chunks,
            out_specs=[own] + [double_spec(rows)] * chunks,
            scratch_shapes=[pltpu.VMEM((LANES, rows), F32)],
        ),
        compiler_params=pltpu.CompilerParams(vmem_limit_bytes=VMEM_BYTES),
        cost_estimate=pl.CostEstimate(
            flops=10 * chunks * rows * rows * width * 2,
            bytes_accessed=4 * chunks * rows * width * 2 + bias.size * 4,
            transcendentals=0,
        ),
        name="attend_back",
    )(flags, queries, bias, grad, full, log_total, *key_values)
    return results[0], results[1:]


def swap_cores(block):
    return lax.ppermute(block, "section", [(0, 1), (1, 0)])


def exchange(block, axis, bit):
    return lax.ppermute(block, axis, [(i, i ^ bit) for i in range(lax.axis_size(axis))])


def after(value, *others):
    return lax.optimization_barrier((value, others))[0]


def tp_scatter(halves):
    ranks = lax.axis_size("tp")
    rows, width = halves[0].shape
    first, second = [half.reshape(ranks, rows // ranks, width) for half in halves]
    if ranks != 4:
        both = jnp.concatenate([first, second], axis=2)
        total = both[0].astype(F32)
        for k in range(1, ranks):
            total = total + exchange(both[k], "tp", k).astype(F32)
        return total
    near = exchange(jnp.stack([first[1], first[3]]), "tp", 1).astype(F32)
    far = exchange(second[2:], "tp", 2).astype(F32)
    across_first = exchange((first[2].astype(F32) + near[1]).astype(BF16), "tp", 2)
    across_second = exchange((second[1].astype(F32) + far[1]).astype(BF16), "tp", 1)
    return jnp.concatenate(
        [
            first[0].astype(F32) + near[0] + across_first.astype(F32),
            second[0].astype(F32) + far[0] + across_second.astype(F32),
        ],
        axis=1,
    )


def tp_gather(piece):
    ranks = lax.axis_size("tp")
    middle = piece.shape[1] // 2
    first, second = piece[:, :middle], piece[:, middle:]
    if ranks != 4:
        blocks = [piece] + [exchange(piece, "tp", k) for k in range(1, ranks)]
        whole = jnp.concatenate(blocks, axis=0)
        return [whole[:, :middle], whole[:, middle:]]
    first_far = exchange(first, "tp", 2)
    second_near = exchange(second, "tp", 1)
    first_rest = exchange(jnp.stack([first, first_far]), "tp", 1)
    second_rest = exchange(jnp.concatenate([second, second_near]), "tp", 2)
    return [
        jnp.concatenate([first, first_rest[0], first_far, first_rest[1]]),
        jnp.concatenate([second, second_near, second_rest]),
    ]


def across(blocks, bit, upward):
    count = lax.axis_size("ctx")
    pairs = [(i, i ^ bit) for i in range(count)]
    if bit == count // 4:
        pairs = [(i, j) for i, j in pairs if (step_of(i, count) < step_of(j, count)) == upward]
    return [lax.ppermute(block, "ctx", pairs) for block in blocks]


def step_of(index, count):
    return index if index < count // 2 else count - 1 - index


def gather_chunks(own):
    count = lax.axis_size("ctx")
    blocks = [own]
    bit = 1
    while bit < count // 2:
        blocks = blocks + across(blocks, bit, True)
        bit *= 2
    arrived = [swap_cores(block) for block in blocks]
    return [block for pair in zip(blocks, arrived) for block in pair]


def scatter_chunks(blocks):
    count = lax.axis_size("ctx")
    arrived = [swap_cores(block) for block in blocks[1::2]]
    blocks = [
        mine.astype(F32) + other.astype(F32) for mine, other in zip(blocks[::2], arrived)
    ]
    bit = count // 4
    while bit >= 1:
        arrived = across([block.astype(BF16) for block in blocks[bit:]], bit, False)
        blocks = [mine + other.astype(F32) for mine, other in zip(blocks[:bit], arrived)]
        bit //= 2
    return blocks[0]


def norm_forward(values, gain, shift):
    mean = jnp.mean(values, axis=1, keepdims=True)
    centred = values - mean
    spread = jnp.mean(centred * centred, axis=1, keepdims=True)
    inverse = lax.rsqrt(spread + EPSILON)
    return (centred * inverse * gain + shift).astype(BF16), (mean, inverse)


def norm_backward(values, statistics, gain, grad):
    mean, inverse = statistics
    hat = (values - mean) * inverse
    scaled = gain * grad
    first = jnp.mean(scaled, axis=1, keepdims=True)
    second = jnp.mean(scaled * hat, axis=1, keepdims=True)
    moved = inverse * (scaled - first - hat * second)
    return moved, jnp.sum(grad * hat, axis=0), jnp.sum(grad, axis=0)


def rotary_tables(local_place, width):
    half = ROTATED_ENTRIES // 2
    entry = jnp.arange(HEAD_DIM)
    frequency = jnp.exp(
        -((entry % half).astype(F32) * 2.0 / ROTATED_ENTRIES) * math.log(ROTARY_BASE)
    )
    frequency = jnp.where(entry < ROTATED_ENTRIES, frequency, 0.0)
    angle = local_place.astype(F32)[:, None] * frequency[None, :]
    sine = jnp.sin(angle)
    tables = (
        jnp.cos(angle),
        jnp.where(entry < half, -sine, 0.0),
        jnp.where(entry >= half, sine, 0.0),
    )
    return tuple(jnp.tile(table, (1, width // HEAD_DIM)) for table in tables)


def rotate(values, tables, sign):
    half = ROTATED_ENTRIES // 2
    cosine, low, high = tables
    return (
        values * cosine
        + jnp.roll(values, -half, axis=1) * (low * sign)
        + jnp.roll(values, half, axis=1) * (high * sign)
    )


def dot(left, right):
    return jnp.dot(left, right, preferred_element_type=F32)


def dot_back(left, right):
    return lax.dot_general(left, right, CONTRACT_LAST, preferred_element_type=F32)


def token_sum(left, right):
    return lax.dot_general(left, right, CONTRACT_FIRST, preferred_element_type=F32)


def into(values, halves):
    return dot(values[0], halves[0]) + dot(values[1], halves[1])


def out_of(values, halves):
    return [dot_back(values, half).astype(BF16) for half in halves]


def all_sum(value, axes):
    for axis in axes:
        bit = 1
        while bit < lax.axis_size(axis):
            value = value + exchange(value, axis, bit)
            bit *= 2
    return value


def earlier_chip(normed_piece):
    if lax.axis_size("ctx") != 4:
        return None
    return across([normed_piece], 1, True)[0]


def project_forward(normed, earlier, weights, bias_row, layout):
    tables, earlier_tables, mask, flags = layout

    def project(rows, c):
        return into(rows, [half[c] for half in weights]) + bias_row[c][None]

    def key_value(rows, turn):
        return jnp.stack(
            [rotate(project(rows, 1), turn, 1.0).astype(BF16), project(rows, 2).astype(BF16)]
        )

    own = key_value(normed, tables)
    if earlier is None:
        key_values = gather_chunks(own)
    else:
        blocks = [own, key_value(earlier, earlier_tables)]
        key_values = [each for block in blocks for each in (block, swap_cores(block))]
    return rotate(project(normed, 0), tables, 1.0).astype(BF16), key_values


def attention_forward(piece, queries, key_values, out_weights, layout):
    tables, earlier_tables, mask, flags = layout
    attended, attended_low, log_total = attend(queries, key_values, mask, flags)
    partial = out_of(attended_low, [half[0] for half in out_weights])
    hidden = piece.astype(F32) + tp_scatter(partial)
    return hidden, (queries, key_values, attended, attended_low, log_total)


def gate_forward(normed, weights):
    gate, up = [into(normed, [half[c] for half in weights]) for c in range(2)]
    activated = (gate * jax.nn.sigmoid(gate) * up).astype(BF16)
    return gate, up, activated


def down_forward(hidden, activated, weights):
    partial = out_of(activated, [half[0] for half in weights])
    return (hidden + tp_scatter(partial)).astype(BF16)


def shared_weight_grad(own, other):
    arrived = swap_cores(other.astype(BF16))
    return (own + arrived.astype(F32)).astype(BF16)


def weight_grad(values, grads):
    own, other = [jnp.stack([token_sum(half, grad) for grad in grads]) for half in values]
    return shared_weight_grad(own, other)


def scatter_weight_grad(total):
    return lax.psum_scatter(total, "ctx", scatter_dimension=1, tiled=True)


def gate_backward(grad_full, kept, down):
    gate, up, activated = kept
    activated_grad = into(grad_full, [half[0] for half in down])
    sigmoid = jax.nn.sigmoid(gate)
    swish = gate * sigmoid
    gate_grad = (activated_grad * up * (sigmoid * (1.0 + gate * (1.0 - sigmoid)))).astype(BF16)
    up_grad = (activated_grad * swish).astype(BF16)
    return gate_grad, up_grad


def feed_partial(gate_grad, up_grad, weights):
    return [
        (dot_back(gate_grad, half[0]) + dot_back(up_grad, half[1])).astype(BF16)
        for half in weights
    ]


def projected_partial(projected, weights):
    return [
        sum(dot_back(part, half[c]) for c, part in enumerate(projected)).astype(BF16)
        for half in weights
    ]


def body(
    inputs,
    cotangent,
    lengths,
    norm_gains,
    norm_shifts,
    qkv_weight,
    qkv_bias,
    out_weight,
    gate_up_weight,
    down_weight,
):
    core = lax.axis_index("section")
    place_index = lax.axis_index("ctx")
    rank = lax.axis_index("tp")
    ranks = lax.axis_size("tp")
    count = lax.axis_size("ctx")
    rows, features = inputs.shape[1:]
    width = qkv_weight.shape[3]
    far = count // 2
    batch = place_index // far
    position = 2 * jnp.where(batch == 0, place_index, count - 1 - place_index) + core
    first_core = core == 0
    both = ("section", "ctx")
    piece_rows = rows // ranks

    def by_core(zero, one):
        return jnp.where(first_core, zero, one)

    def pick(array, index, axis=0):
        return lax.dynamic_index_in_dim(array, index, axis, keepdims=False)

    def reorder(block):
        pieces = block.reshape(ranks, piece_rows, -1)
        return jnp.concatenate(
            [pick(pieces, jnp.bitwise_xor(rank, k)) for k in range(ranks)], axis=0
        )

    def split(array):
        cut = array.reshape(array.shape[:-1] + (count, 2, features // (2 * count)))
        shape = array.shape[:-1] + (features // 2,)
        axis = cut.ndim - 2
        return jnp.concatenate(
            [pick(cut, index, axis).reshape(shape) for index in (core, 1 - core)], axis=-1
        )

    def unsplit(array):
        lead = array.shape[:-1]
        cut = array.reshape(lead + (2, count, features // (2 * count)))
        first, second = [lax.index_in_dim(cut, j, len(lead), keepdims=False) for j in range(2)]
        joined = jnp.stack([by_core(first, second), by_core(second, first)], axis=len(lead) + 1)
        return joined.reshape(lead + (features,))

    def seat(index, half):
        step = index // 2
        return (index % 2) * count + (step if half == 0 else count - 1 - step)

    def take_in(array):
        piece = pick(pick(array, core).reshape(ranks, piece_rows, features), rank)
        pairs = [(half * count + i, seat(i, half)) for half in range(2) for i in range(count)]
        return split(lax.ppermute(piece, both, pairs))

    def send_home(layer, piece):
        piece = unsplit(piece)
        return jnp.stack(
            [
                lax.ppermute(piece, both, [(seat(i, half), layer * count + i) for i in range(count)])
                for half in range(2)
            ]
        )

    def spread_home(layer, own):
        blocks = [own]
        for k in range(1, ranks):
            pairs = [(layer * ranks + i, layer * ranks + (i ^ k)) for i in range(ranks)]
            blocks.append(lax.ppermute(own, ("section", "tp"), pairs))
        return blocks

    def assemble(blocks, dtype):
        whole = jnp.zeros((2, rows, features), dtype)
        for k, block in enumerate(blocks):
            start_row = jnp.bitwise_xor(rank, k) * piece_rows
            whole = lax.dynamic_update_slice_in_dim(
                whole, block.astype(dtype), start_row, axis=1
            )
        return whole[None]

    length_row = pick(lengths, batch)
    ends = jnp.cumsum(length_row)
    inner = jnp.arange(rows, dtype=jnp.int32)
    inner = jnp.bitwise_xor(inner // piece_rows, rank) * piece_rows + inner % piece_rows

    def documents(place):
        passed = ends[None, :] <= place[:, None]
        document = jnp.sum(passed.astype(jnp.int32), axis=1)
        begins = jnp.sum(jnp.where(passed, length_row[None, :], 0), axis=1)
        return document, place - begins

    query_place = position * rows + inner
    query_document, local_place = documents(query_place)
    tables = rotary_tables(local_place, width)
    masks = []
    earlier_tables = None
    for index in range(count):
        key_place = jnp.bitwise_xor(position, index) * rows + inner
        key_document, key_local_place = documents(key_place)
        if index == 2 and count == 4:
            earlier_tables = rotary_tables(key_local_place, width)
        masks.append(
            (key_document[:, None] == query_document[None, :])
            & (key_place[:, None] <= query_place[None, :])
        )
    flags = jnp.stack([jnp.any(mask) for mask in masks]).astype(jnp.int32)
    mask = jnp.where(jnp.concatenate(masks, axis=0), 0.0, NEGATIVE).astype(F32)
    layout = (tables, earlier_tables, mask, flags)

    def both_layers(array):
        arrived = swap_cores(array)
        return [by_core(array, arrived), by_core(arrived, array)]

    gains = [split(array) for array in both_layers(norm_gains[0])]
    shifts = [split(array) for array in both_layers(norm_shifts[0])]
    biases = both_layers(qkv_bias[0])

    def shard_halves(shard):
        half = shard.shape[1] // 2
        kept = lax.dynamic_slice_in_dim(shard, core * half, half, 1)
        arrived = swap_cores(lax.dynamic_slice_in_dim(shard, (1 - core) * half, half, 1))
        return [by_core(kept, arrived), by_core(arrived, kept)]

    def gather(piece, *others):
        return lax.all_gather(after(piece, *others), "ctx", axis=1, tiled=True)

    def halves(own, *others):
        own = after(own, *others)
        return own, swap_cores(own)

    attention_shards = shard_halves(jnp.concatenate([qkv_weight[0], out_weight[0].T[None]]))
    gate_up_shards = shard_halves(gate_up_weight[0])
    down_shards = shard_halves(down_weight[0].T[None])

    start = take_in(inputs)
    normed_zero, statistics_zero = norm_forward(start.astype(F32), gains[0][0], shifts[0][0])
    earlier_zero = earlier_chip(normed_zero)
    normed_zero = tp_gather(normed_zero)
    if earlier_zero is not None:
        earlier_zero = tp_gather(earlier_zero)
    attention_zero = gather(attention_shards[0], start)
    attention_zero, normed_zero, earlier_zero, layout = lax.optimization_barrier(
        (attention_zero, normed_zero, earlier_zero, layout)
    )
    feed_zero = gather(jnp.concatenate([gate_up_shards[0], down_shards[0]], axis=0))
    attention_one = gather(attention_shards[1], attention_zero)
    attention_halves = halves(attention_zero)
    qkv_weights = [[half[:3] for half in attention_halves], None]
    out_weights = [[half[3:] for half in attention_halves], None]
    queries_zero, key_values_zero = project_forward(
        normed_zero, earlier_zero, qkv_weights[0], biases[0], layout
    )
    hidden_zero, kept_attention_zero = attention_forward(
        start, queries_zero, key_values_zero, out_weights[0], layout
    )
    second_zero, second_statistics_zero = norm_forward(hidden_zero, gains[0][1], shifts[0][1])
    second_zero = tp_gather(second_zero)
    grad = take_in(after(cotangent, normed_zero))
    grad_full = tp_gather(after(grad, second_zero))
    feed_zero, second_zero, grad_full = lax.optimization_barrier((feed_zero, second_zero, grad_full))
    gate_up_one = gather(gate_up_shards[1], feed_zero)
    feed_halves = halves(feed_zero)
    gate_up_weights = [[half[:2] for half in feed_halves], None]
    down_weights = [[half[2:] for half in feed_halves], None]
    kept_feed_zero = gate_forward(second_zero, gate_up_weights[0])
    middle = down_forward(hidden_zero, kept_feed_zero[2], down_weights[0])
    normed_one, statistics_one = norm_forward(middle.astype(F32), gains[1][0], shifts[1][0])
    earlier_one = earlier_chip(normed_one)
    normed_one = tp_gather(normed_one)
    if earlier_one is not None:
        earlier_one = tp_gather(earlier_one)
    attention_one, normed_one = lax.optimization_barrier((attention_one, normed_one))
    down_one = gather(down_shards[1], attention_one)
    attention_halves = halves(attention_one)
    qkv_weights[1] = [half[:3] for half in attention_halves]
    out_weights[1] = [half[3:] for half in attention_halves]
    queries_one, key_values_one = project_forward(
        normed_one, earlier_one, qkv_weights[1], biases[1], layout
    )
    hidden_one, kept_attention_one = attention_forward(
        middle, queries_one, key_values_one, out_weights[1], layout
    )
    second_one, second_statistics_one = norm_forward(hidden_one, gains[1][1], shifts[1][1])
    second_one = tp_gather(second_one)
    home_zero = send_home(0, after(middle, key_values_one))
    gate_up_one, second_one, home_zero = lax.optimization_barrier(
        (gate_up_one, second_one, home_zero)
    )
    home_zero = spread_home(0, home_zero)
    gate_up_weights[1] = halves(gate_up_one)
    kept_feed_one = gate_forward(second_one, gate_up_weights[1])

    kept_feed = (kept_feed_zero, kept_feed_one)
    kept_attention = (kept_attention_zero, kept_attention_one)
    second_norm = (
        (hidden_zero, second_statistics_zero, gains[0][1]),
        (hidden_one, second_statistics_one, gains[1][1]),
    )
    first_norm = (
        (start.astype(F32), statistics_zero, gains[0][0]),
        (middle.astype(F32), statistics_one, gains[1][0]),
    )
    first_normed = (normed_zero, normed_one)
    second_normed = (second_zero, second_one)
    input_grads = [None, None]
    small_grads = [None, None]
    scattered = [None, None]
    tables, earlier_tables, mask, flags = layout
    for layer in (1, 0):
        down_total = weight_grad(grad_full, [kept_feed[layer][2]])
        if layer == 1:
            down_one, down_total, grad_full = lax.optimization_barrier(
                (down_one, down_total, grad_full)
            )
            down_weights[1] = halves(down_one)
        gate_grad, up_grad = gate_backward(grad_full, kept_feed[layer], down_weights[layer])
        partial = feed_partial(gate_grad, up_grad, gate_up_weights[layer])
        down_grad = scatter_weight_grad(down_total)
        second_grad = tp_scatter(partial)
        gate_total = weight_grad(second_normed[layer], [gate_grad])
        second_grad, gate_total = lax.optimization_barrier((second_grad, gate_total))
        moved, gain_second, shift_second = norm_backward(*second_norm[layer], second_grad)
        hidden_grad = grad.astype(F32) + moved
        branch_grad = tp_gather(hidden_grad.astype(BF16))
        up_total = weight_grad(second_normed[layer], [up_grad])
        branch_grad, up_total = lax.optimization_barrier((branch_grad, up_total))
        if layer == 0:
            branch_grad = after(branch_grad, attention_grad)
        queries, key_values, attended, attended_low, log_total = kept_attention[layer]
        attended_grad = into(branch_grad, [half[0] for half in out_weights[layer]]).astype(BF16)
        if layer == 0:
            last = down_forward(
                hidden_one, after(kept_feed_one[2], attended_grad), down_weights[1]
            )
        query_grad, key_value_grads = attend_back(
            queries, key_values, mask, flags, attended_grad, attended, log_total
        )
        query_grad, key_value_grads = after((query_grad, key_value_grads), down_grad)
        gate_weight_grad = scatter_weight_grad(gate_total)
        key_value_grad = after(scatter_chunks(key_value_grads), gate_weight_grad)
        if layer == 0:
            home_one = send_home(1, after(jnp.concatenate([last, input_grads[1]]), query_grad))
            key_value_grad, home_one = lax.optimization_barrier((key_value_grad, home_one))
        out_total = weight_grad(branch_grad, [attended_low])
        query_grad = rotate(query_grad, tables, -1.0).astype(BF16)
        key_value_grad, out_total, query_grad = lax.optimization_barrier(
            (key_value_grad, out_total, query_grad)
        )
        up_weight_grad = scatter_weight_grad(
            after(jnp.concatenate([up_total, out_total], axis=2), key_value_grad)
        )
        key_grad = rotate(key_value_grad[0], tables, -1.0).astype(BF16)
        projected = (query_grad, key_grad, key_value_grad[1].astype(BF16))
        partial = projected_partial(projected, qkv_weights[layer])
        first_grad = tp_scatter(partial)
        qkv_total = weight_grad(first_normed[layer], projected)
        first_grad, qkv_total = lax.optimization_barrier((first_grad, qkv_total))
        bias_grad = jnp.stack([jnp.sum(part.astype(F32), axis=0) for part in projected])
        moved, gain_first, shift_first = norm_backward(*first_norm[layer], first_grad)
        grad = (hidden_grad + moved).astype(BF16)
        input_grads[layer] = grad
        attention_total = qkv_total
        if layer == 0:
            home_grad = send_home(0, grad)
        attention_grad = scatter_weight_grad(attention_total)
        if layer == 1:
            grad_full = after(tp_gather(grad), up_weight_grad)
        norm_grads = unsplit(jnp.stack([gain_first, gain_second, shift_first, shift_second]))
        small_grads[layer] = (norm_grads, bias_grad)
        feed_width = gate_weight_grad.shape[2]
        gate_up_grad = jnp.concatenate([gate_weight_grad, up_weight_grad[:, :, :feed_width]])
        out_grad = up_weight_grad[:, :, feed_width:]
        scattered[layer] = (attention_grad, out_grad, gate_up_grad, down_grad)

    norm_grads, bias_grads = [jnp.stack(parts) for parts in zip(*small_grads)]
    norm_rows = norm_grads.size // LANES
    packed = jnp.concatenate(
        [all_sum(norm_grads.reshape(-1, LANES), ("tp",)), bias_grads.reshape(-1, LANES)]
    )
    packed = all_sum(packed, ("section",))
    home_one = spread_home(1, after(home_one, packed))
    packed = after(packed, attention_grad)
    packed = packed + sum(exchange(packed, "ctx", k) for k in range(1, count))
    norm_grads = packed[:norm_rows].reshape(norm_grads.shape)
    bias_grads = packed[norm_rows:].reshape(bias_grads.shape)
    norm_grads, bias_grads = by_core(norm_grads[0], norm_grads[1]), by_core(bias_grads[0], bias_grads[1])
    home_grad = spread_home(0, home_grad)
    layer_outputs = assemble(
        [by_core(zero, one[:, :piece_rows]) for zero, one in zip(home_zero, home_one)], BF16
    )
    grad_outputs = assemble(
        [by_core(zero, one[:, piece_rows:]) for zero, one in zip(home_grad, home_one)], F32
    )

    def join_halves(zero, one):
        to_zero = lax.ppermute(zero, "section", [(1, 0)])
        to_one = lax.ppermute(one, "section", [(0, 1)])
        low = by_core(zero, to_one)
        high = by_core(to_zero, one)
        return jnp.concatenate([low, high], axis=1).astype(F32)

    joined = [join_halves(zero, one) for zero, one in zip(*scattered)]
    return (
        layer_outputs,
        grad_outputs,
        norm_grads[None, :2],
        norm_grads[None, 2:],
        joined[0][None],
        bias_grads[None],
        joined[1][0].T[None],
        joined[2][None],
        joined[3][0].T[None],
    )


def solution(mesh):
    placed = (
        P(None, "ctx", None),
        P(None, "ctx", None),
        P(),
        P("section", None, None),
        P("section", None, None),
        P("section", None, "ctx", "tp"),
        P("section", None, "tp"),
        P("section", "tp", "ctx"),
        P("section", None, "ctx", "tp"),
        P("section", "tp", "ctx"),
    )
    return jax.shard_map(
        body,
        mesh=mesh,
        in_specs=placed,
        out_specs=(
            P("section", None, "ctx", None),
            P("section", None, "ctx", None),
            P("section", None, None),
            P("section", None, None),
            P("section", None, "ctx", "tp"),
            P("section", None, "tp"),
            P("section", "tp", "ctx"),
            P("section", None, "ctx", "tp"),
            P("section", "tp", "ctx"),
        ),
        check_vma=False,
    )
```

```python
import math

import jax
import jax.numpy as jnp
from jax import lax
from jax.experimental import pallas as pl
from jax.experimental.pallas import tpu as pltpu
from jax.sharding import PartitionSpec as P

HEAD_DIM = 64
ROTATED_ENTRIES = 16
EPSILON = 1e-05
NEGATIVE = -1e30
ROTARY_BASE = 10000.0
LANES = 128
F32 = jnp.float32
BF16 = jnp.bfloat16
CONTRACT_LAST = (((1,), (1,)), ((), ()))
CONTRACT_FIRST = (((0,), (0,)), ((), ()))
VMEM_BYTES = 48 * 1024 * 1024


def head_rows(values, head):
    lane = lax.broadcasted_iota(jnp.int32, values.shape, 1)
    return jnp.where(lane // HEAD_DIM == head, values, 0.0).astype(BF16)


def attend_kernel(chunks, flags, query_ref, bias_ref, *refs):
    full_ref, low_ref, log_ref, high, total, summed = refs[chunks:]
    rows = query_ref.shape[0]
    heads = LANES // HEAD_DIM
    scaled = query_ref[...].astype(F32) * HEAD_DIM**-0.5
    queries = [head_rows(scaled, head) for head in range(heads)]
    high[...] = jnp.full(high.shape, NEGATIVE, F32)
    total[...] = jnp.zeros(total.shape, F32)
    summed[...] = jnp.zeros(summed.shape, F32)
    for chunk in range(chunks):

        @pl.when(flags[chunk] != 0)
        def _():
            keys = refs[chunk][0]
            values = refs[chunk][1]
            for head in range(heads):
                scores = lax.dot_general(
                    keys, queries[head], CONTRACT_LAST, preferred_element_type=F32
                )
                scores = scores + bias_ref[chunk * rows : (chunk + 1) * rows, :]
                old = high[head]
                new = jnp.maximum(old, jnp.max(scores, axis=0, keepdims=True))
                weights = jnp.exp(scores - new)
                decay = jnp.exp(old - new)
                total[head] = total[head] * decay + jnp.sum(weights, axis=0, keepdims=True)
                summed[head] = summed[head] * decay + lax.dot_general(
                    values, weights.astype(BF16), CONTRACT_FIRST, preferred_element_type=F32
                )
                high[head] = new

    row = lax.broadcasted_iota(jnp.int32, (LANES, rows), 0)
    merged = jnp.zeros((LANES, rows), F32)
    for head in range(heads):
        merged = jnp.where(row // HEAD_DIM == head, summed[head] / total[head], merged)
        log_ref[0, head : head + 1, :] = high[head] + jnp.log(total[head])
    merged = merged.T
    full_ref[...] = merged
    low_ref[...] = merged.astype(BF16)


def column_spec(rows):
    return pl.BlockSpec((rows, LANES), lambda pair, flags: (0, pair))


def double_spec(rows):
    return pl.BlockSpec((2, rows, LANES), lambda pair, flags: (0, 0, pair))


def attend(queries, key_values, bias, flags):
    rows, width = queries.shape
    chunks = len(key_values)
    pairs = width // LANES
    heads = LANES // HEAD_DIM
    own = column_spec(rows)
    return pl.pallas_call(
        lambda *refs: attend_kernel(chunks, *refs),
        out_shape=(
            jax.ShapeDtypeStruct((rows, width), F32),
            jax.ShapeDtypeStruct((rows, width), BF16),
            jax.ShapeDtypeStruct((pairs, heads, rows), F32),
        ),
        grid_spec=pltpu.PrefetchScalarGridSpec(
            num_scalar_prefetch=1,
            grid=(pairs,),
            in_specs=[own, pl.BlockSpec(bias.shape, lambda pair, flags: (0, 0))]
            + [double_spec(rows)] * chunks,
            out_specs=(
                own,
                own,
                pl.BlockSpec((1, heads, rows), lambda pair, flags: (pair, 0, 0)),
            ),
            scratch_shapes=[
                pltpu.VMEM((heads, 1, rows), F32),
                pltpu.VMEM((heads, 1, rows), F32),
                pltpu.VMEM((heads, LANES, rows), F32),
            ],
        ),
        compiler_params=pltpu.CompilerParams(vmem_limit_bytes=VMEM_BYTES),
        cost_estimate=pl.CostEstimate(
            flops=4 * chunks * rows * rows * width * 2,
            bytes_accessed=2 * chunks * rows * width * 2 + bias.size * 4,
            transcendentals=0,
        ),
        name="attend",
    )(flags, queries, bias, *key_values)


def attend_back_kernel(chunks, flags, query_ref, bias_ref, grad_ref, full_ref, log_ref, *refs):
    query_grad_ref = refs[chunks]
    grad_refs = refs[chunks + 1 : 2 * chunks + 1]
    summed = refs[2 * chunks + 1]
    rows = query_ref.shape[0]
    heads = LANES // HEAD_DIM
    scale = HEAD_DIM**-0.5
    scaled = query_ref[...].astype(F32) * scale
    grad = grad_ref[...].astype(F32)
    product = (grad * full_ref[...]).T
    queries = [head_rows(scaled, head) for head in range(heads)]
    grads = [head_rows(grad, head) for head in range(heads)]
    deltas = [
        jnp.sum(product[head * HEAD_DIM : (head + 1) * HEAD_DIM, :], axis=0, keepdims=True)
        for head in range(heads)
    ]
    summed[...] = jnp.zeros(summed.shape, F32)
    for chunk in range(chunks):

        @pl.when(flags[chunk] != 0)
        def _():
            keys = refs[chunk][0]
            values = refs[chunk][1]
            key_float = keys.astype(F32)
            key_grad = jnp.zeros((rows, LANES), F32)
            value_grad = jnp.zeros((rows, LANES), F32)
            query_grad = summed[...]
            for head in range(heads):
                scores = lax.dot_general(
                    keys, queries[head], CONTRACT_LAST, preferred_element_type=F32
                )
                scores = scores + bias_ref[chunk * rows : (chunk + 1) * rows, :]
                weights = jnp.exp(scores - log_ref[0, head : head + 1, :])
                weight_grad = lax.dot_general(
                    values, grads[head], CONTRACT_LAST, preferred_element_type=F32
                )
                score_grad = (weights * (weight_grad - deltas[head])).astype(BF16)
                value_grad = value_grad + jnp.dot(
                    weights.astype(BF16), grads[head], preferred_element_type=F32
                )
                key_grad = key_grad + jnp.dot(
                    score_grad, queries[head], preferred_element_type=F32
                )
                query_grad = query_grad + lax.dot_general(
                    head_rows(key_float, head),
                    score_grad,
                    CONTRACT_FIRST,
                    preferred_element_type=F32,
                )
            summed[...] = query_grad
            grad_refs[chunk][0] = key_grad.astype(BF16)
            grad_refs[chunk][1] = value_grad.astype(BF16)

        @pl.when(flags[chunk] == 0)
        def _():
            grad_refs[chunk][...] = jnp.zeros((2, rows, LANES), BF16)

    query_grad_ref[...] = summed[...].T * scale


def attend_back(queries, key_values, bias, flags, grad, full, log_total):
    rows, width = queries.shape
    chunks = len(key_values)
    pairs = width // LANES
    heads = LANES // HEAD_DIM
    own = column_spec(rows)
    results = pl.pallas_call(
        lambda *refs: attend_back_kernel(chunks, *refs),
        out_shape=[jax.ShapeDtypeStruct((rows, width), F32)]
        + [jax.ShapeDtypeStruct((2, rows, width), BF16)] * chunks,
        grid_spec=pltpu.PrefetchScalarGridSpec(
            num_scalar_prefetch=1,
            grid=(pairs,),
            in_specs=[
                own,
                pl.BlockSpec(bias.shape, lambda pair, flags: (0, 0)),
                own,
                own,
                pl.BlockSpec((1, heads, rows), lambda pair, flags: (pair, 0, 0)),
            ]
            + [double_spec(rows)] * chunks,
            out_specs=[own] + [double_spec(rows)] * chunks,
            scratch_shapes=[pltpu.VMEM((LANES, rows), F32)],
        ),
        compiler_params=pltpu.CompilerParams(vmem_limit_bytes=VMEM_BYTES),
        cost_estimate=pl.CostEstimate(
            flops=10 * chunks * rows * rows * width * 2,
            bytes_accessed=4 * chunks * rows * width * 2 + bias.size * 4,
            transcendentals=0,
        ),
        name="attend_back",
    )(flags, queries, bias, grad, full, log_total, *key_values)
    return results[0], results[1:]


def swap_cores(block):
    return lax.ppermute(block, "section", [(0, 1), (1, 0)])


def exchange(block, axis, bit):
    return lax.ppermute(block, axis, [(i, i ^ bit) for i in range(lax.axis_size(axis))])


def after(value, *others):
    return lax.optimization_barrier((value, others))[0]


def tp_scatter(halves):
    ranks = lax.axis_size("tp")
    rows, width = halves[0].shape
    first, second = [half.reshape(ranks, rows // ranks, width) for half in halves]
    if ranks != 4:
        both = jnp.concatenate([first, second], axis=2)
        total = both[0].astype(F32)
        for k in range(1, ranks):
            total = total + exchange(both[k], "tp", k).astype(F32)
        return total
    near = exchange(jnp.stack([first[1], first[3]]), "tp", 1).astype(F32)
    far = exchange(second[2:], "tp", 2).astype(F32)
    across_first = exchange((first[2].astype(F32) + near[1]).astype(BF16), "tp", 2)
    across_second = exchange((second[1].astype(F32) + far[1]).astype(BF16), "tp", 1)
    return jnp.concatenate(
        [
            first[0].astype(F32) + near[0] + across_first.astype(F32),
            second[0].astype(F32) + far[0] + across_second.astype(F32),
        ],
        axis=1,
    )


def tp_gather(piece):
    ranks = lax.axis_size("tp")
    middle = piece.shape[1] // 2
    first, second = piece[:, :middle], piece[:, middle:]
    if ranks != 4:
        blocks = [piece] + [exchange(piece, "tp", k) for k in range(1, ranks)]
        whole = jnp.concatenate(blocks, axis=0)
        return [whole[:, :middle], whole[:, middle:]]
    first_far = exchange(first, "tp", 2)
    second_near = exchange(second, "tp", 1)
    first_rest = exchange(jnp.stack([first, first_far]), "tp", 1)
    second_rest = exchange(jnp.concatenate([second, second_near]), "tp", 2)
    return [
        jnp.concatenate([first, first_rest[0], first_far, first_rest[1]]),
        jnp.concatenate([second, second_near, second_rest]),
    ]


def across(blocks, bit, upward):
    count = lax.axis_size("ctx")
    pairs = [(i, i ^ bit) for i in range(count)]
    if bit == count // 4:
        pairs = [(i, j) for i, j in pairs if (step_of(i, count) < step_of(j, count)) == upward]
    return [lax.ppermute(block, "ctx", pairs) for block in blocks]


def step_of(index, count):
    return index if index < count // 2 else count - 1 - index


def gather_chunks(own):
    count = lax.axis_size("ctx")
    blocks = [own]
    bit = 1
    while bit < count // 2:
        blocks = blocks + across(blocks, bit, True)
        bit *= 2
    arrived = [swap_cores(block) for block in blocks]
    return [block for pair in zip(blocks, arrived) for block in pair]


def scatter_chunks(blocks):
    count = lax.axis_size("ctx")
    arrived = [swap_cores(block) for block in blocks[1::2]]
    blocks = [
        mine.astype(F32) + other.astype(F32) for mine, other in zip(blocks[::2], arrived)
    ]
    bit = count // 4
    while bit >= 1:
        arrived = across([block.astype(BF16) for block in blocks[bit:]], bit, False)
        blocks = [mine + other.astype(F32) for mine, other in zip(blocks[:bit], arrived)]
        bit //= 2
    return blocks[0]


def norm_forward(values, gain, shift):
    mean = jnp.mean(values, axis=1, keepdims=True)
    centred = values - mean
    spread = jnp.mean(centred * centred, axis=1, keepdims=True)
    inverse = lax.rsqrt(spread + EPSILON)
    return (centred * inverse * gain + shift).astype(BF16), (mean, inverse)


def norm_backward(values, statistics, gain, grad):
    mean, inverse = statistics
    hat = (values - mean) * inverse
    scaled = gain * grad
    first = jnp.mean(scaled, axis=1, keepdims=True)
    second = jnp.mean(scaled * hat, axis=1, keepdims=True)
    moved = inverse * (scaled - first - hat * second)
    return moved, jnp.sum(grad * hat, axis=0), jnp.sum(grad, axis=0)


def rotary_tables(local_place, width):
    half = ROTATED_ENTRIES // 2
    entry = jnp.arange(HEAD_DIM)
    frequency = jnp.exp(
        -((entry % half).astype(F32) * 2.0 / ROTATED_ENTRIES) * math.log(ROTARY_BASE)
    )
    frequency = jnp.where(entry < ROTATED_ENTRIES, frequency, 0.0)
    angle = local_place.astype(F32)[:, None] * frequency[None, :]
    sine = jnp.sin(angle)
    tables = (
        jnp.cos(angle),
        jnp.where(entry < half, -sine, 0.0),
        jnp.where(entry >= half, sine, 0.0),
    )
    return tuple(jnp.tile(table, (1, width // HEAD_DIM)) for table in tables)


def rotate(values, tables, sign):
    half = ROTATED_ENTRIES // 2
    cosine, low, high = tables
    return (
        values * cosine
        + jnp.roll(values, -half, axis=1) * (low * sign)
        + jnp.roll(values, half, axis=1) * (high * sign)
    )


def dot(left, right):
    return jnp.dot(left, right, preferred_element_type=F32)


def dot_back(left, right):
    return lax.dot_general(left, right, CONTRACT_LAST, preferred_element_type=F32)


def token_sum(left, right):
    return lax.dot_general(left, right, CONTRACT_FIRST, preferred_element_type=F32)


def into(values, halves):
    return dot(values[0], halves[0]) + dot(values[1], halves[1])


def out_of(values, halves):
    return [dot_back(values, half).astype(BF16) for half in halves]


def all_sum(value, axes):
    for axis in axes:
        bit = 1
        while bit < lax.axis_size(axis):
            value = value + exchange(value, axis, bit)
            bit *= 2
    return value


def earlier_chip(normed_piece):
    if lax.axis_size("ctx") != 4:
        return None
    return across([normed_piece], 1, True)[0]


def project_forward(normed, earlier, weights, bias_row, layout):
    tables, earlier_tables, mask, flags = layout

    def project(rows, c):
        return into(rows, [half[c] for half in weights]) + bias_row[c][None]

    def key_value(rows, turn):
        return jnp.stack(
            [rotate(project(rows, 1), turn, 1.0).astype(BF16), project(rows, 2).astype(BF16)]
        )

    own = key_value(normed, tables)
    queries = rotate(project(normed, 0), tables, 1.0).astype(BF16)
    if earlier is None:
        return queries, gather_chunks(own)
    own, queries, earlier = lax.optimization_barrier((own, queries, earlier))
    blocks = [own, key_value(tp_gather(earlier), earlier_tables)]
    return queries, [each for block in blocks for each in (block, swap_cores(block))]


def attention_forward(piece, queries, key_values, out_weights, layout):
    tables, earlier_tables, mask, flags = layout
    attended, attended_low, log_total = attend(queries, key_values, mask, flags)
    partial = out_of(attended_low, [half[0] for half in out_weights])
    hidden = piece.astype(F32) + tp_scatter(partial)
    return hidden, (queries, key_values, attended, attended_low, log_total)


def gate_forward(normed, weights):
    gate, up = [into(normed, [half[c] for half in weights]) for c in range(2)]
    activated = (gate * jax.nn.sigmoid(gate) * up).astype(BF16)
    return gate, up, activated


def down_forward(hidden, activated, weights):
    partial = out_of(activated, [half[0] for half in weights])
    return (hidden + tp_scatter(partial)).astype(BF16)


def shared_weight_grad(own, other):
    arrived = swap_cores(other.astype(BF16))
    return (own + arrived.astype(F32)).astype(BF16)


def weight_grad(values, grads):
    own, other = [jnp.stack([token_sum(half, grad) for grad in grads]) for half in values]
    return shared_weight_grad(own, other)


def scatter_weight_grad(total):
    return lax.psum_scatter(total, "ctx", scatter_dimension=1, tiled=True)


def gate_backward(grad_full, kept, down):
    gate, up, activated = kept
    activated_grad = into(grad_full, [half[0] for half in down])
    sigmoid = jax.nn.sigmoid(gate)
    swish = gate * sigmoid
    gate_grad = (activated_grad * up * (sigmoid * (1.0 + gate * (1.0 - sigmoid)))).astype(BF16)
    up_grad = (activated_grad * swish).astype(BF16)
    return gate_grad, up_grad


def feed_partial(gate_grad, up_grad, weights):
    return [
        (dot_back(gate_grad, half[0]) + dot_back(up_grad, half[1])).astype(BF16)
        for half in weights
    ]


def projected_partial(projected, weights):
    return [
        sum(dot_back(part, half[c]) for c, part in enumerate(projected)).astype(BF16)
        for half in weights
    ]


def body(
    inputs,
    cotangent,
    lengths,
    norm_gains,
    norm_shifts,
    qkv_weight,
    qkv_bias,
    out_weight,
    gate_up_weight,
    down_weight,
):
    core = lax.axis_index("section")
    place_index = lax.axis_index("ctx")
    rank = lax.axis_index("tp")
    ranks = lax.axis_size("tp")
    count = lax.axis_size("ctx")
    rows, features = inputs.shape[1:]
    width = qkv_weight.shape[3]
    far = count // 2
    batch = place_index // far
    position = 2 * jnp.where(batch == 0, place_index, count - 1 - place_index) + core
    first_core = core == 0
    both = ("section", "ctx")
    piece_rows = rows // ranks

    def by_core(zero, one):
        return jnp.where(first_core, zero, one)

    def pick(array, index, axis=0):
        return lax.dynamic_index_in_dim(array, index, axis, keepdims=False)

    def reorder(block):
        pieces = block.reshape(ranks, piece_rows, -1)
        return jnp.concatenate(
            [pick(pieces, jnp.bitwise_xor(rank, k)) for k in range(ranks)], axis=0
        )

    def split(array):
        cut = array.reshape(array.shape[:-1] + (count, 2, features // (2 * count)))
        shape = array.shape[:-1] + (features // 2,)
        axis = cut.ndim - 2
        return jnp.concatenate(
            [pick(cut, index, axis).reshape(shape) for index in (core, 1 - core)], axis=-1
        )

    def unsplit(array):
        lead = array.shape[:-1]
        cut = array.reshape(lead + (2, count, features // (2 * count)))
        first, second = [lax.index_in_dim(cut, j, len(lead), keepdims=False) for j in range(2)]
        joined = jnp.stack([by_core(first, second), by_core(second, first)], axis=len(lead) + 1)
        return joined.reshape(lead + (features,))

    def seat(index, half):
        step = index // 2
        return (index % 2) * count + (step if half == 0 else count - 1 - step)

    def take_in(array):
        piece = pick(pick(array, core).reshape(ranks, piece_rows, features), rank)
        pairs = [(half * count + i, seat(i, half)) for half in range(2) for i in range(count)]
        return split(lax.ppermute(piece, both, pairs))

    def send_home(layer, piece):
        piece = unsplit(piece)
        return jnp.stack(
            [
                lax.ppermute(piece, both, [(seat(i, half), layer * count + i) for i in range(count)])
                for half in range(2)
            ]
        )

    def spread_home(layer, own, steps=2):
        def send(block, k):
            pairs = [(layer * ranks + i, layer * ranks + (i ^ k)) for i in range(ranks)]
            return lax.ppermute(block, ("section", "tp"), pairs)

        if ranks != 4 or steps == 1:
            return [own] + [send(own, k) for k in range(1, ranks)]
        middle = features // 2
        first, second = own[..., :middle], own[..., middle:]
        first_far, second_near = send(first, 2), send(second, 1)
        first_rest = send(jnp.stack([first, first_far]), 1)
        second_rest = send(jnp.stack([second, second_near]), 2)
        return [
            jnp.concatenate(pair, axis=-1)
            for pair in zip(
                (first, first_rest[0], first_far, first_rest[1]),
                (second, second_near, second_rest[0], second_rest[1]),
            )
        ]

    def assemble(blocks, dtype):
        whole = jnp.zeros((2, rows, features), dtype)
        for k, block in enumerate(blocks):
            start_row = jnp.bitwise_xor(rank, k) * piece_rows
            whole = lax.dynamic_update_slice_in_dim(
                whole, block.astype(dtype), start_row, axis=1
            )
        return whole[None]

    length_row = pick(lengths, batch)
    ends = jnp.cumsum(length_row)
    inner = jnp.arange(rows, dtype=jnp.int32)
    inner = jnp.bitwise_xor(inner // piece_rows, rank) * piece_rows + inner % piece_rows

    def documents(place):
        passed = ends[None, :] <= place[:, None]
        document = jnp.sum(passed.astype(jnp.int32), axis=1)
        begins = jnp.sum(jnp.where(passed, length_row[None, :], 0), axis=1)
        return document, place - begins

    query_place = position * rows + inner
    query_document, local_place = documents(query_place)
    tables = rotary_tables(local_place, width)
    masks = []
    earlier_tables = None
    for index in range(count):
        key_place = jnp.bitwise_xor(position, index) * rows + inner
        key_document, key_local_place = documents(key_place)
        if index == 2 and count == 4:
            earlier_tables = rotary_tables(key_local_place, width)
        masks.append(
            (key_document[:, None] == query_document[None, :])
            & (key_place[:, None] <= query_place[None, :])
        )
    flags = jnp.stack([jnp.any(mask) for mask in masks]).astype(jnp.int32)
    mask = jnp.where(jnp.concatenate(masks, axis=0), 0.0, NEGATIVE).astype(F32)
    layout = (tables, earlier_tables, mask, flags)

    def both_layers(array):
        arrived = swap_cores(array)
        return [by_core(array, arrived), by_core(arrived, array)]

    gains = [split(array) for array in both_layers(norm_gains[0])]
    shifts = [split(array) for array in both_layers(norm_shifts[0])]
    biases = both_layers(qkv_bias[0])

    def shard_halves(shard):
        half = shard.shape[1] // 2
        kept = lax.dynamic_slice_in_dim(shard, core * half, half, 1)
        arrived = swap_cores(lax.dynamic_slice_in_dim(shard, (1 - core) * half, half, 1))
        return [by_core(kept, arrived), by_core(arrived, kept)]

    def gather(piece, *others):
        return lax.all_gather(after(piece, *others), "ctx", axis=1, tiled=True)

    def halves(own, *others):
        own = after(own, *others)
        return own, swap_cores(own)

    attention_shards = shard_halves(jnp.concatenate([qkv_weight[0], out_weight[0].T[None]]))
    gate_up_shards = shard_halves(gate_up_weight[0])
    down_shards = shard_halves(down_weight[0].T[None])

    start = take_in(inputs)
    normed_zero, statistics_zero = norm_forward(start.astype(F32), gains[0][0], shifts[0][0])
    earlier_zero = earlier_chip(normed_zero)
    feed_shards = jnp.concatenate([gate_up_shards[0], down_shards[0]], axis=0)
    normed_zero, feed_shards, layout = lax.optimization_barrier(
        (normed_zero, feed_shards, layout)
    )
    normed_zero = tp_gather(normed_zero)
    attention_zero = gather(attention_shards[0])
    grad = take_in(after(cotangent, start))
    attention_zero, normed_zero, earlier_zero, layout, grad = lax.optimization_barrier(
        (attention_zero, normed_zero, earlier_zero, layout, grad)
    )
    feed_zero = gather(feed_shards)
    attention_halves = halves(attention_zero)
    qkv_weights = [[half[:3] for half in attention_halves], None]
    out_weights = [[half[3:] for half in attention_halves], None]
    queries_zero, key_values_zero = project_forward(
        normed_zero, earlier_zero, qkv_weights[0], biases[0], layout
    )
    hidden_zero, kept_attention_zero = attention_forward(
        start, queries_zero, key_values_zero, out_weights[0], layout
    )
    second_zero, second_statistics_zero = norm_forward(hidden_zero, gains[0][1], shifts[0][1])
    second_zero, attention_shard_one, gate_up_shard_one, down_shard_one = (
        lax.optimization_barrier(
            (second_zero, attention_shards[1], gate_up_shards[1], down_shards[1])
        )
    )
    attention_one = gather(attention_shard_one, attention_zero)
    second_zero = tp_gather(second_zero)
    grad_full = tp_gather(after(grad, hidden_zero))
    feed_zero, second_zero, grad_full = lax.optimization_barrier((feed_zero, second_zero, grad_full))
    gate_up_one = gather(gate_up_shard_one, feed_zero)
    feed_halves = halves(feed_zero)
    gate_up_weights = [[half[:2] for half in feed_halves], None]
    down_weights = [[half[2:] for half in feed_halves], None]
    kept_feed_zero = gate_forward(second_zero, gate_up_weights[0])
    middle = down_forward(hidden_zero, kept_feed_zero[2], down_weights[0])
    normed_one, statistics_one = norm_forward(middle.astype(F32), gains[1][0], shifts[1][0])
    earlier_one = earlier_chip(normed_one)
    normed_one = tp_gather(normed_one)
    attention_one, normed_one = lax.optimization_barrier((attention_one, normed_one))
    down_one = gather(down_shard_one, attention_one)
    attention_halves = halves(attention_one)
    qkv_weights[1] = [half[:3] for half in attention_halves]
    out_weights[1] = [half[3:] for half in attention_halves]
    queries_one, key_values_one = project_forward(
        normed_one, earlier_one, qkv_weights[1], biases[1], layout
    )
    hidden_one, kept_attention_one = attention_forward(
        middle, queries_one, key_values_one, out_weights[1], layout
    )
    second_one, second_statistics_one = norm_forward(hidden_one, gains[1][1], shifts[1][1])
    home_zero = send_home(0, after(middle, key_values_one))
    gate_up_one, second_one = lax.optimization_barrier((gate_up_one, second_one))
    second_one = tp_gather(second_one)
    second_one, home_zero = lax.optimization_barrier((second_one, home_zero))
    home_zero = spread_home(0, home_zero, steps=1)
    gate_up_weights[1] = halves(gate_up_one)
    kept_feed_one = gate_forward(second_one, gate_up_weights[1])

    kept_feed = (kept_feed_zero, kept_feed_one)
    kept_attention = (kept_attention_zero, kept_attention_one)
    second_norm = (
        (hidden_zero, second_statistics_zero, gains[0][1]),
        (hidden_one, second_statistics_one, gains[1][1]),
    )
    first_norm = (
        (start.astype(F32), statistics_zero, gains[0][0]),
        (middle.astype(F32), statistics_one, gains[1][0]),
    )
    first_normed = (normed_zero, normed_one)
    second_normed = (second_zero, second_one)
    input_grads = [None, None]
    small_grads = [None, None]
    scattered = [None, None]
    tables, earlier_tables, mask, flags = layout
    for layer in (1, 0):
        down_total = weight_grad(grad_full, [kept_feed[layer][2]])
        if layer == 1:
            down_one, down_total, grad_full, home_zero = lax.optimization_barrier(
                (down_one, down_total, grad_full, home_zero)
            )
            down_weights[1] = halves(down_one)
        gate_grad, up_grad = gate_backward(grad_full, kept_feed[layer], down_weights[layer])
        partial = feed_partial(gate_grad, up_grad, gate_up_weights[layer])
        down_grad = scatter_weight_grad(down_total)
        second_grad = tp_scatter(partial)
        gate_total = weight_grad(second_normed[layer], [gate_grad])
        second_grad, gate_total = lax.optimization_barrier((second_grad, gate_total))
        moved, gain_second, shift_second = norm_backward(*second_norm[layer], second_grad)
        hidden_grad = grad.astype(F32) + moved
        branch_grad = tp_gather(hidden_grad.astype(BF16))
        up_total = weight_grad(second_normed[layer], [up_grad])
        branch_grad, up_total = lax.optimization_barrier((branch_grad, up_total))
        if layer == 0:
            branch_grad = after(branch_grad, attention_grad)
        queries, key_values, attended, attended_low, log_total = kept_attention[layer]
        attended_grad = into(branch_grad, [half[0] for half in out_weights[layer]]).astype(BF16)
        if layer == 0:
            last = down_forward(
                hidden_one, after(kept_feed_one[2], attended_grad), down_weights[1]
            )
        query_grad, key_value_grads = attend_back(
            queries, key_values, mask, flags, attended_grad, attended, log_total
        )
        query_grad, key_value_grads = after((query_grad, key_value_grads), down_grad)
        gate_weight_grad = scatter_weight_grad(gate_total)
        key_value_grad = after(scatter_chunks(key_value_grads), gate_weight_grad)
        if layer == 0:
            home_one = send_home(1, after(jnp.concatenate([last, input_grads[1]]), query_grad))
            key_value_grad, home_one = lax.optimization_barrier((key_value_grad, home_one))
        out_total = weight_grad(branch_grad, [attended_low])
        query_grad = rotate(query_grad, tables, -1.0).astype(BF16)
        key_value_grad, out_total, query_grad = lax.optimization_barrier(
            (key_value_grad, out_total, query_grad)
        )
        up_weight_grad = scatter_weight_grad(
            after(jnp.concatenate([up_total, out_total], axis=2), key_value_grad)
        )
        key_grad = rotate(key_value_grad[0], tables, -1.0).astype(BF16)
        projected = (query_grad, key_grad, key_value_grad[1].astype(BF16))
        partial = projected_partial(projected, qkv_weights[layer])
        first_grad = tp_scatter(partial)
        qkv_total = weight_grad(first_normed[layer], projected)
        first_grad, qkv_total = lax.optimization_barrier((first_grad, qkv_total))
        bias_grad = jnp.stack([jnp.sum(part.astype(F32), axis=0) for part in projected])
        moved, gain_first, shift_first = norm_backward(*first_norm[layer], first_grad)
        grad = (hidden_grad + moved).astype(BF16)
        input_grads[layer] = grad
        attention_total = qkv_total
        if layer == 0:
            home_grad = send_home(0, grad)
        attention_grad = scatter_weight_grad(attention_total)
        if layer == 1:
            grad_full = after(tp_gather(grad), up_weight_grad)
        norm_grads = unsplit(jnp.stack([gain_first, gain_second, shift_first, shift_second]))
        small_grads[layer] = (norm_grads, bias_grad)
        feed_width = gate_weight_grad.shape[2]
        gate_up_grad = jnp.concatenate([gate_weight_grad, up_weight_grad[:, :, :feed_width]])
        out_grad = up_weight_grad[:, :, feed_width:]
        scattered[layer] = (attention_grad, out_grad, gate_up_grad, down_grad)

    norm_grads, bias_grads = [jnp.stack(parts) for parts in zip(*small_grads)]
    norm_rows = norm_grads.size // LANES
    norm_grads_sum = all_sum(norm_grads.reshape(-1, LANES), ("tp",))
    home_one = spread_home(1, after(home_one, norm_grads_sum))
    packed = jnp.concatenate([norm_grads_sum, bias_grads.reshape(-1, LANES)])
    packed = all_sum(packed, ("section",))
    packed = after(packed, attention_grad)
    packed = packed + sum(exchange(packed, "ctx", k) for k in range(1, count))
    norm_grads = packed[:norm_rows].reshape(norm_grads.shape)
    bias_grads = packed[norm_rows:].reshape(bias_grads.shape)
    norm_grads, bias_grads = by_core(norm_grads[0], norm_grads[1]), by_core(bias_grads[0], bias_grads[1])
    home_grad = spread_home(0, home_grad)
    layer_outputs = assemble(
        [by_core(zero, one[:, :piece_rows]) for zero, one in zip(home_zero, home_one)], BF16
    )
    grad_outputs = assemble(
        [by_core(zero, one[:, piece_rows:]) for zero, one in zip(home_grad, home_one)], F32
    )

    def join_halves(zero, one):
        to_zero = lax.ppermute(zero, "section", [(1, 0)])
        to_one = lax.ppermute(one, "section", [(0, 1)])
        low = by_core(zero, to_one)
        high = by_core(to_zero, one)
        return jnp.concatenate([low, high], axis=1).astype(F32)

    joined = [join_halves(zero, one) for zero, one in zip(*scattered)]
    return (
        layer_outputs,
        grad_outputs,
        norm_grads[None, :2],
        norm_grads[None, 2:],
        joined[0][None],
        bias_grads[None],
        joined[1][0].T[None],
        joined[2][None],
        joined[3][0].T[None],
    )


def solution(mesh):
    placed = (
        P(None, "ctx", None),
        P(None, "ctx", None),
        P(),
        P("section", None, None),
        P("section", None, None),
        P("section", None, "ctx", "tp"),
        P("section", None, "tp"),
        P("section", "tp", "ctx"),
        P("section", None, "ctx", "tp"),
        P("section", "tp", "ctx"),
    )
    return jax.shard_map(
        body,
        mesh=mesh,
        in_specs=placed,
        out_specs=(
            P("section", None, "ctx", None),
            P("section", None, "ctx", None),
            P("section", None, None),
            P("section", None, None),
            P("section", None, "ctx", "tp"),
            P("section", None, "tp"),
            P("section", "tp", "ctx"),
            P("section", None, "ctx", "tp"),
            P("section", "tp", "ctx"),
        ),
        check_vma=False,
    )
```

```python
import math

import jax
import jax.numpy as jnp
from jax import lax
from jax.experimental import pallas as pl
from jax.experimental.pallas import tpu as pltpu
from jax.sharding import PartitionSpec as P

HEAD_DIM = 64
ROTATED_ENTRIES = 16
EPSILON = 1e-05
NEGATIVE = -1e30
ROTARY_BASE = 10000.0
LANES = 128
F32 = jnp.float32
BF16 = jnp.bfloat16
CONTRACT_LAST = (((1,), (1,)), ((), ()))
CONTRACT_FIRST = (((0,), (0,)), ((), ()))
VMEM_BYTES = 48 * 1024 * 1024


def head_rows(values, head):
    lane = lax.broadcasted_iota(jnp.int32, values.shape, 1)
    return jnp.where(lane // HEAD_DIM == head, values, 0.0).astype(BF16)


def attend_kernel(chunks, flags, query_ref, bias_ref, *refs):
    full_ref, low_ref, log_ref, high, total, summed = refs[chunks:]
    rows = query_ref.shape[0]
    heads = LANES // HEAD_DIM
    scaled = query_ref[...].astype(F32) * HEAD_DIM**-0.5
    queries = [head_rows(scaled, head) for head in range(heads)]
    high[...] = jnp.full(high.shape, NEGATIVE, F32)
    total[...] = jnp.zeros(total.shape, F32)
    summed[...] = jnp.zeros(summed.shape, F32)
    for chunk in range(chunks):

        @pl.when(flags[chunk] != 0)
        def _():
            keys = refs[chunk][0]
            values = refs[chunk][1]
            for head in range(heads):
                scores = lax.dot_general(
                    keys, queries[head], CONTRACT_LAST, preferred_element_type=F32
                )
                scores = scores + bias_ref[chunk * rows : (chunk + 1) * rows, :]
                old = high[head]
                new = jnp.maximum(old, jnp.max(scores, axis=0, keepdims=True))
                weights = jnp.exp(scores - new)
                decay = jnp.exp(old - new)
                total[head] = total[head] * decay + jnp.sum(weights, axis=0, keepdims=True)
                summed[head] = summed[head] * decay + lax.dot_general(
                    values, weights.astype(BF16), CONTRACT_FIRST, preferred_element_type=F32
                )
                high[head] = new

    row = lax.broadcasted_iota(jnp.int32, (LANES, rows), 0)
    merged = jnp.zeros((LANES, rows), F32)
    for head in range(heads):
        merged = jnp.where(row // HEAD_DIM == head, summed[head] / total[head], merged)
        log_ref[0, head : head + 1, :] = high[head] + jnp.log(total[head])
    merged = merged.T
    full_ref[...] = merged
    low_ref[...] = merged.astype(BF16)


def column_spec(rows):
    return pl.BlockSpec((rows, LANES), lambda pair, flags: (0, pair))


def double_spec(rows):
    return pl.BlockSpec((2, rows, LANES), lambda pair, flags: (0, 0, pair))


def attend(queries, key_values, bias, flags):
    rows, width = queries.shape
    chunks = len(key_values)
    pairs = width // LANES
    heads = LANES // HEAD_DIM
    own = column_spec(rows)
    return pl.pallas_call(
        lambda *refs: attend_kernel(chunks, *refs),
        out_shape=(
            jax.ShapeDtypeStruct((rows, width), F32),
            jax.ShapeDtypeStruct((rows, width), BF16),
            jax.ShapeDtypeStruct((pairs, heads, rows), F32),
        ),
        grid_spec=pltpu.PrefetchScalarGridSpec(
            num_scalar_prefetch=1,
            grid=(pairs,),
            in_specs=[own, pl.BlockSpec(bias.shape, lambda pair, flags: (0, 0))]
            + [double_spec(rows)] * chunks,
            out_specs=(
                own,
                own,
                pl.BlockSpec((1, heads, rows), lambda pair, flags: (pair, 0, 0)),
            ),
            scratch_shapes=[
                pltpu.VMEM((heads, 1, rows), F32),
                pltpu.VMEM((heads, 1, rows), F32),
                pltpu.VMEM((heads, LANES, rows), F32),
            ],
        ),
        compiler_params=pltpu.CompilerParams(vmem_limit_bytes=VMEM_BYTES),
        cost_estimate=pl.CostEstimate(
            flops=4 * chunks * rows * rows * width * 2,
            bytes_accessed=2 * chunks * rows * width * 2 + bias.size * 4,
            transcendentals=0,
        ),
        name="attend",
    )(flags, queries, bias, *key_values)


def attend_back_kernel(chunks, flags, query_ref, bias_ref, grad_ref, full_ref, log_ref, *refs):
    query_grad_ref = refs[chunks]
    grad_refs = refs[chunks + 1 : 2 * chunks + 1]
    summed = refs[2 * chunks + 1]
    rows = query_ref.shape[0]
    heads = LANES // HEAD_DIM
    scale = HEAD_DIM**-0.5
    scaled = query_ref[...].astype(F32) * scale
    grad = grad_ref[...].astype(F32)
    product = (grad * full_ref[...]).T
    queries = [head_rows(scaled, head) for head in range(heads)]
    grads = [head_rows(grad, head) for head in range(heads)]
    deltas = [
        jnp.sum(product[head * HEAD_DIM : (head + 1) * HEAD_DIM, :], axis=0, keepdims=True)
        for head in range(heads)
    ]
    summed[...] = jnp.zeros(summed.shape, F32)
    for chunk in range(chunks):

        @pl.when(flags[chunk] != 0)
        def _():
            keys = refs[chunk][0]
            values = refs[chunk][1]
            key_float = keys.astype(F32)
            key_grad = jnp.zeros((rows, LANES), F32)
            value_grad = jnp.zeros((rows, LANES), F32)
            query_grad = summed[...]
            for head in range(heads):
                scores = lax.dot_general(
                    keys, queries[head], CONTRACT_LAST, preferred_element_type=F32
                )
                scores = scores + bias_ref[chunk * rows : (chunk + 1) * rows, :]
                weights = jnp.exp(scores - log_ref[0, head : head + 1, :])
                weight_grad = lax.dot_general(
                    values, grads[head], CONTRACT_LAST, preferred_element_type=F32
                )
                score_grad = (weights * (weight_grad - deltas[head])).astype(BF16)
                value_grad = value_grad + jnp.dot(
                    weights.astype(BF16), grads[head], preferred_element_type=F32
                )
                key_grad = key_grad + jnp.dot(
                    score_grad, queries[head], preferred_element_type=F32
                )
                query_grad = query_grad + lax.dot_general(
                    head_rows(key_float, head),
                    score_grad,
                    CONTRACT_FIRST,
                    preferred_element_type=F32,
                )
            summed[...] = query_grad
            grad_refs[chunk][0] = key_grad.astype(BF16)
            grad_refs[chunk][1] = value_grad.astype(BF16)

        @pl.when(flags[chunk] == 0)
        def _():
            grad_refs[chunk][...] = jnp.zeros((2, rows, LANES), BF16)

    query_grad_ref[...] = summed[...].T * scale


def attend_back(queries, key_values, bias, flags, grad, full, log_total):
    rows, width = queries.shape
    chunks = len(key_values)
    pairs = width // LANES
    heads = LANES // HEAD_DIM
    own = column_spec(rows)
    results = pl.pallas_call(
        lambda *refs: attend_back_kernel(chunks, *refs),
        out_shape=[jax.ShapeDtypeStruct((rows, width), F32)]
        + [jax.ShapeDtypeStruct((2, rows, width), BF16)] * chunks,
        grid_spec=pltpu.PrefetchScalarGridSpec(
            num_scalar_prefetch=1,
            grid=(pairs,),
            in_specs=[
                own,
                pl.BlockSpec(bias.shape, lambda pair, flags: (0, 0)),
                own,
                own,
                pl.BlockSpec((1, heads, rows), lambda pair, flags: (pair, 0, 0)),
            ]
            + [double_spec(rows)] * chunks,
            out_specs=[own] + [double_spec(rows)] * chunks,
            scratch_shapes=[pltpu.VMEM((LANES, rows), F32)],
        ),
        compiler_params=pltpu.CompilerParams(vmem_limit_bytes=VMEM_BYTES),
        cost_estimate=pl.CostEstimate(
            flops=10 * chunks * rows * rows * width * 2,
            bytes_accessed=4 * chunks * rows * width * 2 + bias.size * 4,
            transcendentals=0,
        ),
        name="attend_back",
    )(flags, queries, bias, grad, full, log_total, *key_values)
    return results[0], results[1:]


def swap_cores(block):
    return lax.ppermute(block, "section", [(0, 1), (1, 0)])


def exchange(block, axis, bit):
    return lax.ppermute(block, axis, [(i, i ^ bit) for i in range(lax.axis_size(axis))])


def after(value, *others):
    return lax.optimization_barrier((value, others))[0]


def tp_scatter(halves):
    ranks = lax.axis_size("tp")
    rows, width = halves[0].shape
    first, second = [half.reshape(ranks, rows // ranks, width) for half in halves]
    if ranks != 4:
        both = jnp.concatenate([first, second], axis=2)
        total = both[0].astype(F32)
        for k in range(1, ranks):
            total = total + exchange(both[k], "tp", k).astype(F32)
        return total
    near = exchange(jnp.stack([first[1], first[3]]), "tp", 1).astype(F32)
    far = exchange(second[2:], "tp", 2).astype(F32)
    across_first = exchange((first[2].astype(F32) + near[1]).astype(BF16), "tp", 2)
    across_second = exchange((second[1].astype(F32) + far[1]).astype(BF16), "tp", 1)
    return jnp.concatenate(
        [
            first[0].astype(F32) + near[0] + across_first.astype(F32),
            second[0].astype(F32) + far[0] + across_second.astype(F32),
        ],
        axis=1,
    )


def tp_gather(piece):
    ranks = lax.axis_size("tp")
    middle = piece.shape[1] // 2
    first, second = piece[:, :middle], piece[:, middle:]
    if ranks != 4:
        blocks = [piece] + [exchange(piece, "tp", k) for k in range(1, ranks)]
        whole = jnp.concatenate(blocks, axis=0)
        return [whole[:, :middle], whole[:, middle:]]
    first_far = exchange(first, "tp", 2)
    second_near = exchange(second, "tp", 1)
    first_rest = exchange(jnp.stack([first, first_far]), "tp", 1)
    second_rest = exchange(jnp.concatenate([second, second_near]), "tp", 2)
    return [
        jnp.concatenate([first, first_rest[0], first_far, first_rest[1]]),
        jnp.concatenate([second, second_near, second_rest]),
    ]


def across(blocks, bit, upward):
    count = lax.axis_size("ctx")
    pairs = [(i, i ^ bit) for i in range(count)]
    if bit == count // 4:
        pairs = [(i, j) for i, j in pairs if (step_of(i, count) < step_of(j, count)) == upward]
    return [lax.ppermute(block, "ctx", pairs) for block in blocks]


def step_of(index, count):
    return index if index < count // 2 else count - 1 - index


def gather_chunks(own):
    count = lax.axis_size("ctx")
    blocks = [own]
    bit = 1
    while bit < count // 2:
        blocks = blocks + across(blocks, bit, True)
        bit *= 2
    arrived = [swap_cores(block) for block in blocks]
    return [block for pair in zip(blocks, arrived) for block in pair]


def scatter_chunks(blocks):
    count = lax.axis_size("ctx")
    arrived = [swap_cores(block) for block in blocks[1::2]]
    blocks = [
        mine.astype(F32) + other.astype(F32) for mine, other in zip(blocks[::2], arrived)
    ]
    bit = count // 4
    while bit >= 1:
        arrived = across([block.astype(BF16) for block in blocks[bit:]], bit, False)
        blocks = [mine + other.astype(F32) for mine, other in zip(blocks[:bit], arrived)]
        bit //= 2
    return blocks[0]


def norm_forward(values, gain, shift):
    mean = jnp.mean(values, axis=1, keepdims=True)
    centred = values - mean
    spread = jnp.mean(centred * centred, axis=1, keepdims=True)
    inverse = lax.rsqrt(spread + EPSILON)
    return (centred * inverse * gain + shift).astype(BF16), (mean, inverse)


def norm_backward(values, statistics, gain, grad):
    mean, inverse = statistics
    hat = (values - mean) * inverse
    scaled = gain * grad
    first = jnp.mean(scaled, axis=1, keepdims=True)
    second = jnp.mean(scaled * hat, axis=1, keepdims=True)
    moved = inverse * (scaled - first - hat * second)
    return moved, jnp.sum(grad * hat, axis=0), jnp.sum(grad, axis=0)


def rotary_tables(local_place, width):
    half = ROTATED_ENTRIES // 2
    entry = jnp.arange(HEAD_DIM)
    frequency = jnp.exp(
        -((entry % half).astype(F32) * 2.0 / ROTATED_ENTRIES) * math.log(ROTARY_BASE)
    )
    frequency = jnp.where(entry < ROTATED_ENTRIES, frequency, 0.0)
    angle = local_place.astype(F32)[:, None] * frequency[None, :]
    sine = jnp.sin(angle)
    tables = (
        jnp.cos(angle),
        jnp.where(entry < half, -sine, 0.0),
        jnp.where(entry >= half, sine, 0.0),
    )
    return tuple(jnp.tile(table, (1, width // HEAD_DIM)) for table in tables)


def rotate(values, tables, sign):
    half = ROTATED_ENTRIES // 2
    cosine, low, high = tables
    return (
        values * cosine
        + jnp.roll(values, -half, axis=1) * (low * sign)
        + jnp.roll(values, half, axis=1) * (high * sign)
    )


def dot(left, right):
    return jnp.dot(left, right, preferred_element_type=F32)


def dot_back(left, right):
    return lax.dot_general(left, right, CONTRACT_LAST, preferred_element_type=F32)


def token_sum(left, right):
    return lax.dot_general(left, right, CONTRACT_FIRST, preferred_element_type=F32)


def into(values, halves):
    return dot(values[0], halves[0]) + dot(values[1], halves[1])


def out_of(values, halves):
    return [dot_back(values, half).astype(BF16) for half in halves]


def all_sum(value, axes):
    for axis in axes:
        bit = 1
        while bit < lax.axis_size(axis):
            value = value + exchange(value, axis, bit)
            bit *= 2
    return value


def earlier_chip(normed_piece):
    if lax.axis_size("ctx") != 4:
        return None
    return across([normed_piece], 1, True)[0]


def project_forward(normed, earlier, weights, bias_row, layout):
    tables, earlier_tables, mask, flags = layout

    def project(rows, c):
        return into(rows, [half[c] for half in weights]) + bias_row[c][None]

    def key_value(rows, turn):
        return jnp.stack(
            [rotate(project(rows, 1), turn, 1.0).astype(BF16), project(rows, 2).astype(BF16)]
        )

    own = key_value(normed, tables)
    queries = rotate(project(normed, 0), tables, 1.0).astype(BF16)
    if earlier is None:
        return queries, gather_chunks(own)
    own, queries, earlier = lax.optimization_barrier((own, queries, earlier))
    blocks = [own, key_value(tp_gather(earlier), earlier_tables)]
    return queries, [each for block in blocks for each in (block, swap_cores(block))]


def attention_forward(piece, queries, key_values, out_weights, layout):
    tables, earlier_tables, mask, flags = layout
    attended, attended_low, log_total = attend(queries, key_values, mask, flags)
    partial = out_of(attended_low, [half[0] for half in out_weights])
    hidden = piece.astype(F32) + tp_scatter(partial)
    return hidden, (queries, key_values, attended, attended_low, log_total)


def gate_forward(normed, weights):
    gate, up = [into(normed, [half[c] for half in weights]) for c in range(2)]
    activated = (gate * jax.nn.sigmoid(gate) * up).astype(BF16)
    return gate, up, activated


def down_forward(hidden, activated, weights):
    partial = out_of(activated, [half[0] for half in weights])
    return (hidden + tp_scatter(partial)).astype(BF16)


def shared_weight_grad(own, other):
    arrived = swap_cores(other.astype(BF16))
    return (own + arrived.astype(F32)).astype(BF16)


def weight_grad(values, grads):
    own, other = [jnp.stack([token_sum(half, grad) for grad in grads]) for half in values]
    return shared_weight_grad(own, other)


def scatter_weight_grad(total):
    return lax.psum_scatter(total, "ctx", scatter_dimension=1, tiled=True)


def gate_backward(grad_full, kept, down):
    gate, up, activated = kept
    activated_grad = into(grad_full, [half[0] for half in down])
    sigmoid = jax.nn.sigmoid(gate)
    swish = gate * sigmoid
    gate_grad = (activated_grad * up * (sigmoid * (1.0 + gate * (1.0 - sigmoid)))).astype(BF16)
    up_grad = (activated_grad * swish).astype(BF16)
    return gate_grad, up_grad


def feed_partial(gate_grad, up_grad, weights):
    return [
        (dot_back(gate_grad, half[0]) + dot_back(up_grad, half[1])).astype(BF16)
        for half in weights
    ]


def projected_partial(projected, weights):
    return [
        sum(dot_back(part, half[c]) for c, part in enumerate(projected)).astype(BF16)
        for half in weights
    ]


def body(
    inputs,
    cotangent,
    lengths,
    norm_gains,
    norm_shifts,
    qkv_weight,
    qkv_bias,
    out_weight,
    gate_up_weight,
    down_weight,
):
    core = lax.axis_index("section")
    place_index = lax.axis_index("ctx")
    rank = lax.axis_index("tp")
    ranks = lax.axis_size("tp")
    count = lax.axis_size("ctx")
    rows, features = inputs.shape[1:]
    width = qkv_weight.shape[3]
    far = count // 2
    batch = place_index // far
    position = 2 * jnp.where(batch == 0, place_index, count - 1 - place_index) + core
    first_core = core == 0
    both = ("section", "ctx")
    piece_rows = rows // ranks

    def by_core(zero, one):
        return jnp.where(first_core, zero, one)

    def pick(array, index, axis=0):
        return lax.dynamic_index_in_dim(array, index, axis, keepdims=False)

    def reorder(block):
        pieces = block.reshape(ranks, piece_rows, -1)
        return jnp.concatenate(
            [pick(pieces, jnp.bitwise_xor(rank, k)) for k in range(ranks)], axis=0
        )

    def split(array):
        cut = array.reshape(array.shape[:-1] + (count, 2, features // (2 * count)))
        shape = array.shape[:-1] + (features // 2,)
        axis = cut.ndim - 2
        return jnp.concatenate(
            [pick(cut, index, axis).reshape(shape) for index in (core, 1 - core)], axis=-1
        )

    def unsplit(array):
        lead = array.shape[:-1]
        cut = array.reshape(lead + (2, count, features // (2 * count)))
        first, second = [lax.index_in_dim(cut, j, len(lead), keepdims=False) for j in range(2)]
        joined = jnp.stack([by_core(first, second), by_core(second, first)], axis=len(lead) + 1)
        return joined.reshape(lead + (features,))

    def seat(index, half):
        step = index // 2
        return (index % 2) * count + (step if half == 0 else count - 1 - step)

    def take_in(array):
        piece = pick(pick(array, core).reshape(ranks, piece_rows, features), rank)
        pairs = [(half * count + i, seat(i, half)) for half in range(2) for i in range(count)]
        return split(lax.ppermute(piece, both, pairs))

    def send_home(layer, piece):
        piece = unsplit(piece)
        return jnp.stack(
            [
                lax.ppermute(piece, both, [(seat(i, half), layer * count + i) for i in range(count)])
                for half in range(2)
            ]
        )

    def spread_home(layer, own, steps=2):
        def send(block, k):
            pairs = [(layer * ranks + i, layer * ranks + (i ^ k)) for i in range(ranks)]
            return lax.ppermute(block, ("section", "tp"), pairs)

        if ranks != 4 or steps == 1:
            return [own] + [send(own, k) for k in range(1, ranks)]
        middle = features // 2
        first, second = own[..., :middle], own[..., middle:]
        first_far, second_near = send(first, 2), send(second, 1)
        first_rest = send(jnp.stack([first, first_far]), 1)
        second_rest = send(jnp.stack([second, second_near]), 2)
        return [
            jnp.concatenate(pair, axis=-1)
            for pair in zip(
                (first, first_rest[0], first_far, first_rest[1]),
                (second, second_near, second_rest[0], second_rest[1]),
            )
        ]

    def assemble(blocks, dtype):
        whole = jnp.zeros((2, rows, features), dtype)
        for k, block in enumerate(blocks):
            start_row = jnp.bitwise_xor(rank, k) * piece_rows
            whole = lax.dynamic_update_slice_in_dim(
                whole, block.astype(dtype), start_row, axis=1
            )
        return whole[None]

    length_row = pick(lengths, batch)
    ends = jnp.cumsum(length_row)
    inner = jnp.arange(rows, dtype=jnp.int32)
    inner = jnp.bitwise_xor(inner // piece_rows, rank) * piece_rows + inner % piece_rows

    def documents(place):
        passed = ends[None, :] <= place[:, None]
        document = jnp.sum(passed.astype(jnp.int32), axis=1)
        begins = jnp.sum(jnp.where(passed, length_row[None, :], 0), axis=1)
        return document, place - begins

    query_place = position * rows + inner
    query_document, local_place = documents(query_place)
    tables = rotary_tables(local_place, width)
    masks = []
    earlier_tables = None
    for index in range(count):
        key_place = jnp.bitwise_xor(position, index) * rows + inner
        key_document, key_local_place = documents(key_place)
        if index == 2 and count == 4:
            earlier_tables = rotary_tables(key_local_place, width)
        masks.append(
            (key_document[:, None] == query_document[None, :])
            & (key_place[:, None] <= query_place[None, :])
        )
    flags = jnp.stack([jnp.any(mask) for mask in masks]).astype(jnp.int32)
    mask = jnp.where(jnp.concatenate(masks, axis=0), 0.0, NEGATIVE).astype(F32)
    layout = (tables, earlier_tables, mask, flags)

    def both_layers(array):
        arrived = swap_cores(array)
        return [by_core(array, arrived), by_core(arrived, array)]

    gains = [split(array) for array in both_layers(norm_gains[0])]
    shifts = [split(array) for array in both_layers(norm_shifts[0])]
    biases = both_layers(qkv_bias[0])

    def shard_halves(shard):
        half = shard.shape[1] // 2
        kept = lax.dynamic_slice_in_dim(shard, core * half, half, 1)
        arrived = swap_cores(lax.dynamic_slice_in_dim(shard, (1 - core) * half, half, 1))
        return [by_core(kept, arrived), by_core(arrived, kept)]

    def gather(piece, *others):
        return lax.all_gather(after(piece, *others), "ctx", axis=1, tiled=True)

    def halves(own, *others):
        own = after(own, *others)
        return own, swap_cores(own)

    attention_shards = shard_halves(jnp.concatenate([qkv_weight[0], out_weight[0].T[None]]))
    gate_up_shards = shard_halves(gate_up_weight[0])
    down_shards = shard_halves(down_weight[0].T[None])

    start = take_in(inputs)
    normed_zero, statistics_zero = norm_forward(start.astype(F32), gains[0][0], shifts[0][0])
    earlier_zero = earlier_chip(normed_zero)
    feed_shards = jnp.concatenate([gate_up_shards[0], down_shards[0]], axis=0)
    normed_zero, feed_shards, layout = lax.optimization_barrier(
        (normed_zero, feed_shards, layout)
    )
    normed_zero = tp_gather(normed_zero)
    attention_zero = gather(attention_shards[0])
    grad = take_in(after(cotangent, start))
    attention_zero, normed_zero, earlier_zero, layout, grad = lax.optimization_barrier(
        (attention_zero, normed_zero, earlier_zero, layout, grad)
    )
    feed_zero = gather(feed_shards)
    attention_halves = halves(attention_zero)
    qkv_weights = [[half[:3] for half in attention_halves], None]
    out_weights = [[half[3:] for half in attention_halves], None]
    queries_zero, key_values_zero = project_forward(
        normed_zero, earlier_zero, qkv_weights[0], biases[0], layout
    )
    hidden_zero, kept_attention_zero = attention_forward(
        start, queries_zero, key_values_zero, out_weights[0], layout
    )
    second_zero, second_statistics_zero = norm_forward(hidden_zero, gains[0][1], shifts[0][1])
    second_zero, attention_shard_one, gate_up_shard_one, down_shard_one = (
        lax.optimization_barrier(
            (second_zero, attention_shards[1], gate_up_shards[1], down_shards[1])
        )
    )
    attention_one = gather(attention_shard_one, attention_zero)
    second_zero = tp_gather(second_zero)
    grad_full = tp_gather(after(grad, hidden_zero))
    feed_zero, second_zero, grad_full = lax.optimization_barrier((feed_zero, second_zero, grad_full))
    gate_up_one = gather(gate_up_shard_one, feed_zero)
    feed_halves = halves(feed_zero)
    gate_up_weights = [[half[:2] for half in feed_halves], None]
    down_weights = [[half[2:] for half in feed_halves], None]
    kept_feed_zero = gate_forward(second_zero, gate_up_weights[0])
    middle = down_forward(hidden_zero, kept_feed_zero[2], down_weights[0])
    normed_one, statistics_one = norm_forward(middle.astype(F32), gains[1][0], shifts[1][0])
    earlier_one = earlier_chip(normed_one)
    normed_one = tp_gather(normed_one)
    attention_one, normed_one = lax.optimization_barrier((attention_one, normed_one))
    down_one = gather(down_shard_one, attention_one)
    attention_halves = halves(attention_one)
    qkv_weights[1] = [half[:3] for half in attention_halves]
    out_weights[1] = [half[3:] for half in attention_halves]
    queries_one, key_values_one = project_forward(
        normed_one, earlier_one, qkv_weights[1], biases[1], layout
    )
    hidden_one, kept_attention_one = attention_forward(
        middle, queries_one, key_values_one, out_weights[1], layout
    )
    second_one, second_statistics_one = norm_forward(hidden_one, gains[1][1], shifts[1][1])
    home_zero = send_home(0, after(middle, key_values_one))
    gate_up_one, second_one = lax.optimization_barrier((gate_up_one, second_one))
    second_one = tp_gather(second_one)
    second_one, home_zero = lax.optimization_barrier((second_one, home_zero))
    home_zero = spread_home(0, home_zero, steps=1)
    gate_up_weights[1] = halves(gate_up_one)
    kept_feed_one = gate_forward(second_one, gate_up_weights[1])

    kept_feed = (kept_feed_zero, kept_feed_one)
    kept_attention = (kept_attention_zero, kept_attention_one)
    second_norm = (
        (hidden_zero, second_statistics_zero, gains[0][1]),
        (hidden_one, second_statistics_one, gains[1][1]),
    )
    first_norm = (
        (start.astype(F32), statistics_zero, gains[0][0]),
        (middle.astype(F32), statistics_one, gains[1][0]),
    )
    first_normed = (normed_zero, normed_one)
    second_normed = (second_zero, second_one)
    input_grads = [None, None]
    small_grads = [None, None]
    scattered = [None, None]
    tables, earlier_tables, mask, flags = layout
    for layer in (1, 0):
        down_total = weight_grad(grad_full, [kept_feed[layer][2]])
        if layer == 1:
            down_one, down_total, grad_full, home_zero = lax.optimization_barrier(
                (down_one, down_total, grad_full, home_zero)
            )
            down_weights[1] = halves(down_one)
        gate_grad, up_grad = gate_backward(grad_full, kept_feed[layer], down_weights[layer])
        partial = feed_partial(gate_grad, up_grad, gate_up_weights[layer])
        down_grad = scatter_weight_grad(down_total)
        second_grad = tp_scatter(partial)
        gate_total = weight_grad(second_normed[layer], [gate_grad])
        second_grad, gate_total = lax.optimization_barrier((second_grad, gate_total))
        moved, gain_second, shift_second = norm_backward(*second_norm[layer], second_grad)
        hidden_grad = grad.astype(F32) + moved
        branch_grad = tp_gather(hidden_grad.astype(BF16))
        up_total = weight_grad(second_normed[layer], [up_grad])
        branch_grad, up_total = lax.optimization_barrier((branch_grad, up_total))
        if layer == 0:
            branch_grad = after(branch_grad, attention_grad)
        queries, key_values, attended, attended_low, log_total = kept_attention[layer]
        attended_grad = into(branch_grad, [half[0] for half in out_weights[layer]]).astype(BF16)
        if layer == 0:
            out_total = weight_grad(branch_grad, [attended_low])
            attended_grad, out_total = lax.optimization_barrier((attended_grad, out_total))
            gate_total = jnp.concatenate([gate_total, out_total], axis=2)
            last = down_forward(
                hidden_one, after(kept_feed_one[2], attended_grad), down_weights[1]
            )
        query_grad, key_value_grads = attend_back(
            queries, key_values, mask, flags, attended_grad, attended, log_total
        )
        query_grad, key_value_grads = after((query_grad, key_value_grads), down_grad)
        gate_weight_grad = scatter_weight_grad(gate_total)
        key_value_grad = after(scatter_chunks(key_value_grads), gate_weight_grad)
        if layer == 0:
            home_one = send_home(
                1, after(jnp.concatenate([last, input_grads[1]]), key_value_grad)
            )
        if layer == 1:
            out_total = weight_grad(branch_grad, [attended_low])
            up_total = jnp.concatenate([up_total, out_total], axis=2)
        query_grad = rotate(query_grad, tables, -1.0).astype(BF16)
        key_value_grad, up_total, query_grad = lax.optimization_barrier(
            (key_value_grad, up_total, query_grad)
        )
        up_weight_grad = scatter_weight_grad(up_total)
        key_grad = rotate(key_value_grad[0], tables, -1.0).astype(BF16)
        projected = (query_grad, key_grad, key_value_grad[1].astype(BF16))
        partial = projected_partial(projected, qkv_weights[layer])
        first_grad = tp_scatter(partial)
        qkv_total = weight_grad(first_normed[layer], projected)
        first_grad, qkv_total = lax.optimization_barrier((first_grad, qkv_total))
        bias_grad = jnp.stack([jnp.sum(part.astype(F32), axis=0) for part in projected])
        moved, gain_first, shift_first = norm_backward(*first_norm[layer], first_grad)
        grad = (hidden_grad + moved).astype(BF16)
        input_grads[layer] = grad
        attention_total = qkv_total
        if layer == 0:
            home_grad = send_home(0, grad)
        attention_grad = scatter_weight_grad(attention_total)
        if layer == 1:
            grad_full = after(tp_gather(grad), up_weight_grad)
        norm_grads = unsplit(jnp.stack([gain_first, gain_second, shift_first, shift_second]))
        small_grads[layer] = (norm_grads, bias_grad)
        feed_width = down_grad.shape[2]
        gate_up_grad = jnp.concatenate(
            [gate_weight_grad[:, :, :feed_width], up_weight_grad[:, :, :feed_width]]
        )
        out_grad = (up_weight_grad if layer == 1 else gate_weight_grad)[:, :, feed_width:]
        scattered[layer] = (attention_grad, out_grad, gate_up_grad, down_grad)

    norm_grads, bias_grads = [jnp.stack(parts) for parts in zip(*small_grads)]
    norm_rows = norm_grads.size // LANES
    norm_grads_sum = all_sum(norm_grads.reshape(-1, LANES), ("tp",))
    home_one = spread_home(1, after(home_one, norm_grads_sum))
    packed = jnp.concatenate([norm_grads_sum, bias_grads.reshape(-1, LANES)])
    packed = all_sum(packed, ("section",))
    packed = after(packed, attention_grad)
    packed = packed + sum(exchange(packed, "ctx", k) for k in range(1, count))
    norm_grads = packed[:norm_rows].reshape(norm_grads.shape)
    bias_grads = packed[norm_rows:].reshape(bias_grads.shape)
    norm_grads, bias_grads = by_core(norm_grads[0], norm_grads[1]), by_core(bias_grads[0], bias_grads[1])
    home_grad = list(after(spread_home(0, home_grad), attention_grad))
    layer_outputs = assemble(
        [by_core(zero, one[:, :piece_rows]) for zero, one in zip(home_zero, home_one)], BF16
    )
    grad_outputs = assemble(
        [by_core(zero, one[:, piece_rows:]) for zero, one in zip(home_grad, home_one)], F32
    )

    def join_halves(zero, one):
        to_zero = lax.ppermute(zero, "section", [(1, 0)])
        to_one = lax.ppermute(one, "section", [(0, 1)])
        low = by_core(zero, to_one)
        high = by_core(to_zero, one)
        return jnp.concatenate([low, high], axis=1).astype(F32)

    joined = [join_halves(zero, one) for zero, one in zip(*scattered)]
    return (
        layer_outputs,
        grad_outputs,
        norm_grads[None, :2],
        norm_grads[None, 2:],
        joined[0][None],
        bias_grads[None],
        joined[1][0].T[None],
        joined[2][None],
        joined[3][0].T[None],
    )


def solution(mesh):
    placed = (
        P(None, "ctx", None),
        P(None, "ctx", None),
        P(),
        P("section", None, None),
        P("section", None, None),
        P("section", None, "ctx", "tp"),
        P("section", None, "tp"),
        P("section", "tp", "ctx"),
        P("section", None, "ctx", "tp"),
        P("section", "tp", "ctx"),
    )
    return jax.shard_map(
        body,
        mesh=mesh,
        in_specs=placed,
        out_specs=(
            P("section", None, "ctx", None),
            P("section", None, "ctx", None),
            P("section", None, None),
            P("section", None, None),
            P("section", None, "ctx", "tp"),
            P("section", None, "tp"),
            P("section", "tp", "ctx"),
            P("section", None, "ctx", "tp"),
            P("section", "tp", "ctx"),
        ),
        check_vma=False,
    )
```

```python
import math

import jax
import jax.numpy as jnp
from jax import lax
from jax.experimental import pallas as pl
from jax.experimental.pallas import tpu as pltpu
from jax.sharding import PartitionSpec as P

HEAD_DIM = 64
ROTATED_ENTRIES = 16
EPSILON = 1e-05
NEGATIVE = -1e30
ROTARY_BASE = 10000.0
LANES = 128
F32 = jnp.float32
BF16 = jnp.bfloat16
CONTRACT_LAST = (((1,), (1,)), ((), ()))
CONTRACT_FIRST = (((0,), (0,)), ((), ()))
VMEM_BYTES = 48 * 1024 * 1024


def head_rows(values, head):
    lane = lax.broadcasted_iota(jnp.int32, values.shape, 1)
    return jnp.where(lane // HEAD_DIM == head, values, 0.0).astype(BF16)


def attend_kernel(chunks, flags, query_ref, bias_ref, *refs):
    full_ref, low_ref, log_ref, high, total, summed = refs[chunks:]
    rows = query_ref.shape[0]
    heads = LANES // HEAD_DIM
    scaled = query_ref[...].astype(F32) * HEAD_DIM**-0.5
    queries = [head_rows(scaled, head) for head in range(heads)]
    high[...] = jnp.full(high.shape, NEGATIVE, F32)
    total[...] = jnp.zeros(total.shape, F32)
    summed[...] = jnp.zeros(summed.shape, F32)
    for chunk in range(chunks):

        @pl.when(flags[chunk] != 0)
        def _():
            keys = refs[chunk][0]
            values = refs[chunk][1]
            for head in range(heads):
                scores = lax.dot_general(
                    keys, queries[head], CONTRACT_LAST, preferred_element_type=F32
                )
                scores = scores + bias_ref[chunk * rows : (chunk + 1) * rows, :]
                old = high[head]
                new = jnp.maximum(old, jnp.max(scores, axis=0, keepdims=True))
                weights = jnp.exp(scores - new)
                decay = jnp.exp(old - new)
                total[head] = total[head] * decay + jnp.sum(weights, axis=0, keepdims=True)
                summed[head] = summed[head] * decay + lax.dot_general(
                    values, weights.astype(BF16), CONTRACT_FIRST, preferred_element_type=F32
                )
                high[head] = new

    row = lax.broadcasted_iota(jnp.int32, (LANES, rows), 0)
    merged = jnp.zeros((LANES, rows), F32)
    for head in range(heads):
        merged = jnp.where(row // HEAD_DIM == head, summed[head] / total[head], merged)
        log_ref[0, head : head + 1, :] = high[head] + jnp.log(total[head])
    merged = merged.T
    full_ref[...] = merged
    low_ref[...] = merged.astype(BF16)


def column_spec(rows):
    return pl.BlockSpec((rows, LANES), lambda pair, flags: (0, pair))


def double_spec(rows):
    return pl.BlockSpec((2, rows, LANES), lambda pair, flags: (0, 0, pair))


def attend(queries, key_values, bias, flags):
    rows, width = queries.shape
    chunks = len(key_values)
    pairs = width // LANES
    heads = LANES // HEAD_DIM
    own = column_spec(rows)
    return pl.pallas_call(
        lambda *refs: attend_kernel(chunks, *refs),
        out_shape=(
            jax.ShapeDtypeStruct((rows, width), F32),
            jax.ShapeDtypeStruct((rows, width), BF16),
            jax.ShapeDtypeStruct((pairs, heads, rows), F32),
        ),
        grid_spec=pltpu.PrefetchScalarGridSpec(
            num_scalar_prefetch=1,
            grid=(pairs,),
            in_specs=[own, pl.BlockSpec(bias.shape, lambda pair, flags: (0, 0))]
            + [double_spec(rows)] * chunks,
            out_specs=(
                own,
                own,
                pl.BlockSpec((1, heads, rows), lambda pair, flags: (pair, 0, 0)),
            ),
            scratch_shapes=[
                pltpu.VMEM((heads, 1, rows), F32),
                pltpu.VMEM((heads, 1, rows), F32),
                pltpu.VMEM((heads, LANES, rows), F32),
            ],
        ),
        compiler_params=pltpu.CompilerParams(vmem_limit_bytes=VMEM_BYTES),
        cost_estimate=pl.CostEstimate(
            flops=4 * chunks * rows * rows * width * 2,
            bytes_accessed=2 * chunks * rows * width * 2 + bias.size * 4,
            transcendentals=0,
        ),
        name="attend",
    )(flags, queries, bias, *key_values)


def attend_back_kernel(chunks, flags, query_ref, bias_ref, grad_ref, full_ref, log_ref, *refs):
    query_grad_ref = refs[chunks]
    grad_refs = refs[chunks + 1 : 2 * chunks + 1]
    summed = refs[2 * chunks + 1]
    rows = query_ref.shape[0]
    heads = LANES // HEAD_DIM
    scale = HEAD_DIM**-0.5
    scaled = query_ref[...].astype(F32) * scale
    grad = grad_ref[...].astype(F32)
    product = (grad * full_ref[...]).T
    queries = [head_rows(scaled, head) for head in range(heads)]
    grads = [head_rows(grad, head) for head in range(heads)]
    deltas = [
        jnp.sum(product[head * HEAD_DIM : (head + 1) * HEAD_DIM, :], axis=0, keepdims=True)
        for head in range(heads)
    ]
    summed[...] = jnp.zeros(summed.shape, F32)
    for chunk in range(chunks):

        @pl.when(flags[chunk] != 0)
        def _():
            keys = refs[chunk][0]
            values = refs[chunk][1]
            key_float = keys.astype(F32)
            key_grad = jnp.zeros((rows, LANES), F32)
            value_grad = jnp.zeros((rows, LANES), F32)
            query_grad = summed[...]
            for head in range(heads):
                scores = lax.dot_general(
                    keys, queries[head], CONTRACT_LAST, preferred_element_type=F32
                )
                scores = scores + bias_ref[chunk * rows : (chunk + 1) * rows, :]
                weights = jnp.exp(scores - log_ref[0, head : head + 1, :])
                weight_grad = lax.dot_general(
                    values, grads[head], CONTRACT_LAST, preferred_element_type=F32
                )
                score_grad = (weights * (weight_grad - deltas[head])).astype(BF16)
                value_grad = value_grad + jnp.dot(
                    weights.astype(BF16), grads[head], preferred_element_type=F32
                )
                key_grad = key_grad + jnp.dot(
                    score_grad, queries[head], preferred_element_type=F32
                )
                query_grad = query_grad + lax.dot_general(
                    head_rows(key_float, head),
                    score_grad,
                    CONTRACT_FIRST,
                    preferred_element_type=F32,
                )
            summed[...] = query_grad
            grad_refs[chunk][0] = key_grad.astype(BF16)
            grad_refs[chunk][1] = value_grad.astype(BF16)

        @pl.when(flags[chunk] == 0)
        def _():
            grad_refs[chunk][...] = jnp.zeros((2, rows, LANES), BF16)

    query_grad_ref[...] = summed[...].T * scale


def attend_back(queries, key_values, bias, flags, grad, full, log_total):
    rows, width = queries.shape
    chunks = len(key_values)
    pairs = width // LANES
    heads = LANES // HEAD_DIM
    own = column_spec(rows)
    results = pl.pallas_call(
        lambda *refs: attend_back_kernel(chunks, *refs),
        out_shape=[jax.ShapeDtypeStruct((rows, width), F32)]
        + [jax.ShapeDtypeStruct((2, rows, width), BF16)] * chunks,
        grid_spec=pltpu.PrefetchScalarGridSpec(
            num_scalar_prefetch=1,
            grid=(pairs,),
            in_specs=[
                own,
                pl.BlockSpec(bias.shape, lambda pair, flags: (0, 0)),
                own,
                own,
                pl.BlockSpec((1, heads, rows), lambda pair, flags: (pair, 0, 0)),
            ]
            + [double_spec(rows)] * chunks,
            out_specs=[own] + [double_spec(rows)] * chunks,
            scratch_shapes=[pltpu.VMEM((LANES, rows), F32)],
        ),
        compiler_params=pltpu.CompilerParams(vmem_limit_bytes=VMEM_BYTES),
        cost_estimate=pl.CostEstimate(
            flops=10 * chunks * rows * rows * width * 2,
            bytes_accessed=4 * chunks * rows * width * 2 + bias.size * 4,
            transcendentals=0,
        ),
        name="attend_back",
    )(flags, queries, bias, grad, full, log_total, *key_values)
    return results[0], results[1:]


def swap_cores(block):
    return lax.ppermute(block, "section", [(0, 1), (1, 0)])


def exchange(block, axis, bit):
    return lax.ppermute(block, axis, [(i, i ^ bit) for i in range(lax.axis_size(axis))])


def after(value, *others):
    return lax.optimization_barrier((value, others))[0]


def tp_scatter(halves):
    ranks = lax.axis_size("tp")
    rows, width = halves[0].shape
    first, second = [half.reshape(ranks, rows // ranks, width) for half in halves]
    if ranks != 4:
        both = jnp.concatenate([first, second], axis=2)
        total = both[0].astype(F32)
        for k in range(1, ranks):
            total = total + exchange(both[k], "tp", k).astype(F32)
        return total
    near = exchange(jnp.stack([first[1], first[3]]), "tp", 1).astype(F32)
    far = exchange(second[2:], "tp", 2).astype(F32)
    across_first = exchange((first[2].astype(F32) + near[1]).astype(BF16), "tp", 2)
    across_second = exchange((second[1].astype(F32) + far[1]).astype(BF16), "tp", 1)
    return jnp.concatenate(
        [
            first[0].astype(F32) + near[0] + across_first.astype(F32),
            second[0].astype(F32) + far[0] + across_second.astype(F32),
        ],
        axis=1,
    )


def tp_gather(piece):
    ranks = lax.axis_size("tp")
    middle = piece.shape[1] // 2
    first, second = piece[:, :middle], piece[:, middle:]
    if ranks != 4:
        blocks = [piece] + [exchange(piece, "tp", k) for k in range(1, ranks)]
        whole = jnp.concatenate(blocks, axis=0)
        return [whole[:, :middle], whole[:, middle:]]
    first_far = exchange(first, "tp", 2)
    second_near = exchange(second, "tp", 1)
    first_rest = exchange(jnp.stack([first, first_far]), "tp", 1)
    second_rest = exchange(jnp.concatenate([second, second_near]), "tp", 2)
    return [
        jnp.concatenate([first, first_rest[0], first_far, first_rest[1]]),
        jnp.concatenate([second, second_near, second_rest]),
    ]


def across(blocks, bit, upward):
    count = lax.axis_size("ctx")
    pairs = [(i, i ^ bit) for i in range(count)]
    if bit == count // 4:
        pairs = [(i, j) for i, j in pairs if (step_of(i, count) < step_of(j, count)) == upward]
    return [lax.ppermute(block, "ctx", pairs) for block in blocks]


def step_of(index, count):
    return index if index < count // 2 else count - 1 - index


def gather_chunks(own):
    count = lax.axis_size("ctx")
    blocks = [own]
    bit = 1
    while bit < count // 2:
        blocks = blocks + across(blocks, bit, True)
        bit *= 2
    arrived = [swap_cores(block) for block in blocks]
    return [block for pair in zip(blocks, arrived) for block in pair]


def scatter_chunks(blocks):
    count = lax.axis_size("ctx")
    arrived = [swap_cores(block) for block in blocks[1::2]]
    blocks = [
        mine.astype(F32) + other.astype(F32) for mine, other in zip(blocks[::2], arrived)
    ]
    bit = count // 4
    while bit >= 1:
        arrived = across([block.astype(BF16) for block in blocks[bit:]], bit, False)
        blocks = [mine + other.astype(F32) for mine, other in zip(blocks[:bit], arrived)]
        bit //= 2
    return blocks[0]


def norm_forward(values, gain, shift):
    mean = jnp.mean(values, axis=1, keepdims=True)
    centred = values - mean
    spread = jnp.mean(centred * centred, axis=1, keepdims=True)
    inverse = lax.rsqrt(spread + EPSILON)
    return (centred * inverse * gain + shift).astype(BF16), (mean, inverse)


def norm_backward(values, statistics, gain, grad):
    mean, inverse = statistics
    hat = (values - mean) * inverse
    scaled = gain * grad
    first = jnp.mean(scaled, axis=1, keepdims=True)
    second = jnp.mean(scaled * hat, axis=1, keepdims=True)
    moved = inverse * (scaled - first - hat * second)
    return moved, jnp.sum(grad * hat, axis=0), jnp.sum(grad, axis=0)


def rotary_tables(local_place, width):
    half = ROTATED_ENTRIES // 2
    entry = jnp.arange(HEAD_DIM)
    frequency = jnp.exp(
        -((entry % half).astype(F32) * 2.0 / ROTATED_ENTRIES) * math.log(ROTARY_BASE)
    )
    frequency = jnp.where(entry < ROTATED_ENTRIES, frequency, 0.0)
    angle = local_place.astype(F32)[:, None] * frequency[None, :]
    sine = jnp.sin(angle)
    tables = (
        jnp.cos(angle),
        jnp.where(entry < half, -sine, 0.0),
        jnp.where(entry >= half, sine, 0.0),
    )
    return tuple(jnp.tile(table, (1, width // HEAD_DIM)) for table in tables)


def rotate(values, tables, sign):
    half = ROTATED_ENTRIES // 2
    cosine, low, high = tables
    return (
        values * cosine
        + jnp.roll(values, -half, axis=1) * (low * sign)
        + jnp.roll(values, half, axis=1) * (high * sign)
    )


def dot(left, right):
    return jnp.dot(left, right, preferred_element_type=F32)


def dot_back(left, right):
    return lax.dot_general(left, right, CONTRACT_LAST, preferred_element_type=F32)


def token_sum(left, right):
    return lax.dot_general(left, right, CONTRACT_FIRST, preferred_element_type=F32)


def into(values, halves):
    return dot(values[0], halves[0]) + dot(values[1], halves[1])


def out_of(values, halves):
    return [dot_back(values, half).astype(BF16) for half in halves]


def all_sum(value, axes):
    for axis in axes:
        bit = 1
        while bit < lax.axis_size(axis):
            value = value + exchange(value, axis, bit)
            bit *= 2
    return value


def earlier_chip(normed_piece):
    if lax.axis_size("ctx") != 4:
        return None
    return across([normed_piece], 1, True)[0]


def project_forward(normed, earlier, weights, bias_row, layout):
    tables, earlier_tables, mask, flags = layout

    def project(rows, c):
        return into(rows, [half[c] for half in weights]) + bias_row[c][None]

    def key_value(rows, turn):
        return jnp.stack(
            [rotate(project(rows, 1), turn, 1.0).astype(BF16), project(rows, 2).astype(BF16)]
        )

    own = key_value(normed, tables)
    queries = rotate(project(normed, 0), tables, 1.0).astype(BF16)
    if earlier is None:
        return queries, gather_chunks(own)
    own, queries, earlier = lax.optimization_barrier((own, queries, earlier))
    blocks = [own, key_value(tp_gather(earlier), earlier_tables)]
    return queries, [each for block in blocks for each in (block, swap_cores(block))]


def attention_forward(piece, queries, key_values, out_weights, layout):
    tables, earlier_tables, mask, flags = layout
    attended, attended_low, log_total = attend(queries, key_values, mask, flags)
    partial = out_of(attended_low, [half[0] for half in out_weights])
    hidden = piece.astype(F32) + tp_scatter(partial)
    return hidden, (queries, key_values, attended, attended_low, log_total)


def gate_forward(normed, weights):
    gate, up = [into(normed, [half[c] for half in weights]) for c in range(2)]
    activated = (gate * jax.nn.sigmoid(gate) * up).astype(BF16)
    return gate, up, activated


def down_forward(hidden, activated, weights):
    partial = out_of(activated, [half[0] for half in weights])
    return (hidden + tp_scatter(partial)).astype(BF16)


def shared_weight_grad(own, other):
    arrived = swap_cores(other.astype(BF16))
    return (own + arrived.astype(F32)).astype(BF16)


def weight_grad(values, grads):
    own, other = [jnp.stack([token_sum(half, grad) for grad in grads]) for half in values]
    return shared_weight_grad(own, other)


def scatter_weight_grad(total):
    return lax.psum_scatter(total, "ctx", scatter_dimension=1, tiled=True)


def gate_backward(grad_full, kept, down):
    gate, up, activated = kept
    activated_grad = into(grad_full, [half[0] for half in down])
    sigmoid = jax.nn.sigmoid(gate)
    swish = gate * sigmoid
    gate_grad = (activated_grad * up * (sigmoid * (1.0 + gate * (1.0 - sigmoid)))).astype(BF16)
    up_grad = (activated_grad * swish).astype(BF16)
    return gate_grad, up_grad


def feed_partial(gate_grad, up_grad, weights):
    return [
        (dot_back(gate_grad, half[0]) + dot_back(up_grad, half[1])).astype(BF16)
        for half in weights
    ]


def projected_partial(projected, weights):
    return [
        sum(dot_back(part, half[c]) for c, part in enumerate(projected)).astype(BF16)
        for half in weights
    ]


def body(
    inputs,
    cotangent,
    lengths,
    norm_gains,
    norm_shifts,
    qkv_weight,
    qkv_bias,
    out_weight,
    gate_up_weight,
    down_weight,
):
    core = lax.axis_index("section")
    place_index = lax.axis_index("ctx")
    rank = lax.axis_index("tp")
    ranks = lax.axis_size("tp")
    count = lax.axis_size("ctx")
    rows, features = inputs.shape[1:]
    width = qkv_weight.shape[3]
    far = count // 2
    batch = place_index // far
    position = 2 * jnp.where(batch == 0, place_index, count - 1 - place_index) + core
    first_core = core == 0
    both = ("section", "ctx")
    piece_rows = rows // ranks

    def by_core(zero, one):
        return jnp.where(first_core, zero, one)

    def pick(array, index, axis=0):
        return lax.dynamic_index_in_dim(array, index, axis, keepdims=False)

    def reorder(block):
        pieces = block.reshape(ranks, piece_rows, -1)
        return jnp.concatenate(
            [pick(pieces, jnp.bitwise_xor(rank, k)) for k in range(ranks)], axis=0
        )

    def split(array):
        cut = array.reshape(array.shape[:-1] + (count, 2, features // (2 * count)))
        shape = array.shape[:-1] + (features // 2,)
        axis = cut.ndim - 2
        return jnp.concatenate(
            [pick(cut, index, axis).reshape(shape) for index in (core, 1 - core)], axis=-1
        )

    def unsplit(array):
        lead = array.shape[:-1]
        cut = array.reshape(lead + (2, count, features // (2 * count)))
        first, second = [lax.index_in_dim(cut, j, len(lead), keepdims=False) for j in range(2)]
        joined = jnp.stack([by_core(first, second), by_core(second, first)], axis=len(lead) + 1)
        return joined.reshape(lead + (features,))

    def seat(index, half):
        step = index // 2
        return (index % 2) * count + (step if half == 0 else count - 1 - step)

    def take_in(array):
        piece = pick(pick(array, core).reshape(ranks, piece_rows, features), rank)
        pairs = [(half * count + i, seat(i, half)) for half in range(2) for i in range(count)]
        return split(lax.ppermute(piece, both, pairs))

    def send_home(layer, piece):
        piece = unsplit(piece)
        return jnp.stack(
            [
                lax.ppermute(piece, both, [(seat(i, half), layer * count + i) for i in range(count)])
                for half in range(2)
            ]
        )

    def spread_home(layer, own, steps=2):
        def send(block, k):
            pairs = [(layer * ranks + i, layer * ranks + (i ^ k)) for i in range(ranks)]
            return lax.ppermute(block, ("section", "tp"), pairs)

        if ranks != 4 or steps == 1:
            return [own] + [send(own, k) for k in range(1, ranks)]
        middle = features // 2
        first, second = own[..., :middle], own[..., middle:]
        first_far, second_near = send(first, 2), send(second, 1)
        first_rest = send(jnp.stack([first, first_far]), 1)
        second_rest = send(jnp.stack([second, second_near]), 2)
        return [
            jnp.concatenate(pair, axis=-1)
            for pair in zip(
                (first, first_rest[0], first_far, first_rest[1]),
                (second, second_near, second_rest[0], second_rest[1]),
            )
        ]

    def assemble(blocks, dtype):
        whole = jnp.zeros((2, rows, features), dtype)
        for k, block in enumerate(blocks):
            start_row = jnp.bitwise_xor(rank, k) * piece_rows
            whole = lax.dynamic_update_slice_in_dim(
                whole, block.astype(dtype), start_row, axis=1
            )
        return whole[None]

    length_row = pick(lengths, batch)
    ends = jnp.cumsum(length_row)
    inner = jnp.arange(rows, dtype=jnp.int32)
    inner = jnp.bitwise_xor(inner // piece_rows, rank) * piece_rows + inner % piece_rows

    def documents(place):
        passed = ends[None, :] <= place[:, None]
        document = jnp.sum(passed.astype(jnp.int32), axis=1)
        begins = jnp.sum(jnp.where(passed, length_row[None, :], 0), axis=1)
        return document, place - begins

    query_place = position * rows + inner
    query_document, local_place = documents(query_place)
    tables = rotary_tables(local_place, width)
    masks = []
    earlier_tables = None
    for index in range(count):
        key_place = jnp.bitwise_xor(position, index) * rows + inner
        key_document, key_local_place = documents(key_place)
        if index == 2 and count == 4:
            earlier_tables = rotary_tables(key_local_place, width)
        masks.append(
            (key_document[:, None] == query_document[None, :])
            & (key_place[:, None] <= query_place[None, :])
        )
    flags = jnp.stack([jnp.any(mask) for mask in masks]).astype(jnp.int32)
    mask = jnp.where(jnp.concatenate(masks, axis=0), 0.0, NEGATIVE).astype(F32)
    layout = (tables, earlier_tables, mask, flags)

    def both_layers(array):
        arrived = swap_cores(array)
        return [by_core(array, arrived), by_core(arrived, array)]

    gains = [split(array) for array in both_layers(norm_gains[0])]
    shifts = [split(array) for array in both_layers(norm_shifts[0])]
    biases = both_layers(qkv_bias[0])

    def shard_halves(shard):
        half = shard.shape[1] // 2
        kept = lax.dynamic_slice_in_dim(shard, core * half, half, 1)
        arrived = swap_cores(lax.dynamic_slice_in_dim(shard, (1 - core) * half, half, 1))
        return [by_core(kept, arrived), by_core(arrived, kept)]

    def gather(piece, *others):
        return lax.all_gather(after(piece, *others), "ctx", axis=1, tiled=True)

    def halves(own, *others):
        own = after(own, *others)
        return own, swap_cores(own)

    attention_shards = shard_halves(jnp.concatenate([qkv_weight[0], out_weight[0].T[None]]))
    gate_up_shards = shard_halves(gate_up_weight[0])
    down_shards = shard_halves(down_weight[0].T[None])

    start = take_in(inputs)
    normed_zero, statistics_zero = norm_forward(start.astype(F32), gains[0][0], shifts[0][0])
    earlier_zero = earlier_chip(normed_zero)
    feed_shards = jnp.concatenate([gate_up_shards[0], down_shards[0]], axis=0)
    normed_zero, feed_shards, layout = lax.optimization_barrier(
        (normed_zero, feed_shards, layout)
    )
    normed_zero = tp_gather(normed_zero)
    attention_zero = gather(attention_shards[0])
    grad = take_in(after(cotangent, start))
    attention_zero, normed_zero, earlier_zero, layout, grad = lax.optimization_barrier(
        (attention_zero, normed_zero, earlier_zero, layout, grad)
    )
    feed_zero = gather(feed_shards)
    attention_halves = halves(attention_zero)
    qkv_weights = [[half[:3] for half in attention_halves], None]
    out_weights = [[half[3:] for half in attention_halves], None]
    queries_zero, key_values_zero = project_forward(
        normed_zero, earlier_zero, qkv_weights[0], biases[0], layout
    )
    hidden_zero, kept_attention_zero = attention_forward(
        start, queries_zero, key_values_zero, out_weights[0], layout
    )
    second_zero, second_statistics_zero = norm_forward(hidden_zero, gains[0][1], shifts[0][1])
    second_zero, attention_shard_one, gate_up_shard_one, down_shard_one = (
        lax.optimization_barrier(
            (second_zero, attention_shards[1], gate_up_shards[1], down_shards[1])
        )
    )
    attention_one = gather(attention_shard_one, attention_zero)
    second_zero = tp_gather(second_zero)
    grad_full = tp_gather(after(grad, hidden_zero))
    feed_zero, second_zero, grad_full = lax.optimization_barrier((feed_zero, second_zero, grad_full))
    gate_up_one = gather(gate_up_shard_one, feed_zero)
    feed_halves = halves(feed_zero)
    gate_up_weights = [[half[:2] for half in feed_halves], None]
    down_weights = [[half[2:] for half in feed_halves], None]
    kept_feed_zero = gate_forward(second_zero, gate_up_weights[0])
    middle = down_forward(hidden_zero, kept_feed_zero[2], down_weights[0])
    normed_one, statistics_one = norm_forward(middle.astype(F32), gains[1][0], shifts[1][0])
    earlier_one = earlier_chip(normed_one)
    normed_one = tp_gather(normed_one)
    attention_one, normed_one = lax.optimization_barrier((attention_one, normed_one))
    down_one = gather(down_shard_one, attention_one)
    attention_halves = halves(attention_one)
    qkv_weights[1] = [half[:3] for half in attention_halves]
    out_weights[1] = [half[3:] for half in attention_halves]
    queries_one, key_values_one = project_forward(
        normed_one, earlier_one, qkv_weights[1], biases[1], layout
    )
    hidden_one, kept_attention_one = attention_forward(
        middle, queries_one, key_values_one, out_weights[1], layout
    )
    second_one, second_statistics_one = norm_forward(hidden_one, gains[1][1], shifts[1][1])
    home_zero = send_home(0, after(middle, key_values_one))
    gate_up_one, second_one = lax.optimization_barrier((gate_up_one, second_one))
    second_one = tp_gather(second_one)
    second_one, home_zero = lax.optimization_barrier((second_one, home_zero))
    home_zero = spread_home(0, home_zero, steps=1)
    gate_up_weights[1] = halves(gate_up_one)
    kept_feed_one = gate_forward(second_one, gate_up_weights[1])

    kept_feed = (kept_feed_zero, kept_feed_one)
    kept_attention = (kept_attention_zero, kept_attention_one)
    second_norm = (
        (hidden_zero, second_statistics_zero, gains[0][1]),
        (hidden_one, second_statistics_one, gains[1][1]),
    )
    first_norm = (
        (start.astype(F32), statistics_zero, gains[0][0]),
        (middle.astype(F32), statistics_one, gains[1][0]),
    )
    first_normed = (normed_zero, normed_one)
    second_normed = (second_zero, second_one)
    input_grads = [None, None]
    small_grads = [None, None]
    scattered = [None, None]
    tables, earlier_tables, mask, flags = layout
    for layer in (1, 0):
        down_total = weight_grad(grad_full, [kept_feed[layer][2]])
        if layer == 1:
            down_one, down_total, grad_full, home_zero = lax.optimization_barrier(
                (down_one, down_total, grad_full, home_zero)
            )
            down_weights[1] = halves(down_one)
        gate_grad, up_grad = gate_backward(grad_full, kept_feed[layer], down_weights[layer])
        partial = feed_partial(gate_grad, up_grad, gate_up_weights[layer])
        down_grad = scatter_weight_grad(down_total)
        second_grad = tp_scatter(partial)
        gate_total = weight_grad(second_normed[layer], [gate_grad])
        second_grad, gate_total = lax.optimization_barrier((second_grad, gate_total))
        moved, gain_second, shift_second = norm_backward(*second_norm[layer], second_grad)
        hidden_grad = grad.astype(F32) + moved
        branch_grad = tp_gather(hidden_grad.astype(BF16))
        up_total = weight_grad(second_normed[layer], [up_grad])
        branch_grad, up_total = lax.optimization_barrier((branch_grad, up_total))
        if layer == 0:
            branch_grad = after(branch_grad, attention_grad)
        queries, key_values, attended, attended_low, log_total = kept_attention[layer]
        attended_grad = into(branch_grad, [half[0] for half in out_weights[layer]]).astype(BF16)
        if layer == 0:
            out_total = weight_grad(branch_grad, [attended_low])
            attended_grad, out_total = lax.optimization_barrier((attended_grad, out_total))
            gate_total = jnp.concatenate([gate_total, out_total], axis=2)
            last = down_forward(
                hidden_one, after(kept_feed_one[2], attended_grad), down_weights[1]
            )
        query_grad, key_value_grads = attend_back(
            queries, key_values, mask, flags, attended_grad, attended, log_total
        )
        query_grad, key_value_grads = after((query_grad, key_value_grads), down_grad)
        gate_weight_grad = scatter_weight_grad(gate_total)
        key_value_grad = after(scatter_chunks(key_value_grads), gate_weight_grad)
        if layer == 0:
            home_one = send_home(
                1, after(jnp.concatenate([last, input_grads[1]]), key_value_grad)
            )
        if layer == 1:
            out_total = weight_grad(branch_grad, [attended_low])
            up_total = jnp.concatenate([up_total, out_total], axis=2)
        query_grad = rotate(query_grad, tables, -1.0).astype(BF16)
        key_value_grad, up_total, query_grad = lax.optimization_barrier(
            (key_value_grad, up_total, query_grad)
        )
        up_weight_grad = scatter_weight_grad(up_total)
        key_grad = rotate(key_value_grad[0], tables, -1.0).astype(BF16)
        projected = (query_grad, key_grad, key_value_grad[1].astype(BF16))
        partial = projected_partial(projected, qkv_weights[layer])
        first_grad = tp_scatter(partial)
        qkv_total = weight_grad(first_normed[layer], projected)
        first_grad, qkv_total = lax.optimization_barrier((first_grad, qkv_total))
        bias_grad = jnp.stack([jnp.sum(part.astype(F32), axis=0) for part in projected])
        moved, gain_first, shift_first = norm_backward(*first_norm[layer], first_grad)
        grad = (hidden_grad + moved).astype(BF16)
        input_grads[layer] = grad
        attention_total = qkv_total
        if layer == 0:
            home_grad = send_home(0, grad)
        attention_grad = scatter_weight_grad(attention_total)
        if layer == 1:
            grad_full = after(tp_gather(grad), up_weight_grad)
        norm_grads = unsplit(jnp.stack([gain_first, gain_second, shift_first, shift_second]))
        small_grads[layer] = (norm_grads, bias_grad)
        feed_width = down_grad.shape[2]
        gate_up_grad = jnp.concatenate(
            [gate_weight_grad[:, :, :feed_width], up_weight_grad[:, :, :feed_width]]
        )
        out_grad = (up_weight_grad if layer == 1 else gate_weight_grad)[:, :, feed_width:]
        scattered[layer] = (attention_grad, out_grad, gate_up_grad, down_grad)

    norm_grads, bias_grads = [jnp.stack(parts) for parts in zip(*small_grads)]
    norm_rows = norm_grads.size // LANES
    norm_grads_sum = all_sum(norm_grads.reshape(-1, LANES), ("tp",))
    home_one = spread_home(1, after(home_one, norm_grads_sum))
    packed = jnp.concatenate([norm_grads_sum, bias_grads.reshape(-1, LANES)])
    packed = all_sum(packed, ("section",))
    packed = after(packed, attention_grad)
    packed = packed + sum(exchange(packed, "ctx", k) for k in range(1, count))
    norm_grads = packed[:norm_rows].reshape(norm_grads.shape)
    bias_grads = packed[norm_rows:].reshape(bias_grads.shape)
    norm_grads, bias_grads = by_core(norm_grads[0], norm_grads[1]), by_core(bias_grads[0], bias_grads[1])
    home_grad, home_one = after((spread_home(0, home_grad), home_one), attention_grad)
    layer_outputs = assemble(
        [by_core(zero, one[:, :piece_rows]) for zero, one in zip(home_zero, home_one)], BF16
    )
    grad_outputs = assemble(
        [by_core(zero, one[:, piece_rows:]) for zero, one in zip(home_grad, home_one)], F32
    )

    def join_halves(zero, one):
        to_zero = lax.ppermute(zero, "section", [(1, 0)])
        to_one = lax.ppermute(one, "section", [(0, 1)])
        low = by_core(zero, to_one)
        high = by_core(to_zero, one)
        return jnp.concatenate([low, high], axis=1).astype(F32)

    joined = [join_halves(zero, one) for zero, one in zip(*scattered)]
    return (
        layer_outputs,
        grad_outputs,
        norm_grads[None, :2],
        norm_grads[None, 2:],
        joined[0][None],
        bias_grads[None],
        joined[1][0].T[None],
        joined[2][None],
        joined[3][0].T[None],
    )


def solution(mesh):
    placed = (
        P(None, "ctx", None),
        P(None, "ctx", None),
        P(),
        P("section", None, None),
        P("section", None, None),
        P("section", None, "ctx", "tp"),
        P("section", None, "tp"),
        P("section", "tp", "ctx"),
        P("section", None, "ctx", "tp"),
        P("section", "tp", "ctx"),
    )
    return jax.shard_map(
        body,
        mesh=mesh,
        in_specs=placed,
        out_specs=(
            P("section", None, "ctx", None),
            P("section", None, "ctx", None),
            P("section", None, None),
            P("section", None, None),
            P("section", None, "ctx", "tp"),
            P("section", None, "tp"),
            P("section", "tp", "ctx"),
            P("section", None, "ctx", "tp"),
            P("section", "tp", "ctx"),
        ),
        check_vma=False,
    )
```
